32 devices in a mesh: dp: 8 (over z, y), tensor: 4 (over x, core).
Axes of the slice: x: 2, y: 2, z: 4, core: 2. Of those that a mesh axis runs over, the one named last changes fastest.
Arguments:
- hidden: bfloat16 [8192, 768], P(('dp', 'tensor'))
- long_lengths: int32 [8], P('dp'), may hold values from 128 to 512, as said below
- short_lengths: int32 [32], P('dp'), may hold values from 32 to 128, as said below
- w_qkv: bfloat16 [2, 3, 768, 768], P(None, None, None, 'tensor'), may hold values from -0.3125 to 0.3125
- bias_qv: float32 [2, 2, 768], P(None, None, 'tensor'), may hold values from -3 to 3
- w_out: bfloat16 [2, 768, 768], P(None, 'tensor'), may hold values from -1.25 to 1.25
- bias_out: float32 [2, 768], replicated, may hold values from -3 to 3
- ln_gain: float32 [2, 2, 768], replicated, may hold values from 0.25 to 1.75
- ln_bias: float32 [2, 2, 768], replicated, may hold values from -2 to 2
- w_up: bfloat16 [2, 768, 3072], P(None, None, 'tensor'), may hold values from -0.21875 to 0.21875
- bias_up: float32 [2, 3072], P(None, 'tensor'), may hold values from -3 to 3
- w_down: bfloat16 [2, 3072, 768], P(None, 'tensor'), may hold values from -0.21875 to 0.21875
- bias_down: float32 [2, 768], replicated, may hold values from -3 to 3
- cotangent: bfloat16 [8192, 768], P(('dp', 'tensor')), may hold values from -6 to 6
Outputs:
- hidden_out: bfloat16 [8192, 768], P(('dp', 'tensor'))
- grad_hidden: float32 [8192, 768], P(('dp', 'tensor'))
- grad_qkv: float32 [2, 3, 768, 768], P(None, None, 'dp', 'tensor')
- grad_bias_qv: float32 [2, 2, 768], P(None, None, 'tensor')
- grad_out: float32 [2, 768, 768], P(None, 'tensor', 'dp')
- grad_bias_out: float32 [2, 768], replicated
- grad_ln_gain: float32 [2, 2, 768], replicated
- grad_ln_bias: float32 [2, 2, 768], replicated
- grad_up: float32 [2, 768, 3072], P(None, 'dp', 'tensor')
- grad_bias_up: float32 [2, 3072], P(None, 'tensor')
- grad_down: float32 [2, 3072, 768], P(None, 'tensor', 'dp')
- grad_bias_down: float32 [2, 768], replicated
- rms_values: float32 [2, 3], replicated
The draws below stay inside these ranges and needn't reach their ends.
Inputs may be any that keep to these rules, and one draw needn't show every extreme that they name: `long_lengths`: live leading slots of each long row of 512; row 0 is full. `short_lengths`: live leading slots of each short row of 128; row 0 is full.
All inputs are finite; a program needn't handle non-finite values. Where the reference program divides by a largest or mean magnitude, that divisor is 1e-20 or more.
Results may differ from the reference program's by a relative error of at most 0.035.
Values may be sent and summed in bfloat16 or wider, within the bound.
No kernel may reach another device: no remote copies, remote signals or barrier semaphores. Data moves between devices by JAX's collectives and lax.ppermute only.
A program may use at most 192 MiB of HBM per device.

```python
from functools import partial
import jax
import jax.numpy as jnp
from jax import lax

D = 768
HEADS = 12
HEAD_DIM = 64
FF = 3072
LAYERS = 2
LONG_LEN = 512
SHORT_LEN = 128
LONG_DEV = 1
SHORT_DEV = 4
TOK_DEV = 1024
TOKENS = 8192
LONG_ROWS = 8
SHORT_ROWS = 32
N_DP = 8


def draw_hidden(key, part):
    key = jax.random.fold_in(key, 11)
    key_one = jax.random.fold_in(key, 0)
    row_scale = 0.6 + 1.2 * jnp.arange(TOKENS, dtype=jnp.float32)[:, None] / TOKENS
    values = jnp.clip(jax.random.normal(key_one, (TOKENS, D), jnp.float32), -5.0, 5.0) * row_scale
    return values.astype(jnp.bfloat16)


def draw_long_lengths(key, part):
    key = jax.random.fold_in(key, 12)
    lengths = jax.random.randint(key, (LONG_ROWS,), LONG_LEN // 4, LONG_LEN + 1, dtype=jnp.int32)
    return lengths.at[0].set(LONG_LEN)


def draw_short_lengths(key, part):
    key = jax.random.fold_in(key, 13)
    lengths = jax.random.randint(key, (SHORT_ROWS,), SHORT_LEN // 4, SHORT_LEN + 1, dtype=jnp.int32)
    return lengths.at[0].set(SHORT_LEN)


def spiked(values, own_key, source, target, blocks, factor):
    owner, partner = [(jnp.arange(values.shape[position]) // (values.shape[position] // blocks)).reshape([-1 if axis == position else 1 for axis in range(values.ndim)]) for position in (source, target)]
    chosen = jax.random.permutation(own_key, blocks)[partner]
    strong = (owner == chosen) | (owner == (partner + blocks // 2) % blocks)
    return jnp.where(strong, factor * values, values)


def levels(own_key, extent, shards, low, largest):
    def one(position, blocks):
        steps = jax.random.uniform(jax.random.fold_in(jax.random.fold_in(own_key, 6), position), (blocks,), jnp.float32, low / len(shards), largest / len(shards))
        return jnp.repeat(jnp.exp(steps), extent[position] // blocks).reshape((-1,) + (1,) * (len(extent) - position - 1))

    loudness = one(*shards[0])
    for cut in shards[1:]:
        loudness = loudness * one(*cut)
    return loudness


def centred(own_key, dims, deviation, reach, cuts=(), held_as=jnp.bfloat16):
    factor_of = levels(own_key, dims, cuts, -0.22, 0.18) if cuts else 1.0
    array = jax.random.normal(own_key, dims, jnp.float32) * deviation * factor_of
    return jnp.minimum(jnp.maximum(array, -reach), reach).astype(held_as)


def gaussian_with(key, shape, scale, reach, cuts, heavy, kind=jnp.bfloat16):
    array = scale * jax.random.normal(key, shape, jnp.float32)
    if cuts:
        array = array * levels(key, shape, cuts, -0.22, 0.18)
    return jnp.clip(spiked(array, jax.random.fold_in(key, 3), *heavy), -reach, reach).astype(kind)


def setup_inputs(seed: int = 0) -> dict:
    arg_keys = jax.random.split(jax.random.key(seed), 15)
    return {
        "hidden": draw_hidden(jax.random.fold_in(arg_keys[14], 71), 0),
        "long_lengths": draw_long_lengths(jax.random.fold_in(arg_keys[14], 71), 0),
        "short_lengths": draw_short_lengths(jax.random.fold_in(arg_keys[14], 71), 0),
        "w_qkv": centred(arg_keys[3], (LAYERS, 3, D, D), (D // 2) ** -0.5, 0.3125, ((3, 4),)),
        "bias_qv": centred(arg_keys[4], (LAYERS, 2, D), 0.5, 3.0, ((2, 4),), jnp.float32),
        "w_out": centred(arg_keys[5], (LAYERS, D, D), (D // 32) ** -0.5, 1.25, ((1, 4),)),
        "bias_out": centred(arg_keys[6], (LAYERS, D), 0.5, 3.0, (), jnp.float32),
        "ln_gain": jnp.clip(1.0 + 0.15 * jax.random.normal(arg_keys[7], (LAYERS, 2, D), jnp.float32), 0.25, 1.75),
        "ln_bias": centred(arg_keys[8], (LAYERS, 2, D), 0.3, 2.0, (), jnp.float32),
        "w_up": centred(arg_keys[9], (LAYERS, D, FF), D ** -0.5, 0.21875, ((2, 4),)),
        "bias_up": centred(arg_keys[10], (LAYERS, FF), 0.5, 3.0, ((1, 4),), jnp.float32),
        "w_down": centred(arg_keys[11], (LAYERS, FF, D), (FF // 4) ** -0.5, 0.21875, ((1, 4),)),
        "bias_down": centred(arg_keys[12], (LAYERS, D), 0.5, 3.0, (), jnp.float32),
        "cotangent": gaussian_with(arg_keys[13], (TOKENS, D), 1.0, 6.0, ((0, 32),), (0, 1, 32, 2.75)),
    }


@jax.custom_vjp
def low(v):
    return lax.optimization_barrier(v.astype(jnp.bfloat16)).astype(jnp.float32)

@jax.custom_vjp
def low_back(v):
    return v

def low_keep(v):
    return (low(v), None)

def low_pass(kept, grad):
    return (grad,)

def back_keep(v):
    return (v, None)

def back_low(kept, grad):
    return (low(grad),)
low.defvjp(low_keep, low_pass)
low_back.defvjp(back_keep, back_low)
eps_norm = 1e-06
eps_clip = 1e-06

def soft_clip(values, fixed_bound):
    if fixed_bound is None:
        clip_bound = jnp.max(jnp.abs(values)) * 0.25 + eps_clip
    else:
        clip_bound = fixed_bound
    return (clip_bound * jnp.tanh(values / clip_bound), clip_bound)

def pick_bound(fixed_bounds, index):
    if fixed_bounds is None:
        return None
    return fixed_bounds[index]

def layer_norm(values, gain_row, shift_row):
    centre = lax.optimization_barrier(jnp.mean(values, axis=-1, keepdims=True))
    spread = lax.optimization_barrier(jnp.mean((values - centre) ** 2, axis=-1, keepdims=True))
    return (values - centre) * lax.rsqrt(spread + eps_norm) * gain_row + shift_row

def attend_group(queries, key_rows, value_rows, lengths):
    scores = jnp.einsum('bqhd,bkhd->bhqk', queries, key_rows, precision=lax.Precision.HIGHEST) * HEAD_DIM ** (-0.5)
    live = jnp.arange(key_rows.shape[1], dtype=jnp.int32)[None, None, None, :] < lengths[:, None, None, None]
    scores = low_back(jnp.where(live, scores, -1000000000.0))
    top_score = lax.optimization_barrier(jnp.max(scores, axis=-1, keepdims=True))
    weights = jnp.exp(scores - top_score)
    probs = weights / lax.optimization_barrier(jnp.sum(weights, axis=-1, keepdims=True))
    return jnp.einsum('bhqk,bkhd->bqhd', low(probs), value_rows, precision=lax.Precision.HIGHEST)

def split_block(block_rows):
    cut_point = LONG_DEV * LONG_LEN
    long_part = block_rows[:cut_point].reshape(LONG_DEV, LONG_LEN, HEADS, HEAD_DIM)
    short_part = block_rows[cut_point:].reshape(SHORT_DEV, SHORT_LEN, HEADS, HEAD_DIM)
    return (long_part, short_part)

def attend_block(packed):
    query_block, key_block, value_block, long_block, short_block = packed
    long_query, short_query = split_block(query_block)
    long_key, short_key = split_block(key_block)
    long_value, short_value = split_block(value_block)
    long_context = attend_group(long_query, long_key, long_value, long_block)
    short_context = attend_group(short_query, short_key, short_value, short_block)
    return jnp.concatenate([long_context.reshape(LONG_DEV * LONG_LEN, D), short_context.reshape(SHORT_DEV * SHORT_LEN, D)], 0)

def block_view(array_in):
    return array_in.reshape(N_DP, TOK_DEV, D)

def one_layer(states, w_qkv, bias_qv, w_out, bias_out, gain_pair, shift_pair, w_up, bias_up, w_down, bias_down, long_lengths, short_lengths, fixed_bounds):
    high = lax.Precision.HIGHEST
    rms_input = jnp.sqrt(jnp.mean(states * states))
    clipped_in, bound_in = soft_clip(states, pick_bound(fixed_bounds, 0))
    inputs_low = low(clipped_in)
    projected = jnp.einsum('td,kde->kte', inputs_low, w_qkv, precision=high)
    queries = low(low_back(projected[0] + bias_qv[0]))
    key_rows = low(low_back(projected[1]))
    value_rows = low(low_back(projected[2] + bias_qv[1]))
    context = lax.map(jax.checkpoint(attend_block), (block_view(queries), block_view(key_rows), block_view(value_rows), long_lengths.reshape(N_DP, LONG_DEV), short_lengths.reshape(N_DP, SHORT_DEV)))
    context = low_back(context.reshape(TOKENS, D))
    clipped_ctx, bound_ctx = soft_clip(context, pick_bound(fixed_bounds, 1))
    context_low = low(clipped_ctx)
    branch = low_back(jnp.dot(context_low, w_out, precision=high) + bias_out)
    middle = layer_norm(states + branch, gain_pair[0], shift_pair[0])
    clipped_mid, bound_mid = soft_clip(middle, pick_bound(fixed_bounds, 2))
    middle_low = low(clipped_mid)
    hidden_units = low_back(jnp.dot(middle_low, w_up, precision=high) + bias_up)
    active = jax.nn.gelu(hidden_units, approximate=False)
    clipped_act, bound_act = soft_clip(active, pick_bound(fixed_bounds, 3))
    active_low = low(clipped_act)
    branch_ffn = low_back(jnp.dot(active_low, w_down, precision=high) + bias_down)
    result = layer_norm(middle + branch_ffn, gain_pair[1], shift_pair[1])
    rms_row = jnp.stack([rms_input, jnp.sqrt(jnp.mean(branch * branch)), jnp.sqrt(jnp.mean(branch_ffn * branch_ffn))])
    return (result, (rms_row, jnp.stack([bound_in, bound_ctx, bound_mid, bound_act])))

def stack_forward(hidden, w_qkv, bias_qv, w_out, bias_out, ln_gain, ln_bias, w_up, bias_up, w_down, bias_down, long_lengths, short_lengths, fixed_bounds):
    states = hidden
    rms_rows = []
    bound_rows = []
    for layer_index in range(LAYERS):
        layer_bounds = pick_bound(fixed_bounds, layer_index)
        states, extras = jax.checkpoint(one_layer)(states, w_qkv[layer_index], bias_qv[layer_index], w_out[layer_index], bias_out[layer_index], ln_gain[layer_index], ln_bias[layer_index], w_up[layer_index], bias_up[layer_index], w_down[layer_index], bias_down[layer_index], long_lengths, short_lengths, layer_bounds)
        rms_rows.append(extras[0])
        bound_rows.append(extras[1])
    return (states, (jnp.stack(rms_rows), jnp.stack(bound_rows)))

def reference(hidden, long_lengths, short_lengths, w_qkv, bias_qv, w_out, bias_out, ln_gain, ln_bias, w_up, bias_up, w_down, bias_down, cotangent):
    floats = (hidden.astype(jnp.float32), w_qkv.astype(jnp.float32), bias_qv.astype(jnp.float32), w_out.astype(jnp.float32), bias_out.astype(jnp.float32), ln_gain.astype(jnp.float32), ln_bias.astype(jnp.float32), w_up.astype(jnp.float32), bias_up.astype(jnp.float32), w_down.astype(jnp.float32), bias_down.astype(jnp.float32))
    first_out, first_extras = stack_forward(*floats, long_lengths=long_lengths, short_lengths=short_lengths, fixed_bounds=None)
    forward_fn = partial(stack_forward, long_lengths=long_lengths, short_lengths=short_lengths, fixed_bounds=first_extras[1])
    result, pull_back, extras = jax.vjp(forward_fn, *floats, has_aux=True)
    rms_values = extras[0]
    grads = pull_back(cotangent.astype(jnp.float32))
    return (result.astype(jnp.bfloat16), grads[0], grads[1], grads[2], grads[3], grads[4], grads[5], grads[6], grads[7], grads[8], grads[9], grads[10], rms_values)
```

```python
from functools import partial

import jax
import jax.numpy as jnp
from jax import lax
from jax.experimental import pallas as pl
from jax.experimental.pallas import tpu as pltpu
from jax.sharding import PartitionSpec as P

HEAD_DIM = 64
LAYERS = 2
LONG_LEN = 512
SHORT_LEN = 128
LONG_DEV = 1
SHORT_DEV = 4

EPS = 1e-06
MASKED = -1e30
BOTH = ("dp", "tensor")
F32 = jnp.float32
BF16 = jnp.bfloat16
VMEM_LIMIT = 40 * 1024 * 1024


def nt(left, right):
    return lax.dot_general(left, right, (((1,), (1,)), ((), ())), preferred_element_type=F32)


def nn(left, right):
    return jnp.dot(left, right, preferred_element_type=F32)


def tn(left, right):
    return lax.dot_general(left, right, (((0,), (0,)), ((), ())), preferred_element_type=F32)


def bound_of(top_ref):
    return jnp.max(top_ref[...]) * 0.25 + EPS


def note_top(top_ref, step, values):
    largest = jnp.full(top_ref.shape, jnp.max(jnp.abs(values)), F32)

    @pl.when(step == 0)
    def _():
        top_ref[...] = largest

    @pl.when(step > 0)
    def _():
        top_ref[...] = jnp.maximum(top_ref[...], largest)


def halves(scal, width):
    part = width // 2
    near = scal[1]
    first = pl.ds(pl.multiple_of(near * part, part), part)
    second = pl.ds(pl.multiple_of((1 - near) * part, part), part)
    return first, second


def qkv_kernel(scal, x_ref, top_ref, own_ref, near_ref, far_ref, bown_ref, both_ref, a_ref, fac_ref, out_ref):
    bound = bound_of(top_ref)
    tangent = jnp.tanh(x_ref[...] * (1.0 / bound))
    low = (bound * tangent).astype(BF16)
    a_ref[...] = low
    fac_ref[...] = (1.0 - tangent * tangent).astype(BF16)
    first, second = halves(scal, low.shape[1])
    low_first, low_second = a_ref[:, first], a_ref[:, second]
    for j in range(3):
        own = nn(low, own_ref[0, j])
        oth = nn(low_first, near_ref[j]) + nn(low_second, far_ref[j])
        if j != 1:
            own = own + bown_ref[0, j // 2][None, :]
            oth = oth + both_ref[0, j // 2][None, :]
        out_ref[0, j] = own.astype(BF16)
        out_ref[1, j] = oth.astype(BF16)


def row_ids(scal, slots, half_rows):
    rows = 2 * half_rows
    slot = jnp.where(slots + half_rows * scal[2] >= rows, slots + half_rows * scal[2] - rows, slots + half_rows * scal[2])
    slot = slot + scal[0] * rows
    short = slot - LONG_DEV * LONG_LEN
    is_long = short < 0
    row = jnp.where(is_long, slot // LONG_LEN, LONG_DEV + short // SHORT_LEN)
    place = jnp.where(is_long, slot % LONG_LEN, short % SHORT_LEN)
    length = jnp.zeros_like(row)
    for i in range(LONG_DEV + SHORT_DEV):
        length = jnp.where(row == i, scal[3 + i], length)
    return row, place < length


HEADS = ((0, 128, 0), (0, 128, 1), (128, 192, None))


def lane_mask(rows, which):
    lane = lax.broadcasted_iota(jnp.int32, (rows, 128), 1)
    return (lane < HEAD_DIM) if which == 0 else (lane >= HEAD_DIM)


def only_head(values, which):
    if which is None:
        return values
    return jnp.where(lane_mask(values.shape[0], which), values, jnp.zeros_like(values))


def attend_kernel(scal, qkv_ref, ctx_ref, e_ref, rinv_ref, top_ref, bias_ref):
    step = pl.program_id(0)
    rows = qkv_ref.shape[2]

    @pl.when(step == 0)
    def _():
        q_row, _ = row_ids(scal, lax.broadcasted_iota(jnp.int32, (rows, 1), 0), rows // 2)
        k_row, k_live = row_ids(scal, lax.broadcasted_iota(jnp.int32, (1, rows), 1), rows // 2)
        k_row = jnp.where(k_live, k_row, -1)
        bias_ref[...] = jnp.where(q_row == k_row, 0.0, MASKED)

    scale = HEAD_DIM ** (-0.5)
    chunk = 128
    heads = []
    for h, (lo, hi, which) in enumerate(HEADS):
        keys = only_head(qkv_ref[0, 1, :, lo:hi], which)
        heads.append((h, lo, hi, which, keys, qkv_ref[0, 2, :, lo:hi]))
    for begin in range(0, rows, chunk):
        span = slice(begin, begin + chunk)
        done = []
        for h, lo, hi, which, keys, vals in heads:
            scores = nt(qkv_ref[0, 0, span, lo:hi], keys) * scale + bias_ref[span, :]
            weights = jnp.exp(scores - jnp.max(scores, axis=1, keepdims=True))
            inverse = 1.0 / jnp.sum(weights, axis=1, keepdims=True)
            low = weights.astype(BF16)
            e_ref[0, h, span, :] = low
            done.append((nn(low, vals) * inverse, inverse))
        left = lane_mask(chunk, 0)
        ctx_ref[0, span, 0:128] = jnp.where(left, done[0][0], done[1][0])
        ctx_ref[0, span, 128:192] = done[2][0]
        rinv_ref[0, span, 0:128] = jnp.where(left, done[0][1], done[1][1])
        rinv_ref[0, span, 128:192] = jnp.broadcast_to(done[2][1], (chunk, HEAD_DIM))
    note_top(top_ref, step, ctx_ref[...])


def out_kernel(scal, ctx_ref, top_ref, own_ref, near_ref, far_ref, c_ref, fac_ref, o_ref):
    bound = bound_of(top_ref)
    tangent = jnp.tanh(ctx_ref[...] * (1.0 / bound))
    c_ref[...] = (bound * tangent).astype(BF16)
    fac_ref[...] = (1.0 - tangent * tangent).astype(BF16)
    for part, ref in zip(halves(scal, o_ref.shape[1]), (near_ref, far_ref)):
        o_ref[:, part] = (nn(c_ref[0], own_ref[0, :, part]) + nn(c_ref[1], ref[...])).astype(BF16)


def norm_kernel(last, x_ref, self_ref, recv_ref, bias_ref, gain_ref, shift_ref, *outs):
    step = pl.program_id(0)
    branch = self_ref[...].astype(F32) + recv_ref[...].astype(F32) + bias_ref[...]
    mixed = x_ref[...].astype(F32) + branch
    centred = mixed - jnp.mean(mixed, axis=1, keepdims=True)
    inverse = lax.rsqrt(jnp.mean(centred * centred, axis=1, keepdims=True) + EPS)
    unit = centred * inverse
    result = unit * gain_ref[...] + shift_ref[...]
    h_ref, unit_ref, inv_ref, sums_ref = outs[:4]
    h_ref[...] = result.astype(h_ref.dtype)
    unit_ref[...] = unit
    inv_ref[...] = jnp.broadcast_to(inverse, inv_ref.shape)

    @pl.when(step == 0)
    def _():
        sums_ref[0:1, :] = jnp.full((1, 128), jnp.sum(branch * branch), F32)
        sums_ref[1:2, :] = jnp.full((1, 128), jnp.sum(result * result), F32)

    if not last:
        note_top(outs[4], step, result)


def up_kernel(scal, h_ref, top_ref, own_ref, near_ref, far_ref, bown_ref, both_ref, low_ref, fac_ref, g_ref, slope_ref, gtop_ref):
    step = pl.program_id(0)
    bound = bound_of(top_ref)
    tangent = jnp.tanh(h_ref[...] * (1.0 / bound))
    low = (bound * tangent).astype(BF16)
    low_ref[...] = low
    fac_ref[...] = (1.0 - tangent * tangent).astype(BF16)
    first, second = halves(scal, low.shape[1])
    for side in range(2):
        if side == 0:
            units = nn(low, own_ref[0]) + bown_ref[...]
        else:
            units = nn(low_ref[:, first], near_ref[...]) + nn(low_ref[:, second], far_ref[...]) + both_ref[...]
        area = 0.5 + 0.5 * lax.erf(units * (0.5**0.5))
        density = jnp.exp(-0.5 * units * units) * 0.3989422804014327
        g_ref[side] = units * area
        slope_ref[side] = (area + units * density).astype(BF16)
    note_top(gtop_ref, step, g_ref[...])


def down_kernel(scal, g_ref, slope_ref, top_ref, own_ref, near_ref, far_ref, low_ref, fac_ref, f_ref):
    bound = bound_of(top_ref)
    tangent = jnp.tanh(g_ref[...] * (1.0 / bound))
    low_ref[...] = (bound * tangent).astype(BF16)
    fac_ref[...] = ((1.0 - tangent * tangent) * slope_ref[...].astype(F32)).astype(BF16)
    first, second = halves(scal, g_ref.shape[2])
    f_ref[...] = (
        nn(low_ref[0], own_ref[0])
        + nn(low_ref[1, :, first], near_ref[...])
        + nn(low_ref[1, :, second], far_ref[...])
    ).astype(BF16)


def norm_back(grad, unit, inverse, gain):
    scaled = grad * gain
    return (
        scaled
        - jnp.mean(scaled, axis=1, keepdims=True)
        - unit * jnp.mean(scaled * unit, axis=1, keepdims=True)
    ) * inverse


def norm_sums(sums_ref, step, grad, unit, low):
    @pl.when(step == 0)
    def _():
        sums_ref[0:1, :] = jnp.sum(grad * unit, axis=0, keepdims=True)
        sums_ref[1:2, :] = jnp.sum(grad, axis=0, keepdims=True)
        sums_ref[2:3, :] = jnp.sum(low.astype(F32), axis=0, keepdims=True)


def ffn_back_kernel(from_input, scal, *refs):
    step = pl.program_id(0)
    if from_input:
        dy_ref, refs = refs[0], refs[1:]
        grad = dy_ref[...].astype(F32)
    else:
        (self_ref, recv_ref, infac_ref, skip_ref), refs = refs[:4], refs[4:]
        grad = (self_ref[...].astype(F32) + recv_ref[...].astype(F32)) * infac_ref[...].astype(F32) + skip_ref[...]
    (unit_ref, inv_ref, gain_ref, fac_ref, down_ref, dnear_ref, dfar_ref, up_ref, unear_ref, ufar_ref) = refs[:10]
    dz_ref, df_ref, du_ref, dh_ref, sums_ref, usum_ref = refs[10:]
    unit = unit_ref[...]
    mixed = norm_back(grad, unit, inv_ref[:, 0:1], gain_ref[...])
    low = mixed.astype(BF16)
    dz_ref[...] = mixed
    df_ref[...] = low
    norm_sums(sums_ref, step, grad, unit, low)
    first, second = halves(scal, low.shape[1])
    du_ref[0] = (nt(low, down_ref[0]) * fac_ref[0].astype(F32)).astype(BF16)
    for part, ref in ((first, dnear_ref), (second, dfar_ref)):
        du_ref[1, :, part] = (nt(low, ref[...]) * fac_ref[1, :, part].astype(F32)).astype(BF16)
    for part, ref in ((first, unear_ref), (second, ufar_ref)):
        dh_ref[:, part] = (nt(du_ref[0], up_ref[0, part, :]) + nt(du_ref[1], ref[...])).astype(BF16)
    for side in range(2):
        total = jnp.sum(du_ref[side].astype(F32), axis=0, keepdims=True)

        @pl.when(step == 0)
        def _():
            usum_ref[side : side + 1, :] = total

        @pl.when(step > 0)
        def _():
            usum_ref[side : side + 1, :] += total


def out_back_kernel(scal, self_ref, recv_ref, hfac_ref, skip_ref, unit_ref, inv_ref, gain_ref, cfac_ref, own_ref, near_ref, far_ref, dz_ref, do_ref, dctx_ref, sums_ref):
    step = pl.program_id(0)
    grad = (self_ref[...].astype(F32) + recv_ref[...].astype(F32)) * hfac_ref[...].astype(F32) + skip_ref[...]
    unit = unit_ref[...]
    mixed = norm_back(grad, unit, inv_ref[:, 0:1], gain_ref[...])
    low = mixed.astype(BF16)
    dz_ref[...] = mixed
    do_ref[...] = low
    norm_sums(sums_ref, step, grad, unit, low)
    first, second = halves(scal, low.shape[1])
    dctx_ref[0] = nt(low, own_ref[0]) * cfac_ref[0].astype(F32)
    oth = nt(do_ref[:, first], near_ref[...]) + nt(do_ref[:, second], far_ref[...])
    dctx_ref[1] = oth * cfac_ref[1].astype(F32)


def attend_back_kernel(qkv_ref, e_ref, rinv_ref, dctx_ref, ctx_ref, out_ref, sums_ref):
    rows = qkv_ref.shape[2]
    scale = HEAD_DIM ** (-0.5)
    low = (dctx_ref[0] * rinv_ref[0]).astype(BF16)
    product = low.astype(F32) * ctx_ref[0]
    results = []
    for h, (lo, hi, which) in enumerate(HEADS):
        inner = jnp.sum(only_head(product[:, lo:hi], which), axis=1, keepdims=True)
        values = only_head(qkv_ref[0, 2, :, lo:hi], which)
        weights = e_ref[0, h]
        grad_weights = nt(low[:, lo:hi], values)
        grad_scores = (weights.astype(F32) * (grad_weights - inner)).astype(BF16)
        dq = nn(grad_scores, qkv_ref[0, 1, :, lo:hi]) * scale
        dk = tn(grad_scores, qkv_ref[0, 0, :, lo:hi]) * scale
        dv = tn(weights, low[:, lo:hi])
        results.append((dq, dk, dv))
    left = lane_mask(rows, 0)
    for j in range(3):
        pair = jnp.where(left, results[0][j], results[1][j]).astype(BF16)
        last = results[2][j].astype(BF16)
        out_ref[0, j, :, 0:128] = pair
        out_ref[0, j, :, 128:192] = last
        if j != 1:
            place = slice(j // 2, j // 2 + 1)
            sums_ref[0, place, 0:128] = jnp.sum(pair.astype(F32), axis=0, keepdims=True)
            sums_ref[0, place, 128:192] = jnp.sum(last.astype(F32), axis=0, keepdims=True)


def qkv_back_kernel(scal, d_ref, own_ref, near_ref, far_ref, da_ref):
    for part, ref in zip(halves(scal, da_ref.shape[1]), (near_ref, far_ref)):
        total = nt(d_ref[0, 0], own_ref[0, 0, part, :]) + nt(d_ref[1, 0], ref[0])
        for j in (1, 2):
            total = total + nt(d_ref[0, j], own_ref[0, j, part, :]) + nt(d_ref[1, j], ref[j])
        da_ref[:, part] = total.astype(BF16)


def ffn_grad_kernel(df_ref, gq_ref, hq_ref, du_ref, down_own, down_oth, up_own, up_oth):
    down_own[...] = tn(df_ref[...], gq_ref[0])
    down_oth[...] = tn(df_ref[...], gq_ref[1]).astype(BF16)
    up_own[...] = tn(hq_ref[...], du_ref[0])
    up_oth[...] = tn(hq_ref[...], du_ref[1]).astype(BF16)


def attn_grad_kernel(a_ref, d_ref, do_ref, c_ref, own_a, oth_a, own_b, oth_b):
    for j in range(2):
        own_a[j] = tn(a_ref[...], d_ref[0, j])
        oth_a[j] = tn(a_ref[...], d_ref[1, j]).astype(BF16)
    own_b[0] = tn(a_ref[...], d_ref[0, 2])
    oth_b[0] = tn(a_ref[...], d_ref[1, 2]).astype(BF16)
    own_b[1] = tn(do_ref[...], c_ref[0])
    oth_b[1] = tn(do_ref[...], c_ref[1]).astype(BF16)


def spec(shape, index):
    return pl.BlockSpec(shape, index)


def whole(array):
    dims = len(array.shape)
    return pl.BlockSpec(array.shape, lambda i: (0,) * dims)


def layer_block(array, layer):
    dims = len(array.shape)
    return pl.BlockSpec((1,) + array.shape[1:], lambda i: (layer,) + (0,) * (dims - 1))


SCALARS = pl.BlockSpec(memory_space=pltpu.SMEM)


def run(kernel, steps, ins, outs, name, flops=0, scratch=()):
    arrays = [array for array, _ in ins]
    moved = sum(a.size * a.dtype.itemsize for a in arrays) + sum(
        jax.ShapeDtypeStruct(s, d).size * jnp.dtype(d).itemsize for s, d, _ in outs
    )
    return pl.pallas_call(
        kernel,
        grid=(steps,),
        in_specs=[s for _, s in ins],
        out_specs=[s for _, _, s in outs],
        out_shape=[jax.ShapeDtypeStruct(s, d) for s, d, _ in outs],
        scratch_shapes=list(scratch),
        name=name,
        cost_estimate=pl.CostEstimate(flops=int(flops), bytes_accessed=int(moved), transcendentals=0),
        compiler_params=pltpu.CompilerParams(vmem_limit_bytes=VMEM_LIMIT),
    )(*arrays)


def body(
    hidden,
    long_lengths,
    short_lengths,
    w_qkv,
    bias_qv,
    w_out,
    bias_out,
    ln_gain,
    ln_bias,
    w_up,
    bias_up,
    w_down,
    bias_down,
    cotangent,
):
    own_rows, width = hidden.shape
    rows = 2 * own_rows
    heads_width = w_qkv.shape[-1]
    units = w_up.shape[-1]
    dp_size, tensor_size = lax.axis_size("dp"), lax.axis_size("tensor")
    devices = dp_size * tensor_size
    count_model = float(own_rows * devices * width)
    dp_index, tensor_index = lax.axis_index("dp"), lax.axis_index("tensor")
    x_index, core_index, y_index = tensor_index // 2, tensor_index % 2, dp_index % 2
    core_pairs = [(i, i ^ 1) for i in range(tensor_size)]
    x_pairs = [(i, i ^ 2) for i in range(tensor_size)]
    dp_pairs = lambda bit: [(i, i ^ bit) for i in range(dp_size)]
    core_swap = lambda v: lax.ppermute(v, "tensor", core_pairs)
    x_swap = lambda v: lax.ppermute(v, "tensor", x_pairs)
    dp_swap = lambda v, bit: lax.ppermute(v, "dp", dp_pairs(bit))

    scal = jnp.concatenate(
        [jnp.stack([x_index, y_index, core_index]).astype(jnp.int32), long_lengths, short_lengths]
    )
    blk = own_rows
    steps = 2

    def over_ranks(top):
        return lax.all_to_all(top, BOTH, 0, 0)

    def relay(values, axis):
        part = values.shape[axis] // 2
        near = x_swap(lax.dynamic_slice_in_dim(values, y_index * part, part, axis))
        return near, dp_swap(near, 1)

    row_block = lambda a: (a, spec((blk,) + a.shape[1:], lambda i: (i, 0)))
    swapped = lambda a: (a, spec((blk,) + a.shape[1:], lambda i: (1 - i, 0)))
    side_block = lambda a: (a, spec((2, blk, a.shape[2]), lambda i: (0, i, 0)))
    full = lambda a: (a, whole(a))
    scalars = (scal, SCALARS)
    out_rows = lambda w, d: ((rows, w), d, spec((blk, w), lambda i: (i, 0)))
    out_sides = lambda w, d: ((2, rows, w), d, spec((2, blk, w), lambda i: (0, i, 0)))
    fixed = lambda s, d: (s, d, spec(s, lambda i: (0,) * len(s)))
    top_shape = (devices, 1, 128)

    hidden_full = jnp.concatenate([hidden, core_swap(hidden)], 0)

    def top_kernel(x_ref, top_ref, sums_ref):
        values = x_ref[...].astype(F32)
        note_top(top_ref, pl.program_id(0), values)
        sums_ref[...] = jnp.full((1, 128), jnp.sum(values * values), F32)

    top, input_sum = run(
        top_kernel, 1, [full(hidden)], [fixed(top_shape, F32), fixed((1, 128), F32)], "input_top"
    )
    top = over_ranks(top)
    states = hidden_full.astype(F32)

    small = jnp.concatenate([bias_qv.reshape(LAYERS, 2 * heads_width), bias_up], 1)
    small = x_swap(small)
    oth_bias_qv = small[:, : 2 * heads_width].reshape(LAYERS, 2, heads_width)
    oth_bias_up = small[:, 2 * heads_width :]
    saved = []
    square_terms = []
    for l in range(LAYERS):
        last = l == LAYERS - 1
        qkv_near, qkv_far = relay(w_qkv[l], 1)
        out_near, out_far = relay(w_out[l], 1)
        up_near, up_far = relay(w_up[l], 0)
        down_near, down_far = relay(w_down[l], 0)
        low_in, fac_in, qkv = run(
            qkv_kernel,
            steps,
            [scalars, row_block(states), full(top), (w_qkv, layer_block(w_qkv, l)), full(qkv_near), full(qkv_far),
             (bias_qv, layer_block(bias_qv, l)), (oth_bias_qv, layer_block(oth_bias_qv, l))],
            [out_rows(width, BF16), out_rows(width, BF16),
             ((2, 3, rows, heads_width), BF16, spec((2, 3, blk, heads_width), lambda i: (0, 0, i, 0)))],
            "qkv",
            flops=2 * rows * width * heads_width * 6,
        )
        ctx, weights, rinv, top = run(
            attend_kernel,
            2,
            [scalars, (qkv, spec((1, 3, rows, heads_width), lambda i: (i, 0, 0, 0)))],
            [((2, rows, heads_width), F32, spec((1, rows, heads_width), lambda i: (i, 0, 0))),
             ((2, 3, rows, rows), BF16, spec((1, 3, rows, rows), lambda i: (i, 0, 0, 0))),
             ((2, rows, heads_width), F32, spec((1, rows, heads_width), lambda i: (i, 0, 0))),
             fixed(top_shape, F32)],
            "attend",
            flops=12 * rows * rows * 128 * 8,
            scratch=[pltpu.VMEM((rows, rows), F32)],
        )
        top = over_ranks(top)
        low_ctx, fac_ctx, part = run(
            out_kernel,
            steps,
            [scalars, side_block(ctx), full(top), (w_out, layer_block(w_out, l)), full(out_near), full(out_far)],
            [out_sides(heads_width, BF16), out_sides(heads_width, BF16), out_rows(width, BF16)],
            "out_proj",
            flops=4 * rows * width * heads_width,
        )
        gain = ln_gain[l]
        shift = ln_bias[l]
        row_vec = lambda v: full(v.reshape(1, -1))
        middle, unit_one, inv_one, sums_one, top = run(
            partial(norm_kernel, False),
            steps,
            [row_block(states), row_block(part), swapped(core_swap(part)), row_vec(bias_out[l]), row_vec(gain[0]), row_vec(shift[0])],
            [out_rows(width, F32), out_rows(width, F32), out_rows(128, F32), fixed((2, 128), F32), fixed(top_shape, F32)],
            "norm_one",
        )
        top = over_ranks(top)
        low_mid, fac_mid, active, slope, top = run(
            up_kernel,
            steps,
            [scalars, row_block(middle), full(top), (w_up, layer_block(w_up, l)), full(up_near), full(up_far),
             row_vec(bias_up[l]), row_vec(oth_bias_up[l])],
            [out_rows(width, BF16), out_rows(width, BF16), out_sides(units, F32), out_sides(units, BF16), fixed(top_shape, F32)],
            "up_proj",
            flops=4 * rows * width * units,
        )
        top = over_ranks(top)
        low_act, fac_act, part = run(
            down_kernel,
            steps,
            [scalars, side_block(active), side_block(slope), full(top), (w_down, layer_block(w_down, l)), full(down_near), full(down_far)],
            [out_sides(units, BF16), out_sides(units, BF16), out_rows(width, BF16)],
            "down_proj",
            flops=4 * rows * width * units,
        )
        outs = run(
            partial(norm_kernel, last),
            steps,
            [row_block(middle), row_block(part), swapped(core_swap(part)), row_vec(bias_down[l]), row_vec(gain[1]), row_vec(shift[1])],
            [out_rows(width, BF16 if last else F32), out_rows(width, F32), out_rows(128, F32), fixed((2, 128), F32)]
            + ([] if last else [fixed(top_shape, F32)]),
            "norm_two",
        )
        unit_two, inv_two, sums_two = outs[1:4]
        square_terms += [input_sum[0, 0], sums_one[0, 0], sums_two[0, 0]]
        input_sum = sums_two[1:2]
        saved.append(
            (low_in, fac_in, qkv, ctx, weights, rinv, low_ctx, fac_ctx, unit_one, inv_one, low_mid, fac_mid,
             low_act, fac_act, unit_two, inv_two, gain, qkv_near, qkv_far, out_near, out_far, up_near, up_far, down_near, down_far)
        )
        states = outs[0]
        if not last:
            top = over_ranks(outs[4])
    output = states[:own_rows]

    cot_full = jnp.concatenate([cotangent, core_swap(cotangent)], 0)

    def take(values, index):
        return lax.dynamic_index_in_dim(values, index, 2, keepdims=False)

    def fold_dp(total, begin_bit):
        bit = begin_bit
        while bit < dp_size:
            mine = (dp_index // bit) % 2
            shape = total.shape
            view = total.reshape(shape[0], shape[1] // 2, 2, *shape[2:])
            total = take(view, mine) + dp_swap(take(view, 1 - mine).astype(BF16), bit).astype(F32)
            bit *= 2
        return total[:, 0]

    def by_slices(values):
        return values.reshape(values.shape[0], dp_size, values.shape[1] // dp_size, values.shape[2])

    def reduce_x_first(own, oth):
        total = own + x_swap(oth).astype(F32)
        return fold_dp(by_slices(total), 1)

    def reduce_y_first(own, oth):
        mine = y_index
        own, oth = by_slices(own), by_slices(oth)
        pair = lambda v: v.reshape(v.shape[0], dp_size // 2, 2, *v.shape[2:])
        own, oth = pair(own), pair(oth)
        away = jnp.stack([take(own, 1 - mine).astype(BF16), take(oth, 1 - mine)])
        got = dp_swap(away, 1).astype(F32)
        other = (take(oth, mine).astype(F32) + got[1]).astype(BF16)
        total = take(own, mine) + got[0] + x_swap(other).astype(F32)
        return fold_dp(total, 2)

    grads = [None] * LAYERS
    sums = [None] * LAYERS
    grad_source = None
    for l in reversed(range(LAYERS)):
        (low_in, fac_in, qkv, ctx, weights, rinv, low_ctx, fac_ctx, unit_one, inv_one, low_mid, fac_mid,
         low_act, fac_act, unit_two, inv_two, gain, qkv_near, qkv_far, out_near, out_far, up_near, up_far, down_near, down_far) = saved[l]
        if grad_source is None:
            first_ins = [row_block(cot_full)]
        else:
            part, fac, skip = grad_source
            first_ins = [row_block(part), swapped(core_swap(part)), row_block(fac), row_block(skip)]
        dz_two, df, du, part, sums_two, unit_sums = run(
            partial(ffn_back_kernel, grad_source is None),
            steps,
            [scalars] + first_ins
            + [row_block(unit_two), row_block(inv_two), row_vec(gain[1]), side_block(fac_act),
               (w_down, layer_block(w_down, l)), full(down_near), full(down_far),
               (w_up, layer_block(w_up, l)), full(up_near), full(up_far)],
            [out_rows(width, F32), out_rows(width, BF16), out_sides(units, BF16), out_rows(width, BF16),
             fixed((3, width), F32), fixed((2, units), F32)],
            "ffn_back",
            flops=8 * rows * width * units,
        )
        down_own, down_oth, up_own, up_oth = run(
            ffn_grad_kernel,
            1,
            [full(df), full(low_act), full(low_mid), full(du)],
            [fixed((width, units), F32), fixed((width, units), BF16), fixed((width, units), F32), fixed((width, units), BF16)],
            "ffn_grad",
            flops=8 * rows * width * units,
        )
        dz_one, do, dctx, sums_one = run(
            out_back_kernel,
            steps,
            [scalars, row_block(part), swapped(core_swap(part)), row_block(fac_mid), row_block(dz_two), row_block(unit_one),
             row_block(inv_one), row_vec(gain[0]), side_block(fac_ctx), (w_out, layer_block(w_out, l)), full(out_near), full(out_far)],
            [out_rows(width, F32), out_rows(width, BF16), out_sides(heads_width, F32), fixed((3, width), F32)],
            "out_back",
            flops=4 * rows * width * heads_width,
        )
        per_side = lambda a: (a, spec((1,) + a.shape[1:], lambda i: (i,) + (0,) * (len(a.shape) - 1)))
        dqkv, head_sums = run(
            attend_back_kernel,
            2,
            [per_side(qkv), per_side(weights), per_side(rinv), per_side(dctx), per_side(ctx)],
            [((2, 3, rows, heads_width), BF16, spec((1, 3, rows, heads_width), lambda i: (i, 0, 0, 0))),
             ((2, 2, heads_width), F32, spec((1, 2, heads_width), lambda i: (i, 0, 0)))],
            "attend_back",
            flops=6 * rows * rows * 128 * 8,
        )
        (part,) = run(
            qkv_back_kernel,
            steps,
            [scalars, (dqkv, spec((2, 3, blk, heads_width), lambda i: (0, 0, i, 0))), (w_qkv, layer_block(w_qkv, l)), full(qkv_near), full(qkv_far)],
            [out_rows(width, BF16)],
            "qkv_back",
            flops=2 * rows * width * heads_width * 6,
        )
        own_a, oth_a, own_b, oth_b = run(
            attn_grad_kernel,
            1,
            [full(low_in), full(dqkv), full(do), full(low_ctx)],
            [fixed((2, width, heads_width), F32), fixed((2, width, heads_width), BF16)] * 2,
            "attn_grad",
            flops=2 * rows * width * heads_width * 8,
        )
        grad_source = (part, fac_in, dz_one)
        grads[l] = (
            reduce_x_first(up_own[None], up_oth[None])[0],
            reduce_y_first(down_own[None], down_oth[None])[0],
            reduce_x_first(own_a, oth_a),
            reduce_y_first(own_b, oth_b),
        )
        sums[l] = (sums_one, sums_two, head_sums, unit_sums)
    part, fac, skip = grad_source
    grad_hidden = (
        part[:own_rows].astype(F32) + core_swap(part[own_rows:]).astype(F32)
    ) * fac[:own_rows].astype(F32) + skip[:own_rows]

    oth_index = tensor_index ^ 2
    pieces = []
    for l in range(LAYERS):
        sums_one, sums_two, head_sums, unit_sums = sums[l]
        pieces += [sums_one.reshape(-1), sums_two.reshape(-1)]
        for values in (head_sums.reshape(2, -1), unit_sums):
            spread = jnp.zeros((tensor_size, values.shape[1]), F32)
            spread = lax.dynamic_update_slice_in_dim(spread, values[0:1], tensor_index, 0)
            spread = lax.dynamic_update_slice_in_dim(spread, values[1:2], oth_index, 0)
            pieces.append(spread.reshape(-1))
    pieces.append(jnp.stack(square_terms))
    flat = jnp.concatenate(pieces)
    chunk = -(-flat.shape[0] // (devices * 128)) * 128
    flat = jnp.pad(flat, (0, devices * chunk - flat.shape[0])).reshape(devices, 1, chunk)
    mine = jnp.sum(lax.all_to_all(flat, BOTH, 0, 0), axis=0, keepdims=True)
    totals = lax.all_to_all(jnp.broadcast_to(mine, flat.shape), BOTH, 0, 0).reshape(-1)
    offset = 0

    def next_piece(shape):
        nonlocal offset
        size = 1
        for n in shape:
            size *= n
        value = totals[offset : offset + size].reshape(shape)
        offset += size
        return value

    gains, shifts, out_biases, down_biases, head_biases, unit_biases = [], [], [], [], [], []
    own_shard = lambda v: lax.dynamic_index_in_dim(v, tensor_index, 0, keepdims=False)
    for l in range(LAYERS):
        one = next_piece((3, width))
        two = next_piece((3, width))
        gains.append(jnp.stack([one[0], two[0]]))
        shifts.append(jnp.stack([one[1], two[1]]))
        out_biases.append(one[2])
        down_biases.append(two[2])
        head_biases.append(own_shard(next_piece((tensor_size, 2, heads_width))))
        unit_biases.append(own_shard(next_piece((tensor_size, units))))
    rms_values = jnp.sqrt(next_piece((LAYERS, 3)) / count_model)
    return (
        output,
        grad_hidden,
        jnp.stack([jnp.concatenate([g[2], g[3][0:1]], 0) for g in grads]),
        jnp.stack(head_biases),
        jnp.stack([g[3][1].T for g in grads]),
        jnp.stack(out_biases),
        jnp.stack(gains),
        jnp.stack(shifts),
        jnp.stack([g[0] for g in grads]),
        jnp.stack(unit_biases),
        jnp.stack([g[1].T for g in grads]),
        jnp.stack(down_biases),
        rms_values,
    )


def solution(mesh):
    in_specs = (
        P(("dp", "tensor"), None),
        P("dp"),
        P("dp"),
        P(None, None, None, "tensor"),
        P(None, None, "tensor"),
        P(None, "tensor", None),
        P(),
        P(),
        P(),
        P(None, None, "tensor"),
        P(None, "tensor"),
        P(None, "tensor", None),
        P(),
        P(("dp", "tensor"), None),
    )
    out_specs = (
        P(("dp", "tensor"), None),
        P(("dp", "tensor"), None),
        P(None, None, "dp", "tensor"),
        P(None, None, "tensor"),
        P(None, "tensor", "dp"),
        P(),
        P(),
        P(),
        P(None, "dp", "tensor"),
        P(None, "tensor"),
        P(None, "tensor", "dp"),
        P(),
        P(),
    )
    return jax.shard_map(body, mesh=mesh, in_specs=in_specs, out_specs=out_specs, check_vma=False)
```

```python
from functools import partial

import jax
import jax.numpy as jnp
from jax import lax
from jax.experimental import pallas as pl
from jax.experimental.pallas import tpu as pltpu
from jax.sharding import PartitionSpec as P

HEAD_DIM = 64
LAYERS = 2
LONG_LEN = 512
SHORT_LEN = 128
LONG_DEV = 1
SHORT_DEV = 4

EPS = 1e-06
MASKED = -1e30
BOTH = ("dp", "tensor")
F32 = jnp.float32
BF16 = jnp.bfloat16
VMEM_LIMIT = 60 * 1024 * 1024

X, Y, CORE, DP, SHARD, LENGTHS = range(6)


def nt(left, right):
    return lax.dot_general(left, right, (((1,), (1,)), ((), ())), preferred_element_type=F32)


def nn(left, right):
    return jnp.dot(left, right, preferred_element_type=F32)


def tn(left, right):
    return lax.dot_general(left, right, (((0,), (0,)), ((), ())), preferred_element_type=F32)


def merge(values):
    return values.reshape(values.shape[0] * values.shape[1], values.shape[2])


def bound_of(top_ref):
    return jnp.max(top_ref[...]) * 0.25 + EPS


def halves(scal, width):
    part = width // 2
    near = scal[Y]
    first = pl.ds(pl.multiple_of(near * part, part), part)
    second = pl.ds(pl.multiple_of((1 - near) * part, part), part)
    return first, second


class Load:
    def __init__(self, shape, dtype, pieces):
        self.shape, self.dtype, self.pieces = tuple(shape), dtype, pieces


class Store:
    def __init__(self, shape, dtype, pieces=((),)):
        self.shape, self.dtype, self.pieces = tuple(shape), dtype, pieces


def view(ref, index):
    return ref.at[index] if index else ref


class Arriving:
    def __init__(self, ref, copies):
        self.ref, self.copies, self.waited = ref, copies, set()

    def wait(self, piece):
        if piece not in self.waited:
            self.copies[piece].wait()
            self.waited.add(piece)
        return self.ref

    def all(self):
        for piece in range(len(self.copies)):
            self.wait(piece)
        return self.ref


class Leaving:
    def __init__(self, ref, copies):
        self.ref, self.copies, self.started = ref, copies, set()

    def flush(self, piece=0):
        self.copies[piece].start()
        self.started.add(piece)


def stream(scal, body, loads, stores, name, flops=0, scratch=(), after=()):
    arrays = []

    def slot(array):
        for i, known in enumerate(arrays):
            if known is array:
                return i
        arrays.append(array)
        return len(arrays) - 1

    plan = [[(slot(a), src, dst) for a, src, dst in load.pieces] for load in loads]
    first_out = len(arrays) + len(after)
    n_in = sum(len(p) for p in plan)
    n_out = sum(len(st.pieces) for st in stores)

    def kernel(scal_ref, *refs):
        sources = refs[: len(arrays)]
        targets = refs[first_out : first_out + len(stores)]
        at = first_out + len(stores)
        vin, at = refs[at : at + len(loads)], at + len(loads)
        vout, at = refs[at : at + len(stores)], at + len(stores)
        extra, (sem_in, sem_out) = refs[at:-2], refs[-2:]
        count = 0
        arriving = []
        for pieces, ref in zip(plan, vin):
            copies = []
            for i, src, dst in pieces:
                copies.append(pltpu.make_async_copy(view(sources[i], src), view(ref, dst), sem_in.at[count]))
                count += 1
            arriving.append(Arriving(ref, copies))
        for piece in range(max(len(p) for p in plan)):
            for a in arriving:
                if piece < len(a.copies):
                    a.copies[piece].start()
        count = 0
        leaving = []
        for st, ref, target in zip(stores, vout, targets):
            copies = []
            for index in st.pieces:
                copies.append(pltpu.make_async_copy(view(ref, index), view(target, index), sem_out.at[count]))
                count += 1
            leaving.append(Leaving(ref, copies))
        body(scal_ref, arriving, leaving, *extra)
        for a in arriving:
            a.all()
        for out in leaving:
            for piece, copy in enumerate(out.copies):
                if piece not in out.started:
                    copy.start()
        for out in leaving:
            for copy in out.copies:
                copy.wait()

    moved = sum(a.size * a.dtype.itemsize for a in arrays)
    for st in stores:
        size = jnp.dtype(st.dtype).itemsize
        for n in st.shape:
            size *= n
        moved += size
    anywhere = pl.BlockSpec(memory_space=pl.ANY)
    return pl.pallas_call(
        kernel,
        in_specs=[pl.BlockSpec(memory_space=pltpu.SMEM)] + [anywhere] * first_out,
        out_specs=[anywhere] * len(stores),
        out_shape=[jax.ShapeDtypeStruct(st.shape, st.dtype) for st in stores],
        scratch_shapes=[pltpu.VMEM(x.shape, x.dtype) for x in list(loads) + list(stores)]
        + list(scratch)
        + [pltpu.SemaphoreType.DMA((n_in,)), pltpu.SemaphoreType.DMA((n_out,))],
        name=name,
        cost_estimate=pl.CostEstimate(flops=int(flops), bytes_accessed=int(moved), transcendentals=0),
        compiler_params=pltpu.CompilerParams(vmem_limit_bytes=VMEM_LIMIT),
    )(scal, *arrays, *after)


ALL = slice(None)


def span(i, size):
    return pl.ds(i * size, size)


def whole_in(a):
    return Load(a.shape, a.dtype, [(a, (), ())])


def layer_in(a, layer):
    return Load(a.shape[1:], a.dtype, [(a, (layer,), ())])


def rows_in(a, count, swap=False):
    size = a.shape[0] // count
    turn = count // 2 if swap else 0
    return Load(a.shape, a.dtype, [(a, (span((i + turn) % count, size),), (span(i, size),)) for i in range(count)])


def pair_in(mine, other, count):
    rows, width = mine.shape
    size = 2 * rows // count
    half = count // 2
    return Load(
        (2 * rows, width),
        mine.dtype,
        [((mine if i < half else other), (span(i % half, size),), (span(i, size),)) for i in range(count)],
    )


def sides_in(a, count):
    size = a.shape[1] // count
    return Load(a.shape, a.dtype, [(a, (ALL, span(i, size)), (ALL, span(i, size))) for i in range(count)])


def per_side_in(a):
    return Load(a.shape, a.dtype, [(a, (i,), (i,)) for i in range(a.shape[0])])


def rows_out(shape, dtype, count):
    size = shape[0] // count
    return Store(shape, dtype, [(span(i, size),) for i in range(count)])


def sides_out(shape, dtype, count):
    size = shape[1] // count
    return Store(shape, dtype, [(ALL, span(i, size)) for i in range(count)])


def side_rows_out(shape, dtype, lead, count):
    size = shape[1 + lead] // count
    return Store(shape, dtype, [(s,) + (ALL,) * lead + (span(i, size),) for s in range(2) for i in range(count)])


def per_side_out(shape, dtype):
    return Store(shape, dtype, [(i,) for i in range(shape[0])])


B_OUT, GAIN_ONE, SHIFT_ONE, B_DOWN, GAIN_TWO, SHIFT_TWO, B_Q, B_V, B_UP, VECS = range(10)


def vec(ref, layer, row, width=None):
    at = layer * VECS + row
    return ref[at : at + 1, :] if width is None else ref[at : at + 1, 0:width]


def start_kernel(scal, hidden_ref, bout_ref, gain_ref, shift_ref, bdown_ref, bqv_ref, bup_ref, vecs_ref, small_ref, top_ref, sums_ref):
    heads_width = bqv_ref.shape[2]
    vecs_ref[...] = jnp.zeros(vecs_ref.shape, F32)
    small_ref[...] = jnp.zeros(small_ref.shape, F32)
    for layer in range(LAYERS):
        base = layer * VECS
        one = slice(layer, layer + 1)
        vecs_ref[base + B_OUT : base + B_OUT + 1, :] = bout_ref[one, :]
        vecs_ref[base + B_DOWN : base + B_DOWN + 1, :] = bdown_ref[one, :]
        vecs_ref[base + GAIN_ONE : base + GAIN_ONE + 1, :] = gain_ref[layer, 0:1, :]
        vecs_ref[base + GAIN_TWO : base + GAIN_TWO + 1, :] = gain_ref[layer, 1:2, :]
        vecs_ref[base + SHIFT_ONE : base + SHIFT_ONE + 1, :] = shift_ref[layer, 0:1, :]
        vecs_ref[base + SHIFT_TWO : base + SHIFT_TWO + 1, :] = shift_ref[layer, 1:2, :]
        for ref, at in ((vecs_ref, base + B_Q), (small_ref, 3 * layer)):
            ref[at : at + 1, 0:heads_width] = bqv_ref[layer, 0:1, :]
            ref[at + 1 : at + 2, 0:heads_width] = bqv_ref[layer, 1:2, :]
            ref[at + 2 : at + 3, :] = bup_ref[one, :]
    values = hidden_ref[...].astype(F32)
    top_ref[...] = jnp.full(top_ref.shape, jnp.max(jnp.abs(values)), F32)
    sums_ref[...] = jnp.full((1, 128), jnp.sum(values * values), F32)


def halves_kernel(scal, wqkv_ref, wout_ref, wup_ref, wdown_ref, *refs):
    att_ref, up_ref, down_ref = refs[-3:]
    att_ref[0:3] = wqkv_ref[...]
    att_ref[3] = wout_ref[...]
    up_ref[...] = wup_ref[...]
    down_ref[...] = wdown_ref[...]


def row_ids(scal, slots, half_rows):
    rows = 2 * half_rows
    slot = slots + half_rows * scal[CORE]
    slot = jnp.where(slot >= rows, slot - rows, slot) + scal[X] * rows
    short = slot - LONG_DEV * LONG_LEN
    is_long = short < 0
    row = jnp.where(is_long, slot // LONG_LEN, LONG_DEV + short // SHORT_LEN)
    place = jnp.where(is_long, slot % LONG_LEN, short % SHORT_LEN)
    length = jnp.zeros_like(row)
    for i in range(LONG_DEV + SHORT_DEV):
        length = jnp.where(row == i, scal[LENGTHS + i], length)
    return row, place < length


HEADS = ((0, 128, 0), (0, 128, 1), (128, 192, None))


def lane_mask(rows, which):
    lane = lax.broadcasted_iota(jnp.int32, (rows, 128), 1)
    return (lane < HEAD_DIM) if which == 0 else (lane >= HEAD_DIM)


def only_head(values, which):
    if which is None:
        return values
    return jnp.where(lane_mask(values.shape[0], which), values, jnp.zeros_like(values))


def largest(values):
    return jnp.max(jnp.abs(values))


def put_top(out, tops):
    top = tops[0]
    for other in tops[1:]:
        top = jnp.maximum(top, other)
    out.ref[...] = jnp.full(out.ref.shape, top, F32)
    out.flush()


def attend_body(layer, count, scal, ins, outs, bias_ref):
    x_in, top_in, vecs_in, own_in, near_in, far_in, small_in = ins
    low_out, fac_out, qkv_out, ctx_out, e_out, rinv_out, top_out = outs
    low_ref, qkv_ref, ctx_ref, e_ref, rinv_ref = (o.ref for o in (low_out, qkv_out, ctx_out, e_out, rinv_out))
    rows, width = low_ref.shape
    heads_width = qkv_ref.shape[3]
    first, second = halves(scal, width)
    q_row, _ = row_ids(scal, lax.broadcasted_iota(jnp.int32, (rows, 1), 0), rows // 2)
    k_row, k_live = row_ids(scal, lax.broadcasted_iota(jnp.int32, (1, rows), 1), rows // 2)
    k_row = jnp.where(k_live, k_row, -1)
    bias_ref[...] = jnp.where(q_row == k_row, 0.0, MASKED)
    bound = bound_of(top_in.all())
    size = rows // count
    vecs_ref = vecs_in.all()
    for i in range(count):
        place = slice(i * size, (i + 1) * size)
        tangent = jnp.tanh(x_in.wait(i)[place, :].astype(F32) * (1.0 / bound))
        low = (bound * tangent).astype(BF16)
        low_ref[place, :] = low
        low_out.flush(i)
        fac_out.ref[place, :] = (1.0 - tangent * tangent).astype(BF16)
        fac_out.flush(i)
        own_ref = own_in.all()
        for j in range(3):
            values = nt(low, own_ref[j])
            if j != 1:
                values = values + vec(vecs_ref, layer, B_Q + j // 2, heads_width)
            qkv_ref[0, j, place, :] = values.astype(BF16)
    qkv_out.flush(0)
    scale = HEAD_DIM ** (-0.5)
    chunk = 128
    chunks = rows // chunk
    tops = []
    for side in range(2):
        if side == 1:
            near_ref, far_ref, small_ref = near_in.all(), far_in.all(), small_in.all()
            for j in range(3):
                values = nt(low_ref[:, first], near_ref[j]) + nt(low_ref[:, second], far_ref[j])
                if j != 1:
                    at = 3 * layer + j // 2
                    values = values + small_ref[at : at + 1, 0:heads_width]
                qkv_ref[1, j] = values.astype(BF16)
            qkv_out.flush(1)
        heads = []
        for h, (lo, hi, which) in enumerate(HEADS):
            keys = only_head(qkv_ref[side, 1, :, lo:hi], which)
            heads.append((h, lo, hi, which, keys, qkv_ref[side, 2, :, lo:hi]))
        left = lane_mask(chunk, 0)
        for i in range(chunks):
            place = slice(i * chunk, (i + 1) * chunk)
            done = []
            for h, lo, hi, which, keys, vals in heads:
                scores = nt(qkv_ref[side, 0, place, lo:hi], keys) * scale + bias_ref[place, :]
                weights = jnp.exp(scores - jnp.max(scores, axis=1, keepdims=True))
                inverse = 1.0 / jnp.sum(weights, axis=1, keepdims=True)
                low = weights.astype(BF16)
                e_ref[side, h, place, :] = low
                done.append((nn(low, vals) * inverse, inverse))
            pair = jnp.where(left, done[0][0], done[1][0])
            ctx_ref[side, place, 0:128] = pair
            ctx_ref[side, place, 128:192] = done[2][0]
            tops += [largest(pair), largest(done[2][0])]
            rinv_ref[side, place, 0:128] = jnp.where(left, done[0][1], done[1][1])
            rinv_ref[side, place, 128:192] = jnp.broadcast_to(done[2][1], (chunk, HEAD_DIM))
            for out in (e_out, ctx_out, rinv_out):
                out.flush(side * chunks + i)
    put_top(top_out, tops)


def out_body(count, scal, ins, outs):
    top_in, ctx_in, own_in, near_in, far_in = ins
    c_out, fac_out, o_out = outs
    bound = bound_of(top_in.all())
    rows, width = o_out.ref.shape
    size = rows // count
    for i in range(count):
        place = slice(i * size, (i + 1) * size)
        tangent = jnp.tanh(ctx_in.wait(i)[:, place, :] * (1.0 / bound))
        low = (bound * tangent).astype(BF16)
        c_out.ref[:, place, :] = low
        c_out.flush(i)
        fac_out.ref[:, place, :] = (1.0 - tangent * tangent).astype(BF16)
        fac_out.flush(i)
        own_ref = own_in.all()
        for part, load in zip(halves(scal, width), (near_in, far_in)):
            o_out.ref[place, part] = (nn(low[0], own_ref[:, part]) + nn(low[1], load.all()[3])).astype(BF16)
        o_out.flush(i)


def norm_forward(mixed, gain, shift):
    centred = mixed - jnp.mean(mixed, axis=1, keepdims=True)
    inverse = lax.rsqrt(jnp.mean(centred * centred, axis=1, keepdims=True) + EPS)
    unit = centred * inverse
    return unit * gain + shift, unit, inverse


def lane_fill(value):
    return jnp.full((1, 128), value, F32)


def norm_body(layer, second, count, scal, ins, outs):
    vecs_in, x_in, self_in, recv_in = ins
    h_out, unit_out, inv_out, sums_out, top_out = outs
    rows, width = h_out.ref.shape
    size = rows // count
    vecs_ref = vecs_in.all()
    bias = vec(vecs_ref, layer, B_DOWN if second else B_OUT)
    gain = vec(vecs_ref, layer, GAIN_TWO if second else GAIN_ONE)
    shift = vec(vecs_ref, layer, SHIFT_TWO if second else SHIFT_ONE)
    tops, branch_sum, result_sum = [], 0.0, 0.0
    for i in range(count):
        place = slice(i * size, (i + 1) * size)
        branch = self_in.wait(i)[place, :].astype(F32) + recv_in.wait(i)[place, :].astype(F32) + bias
        result, unit, inverse = norm_forward(x_in.wait(i)[place, :].astype(F32) + branch, gain, shift)
        h_out.ref[place, :] = result
        h_out.flush(i)
        unit_out.ref[place, :] = unit.astype(unit_out.ref.dtype)
        unit_out.flush(i)
        inv_out.ref[place, :] = jnp.broadcast_to(inverse, (size, 128))
        inv_out.flush(i)
        tops.append(largest(result))
        if i < count // 2:
            branch_sum = branch_sum + jnp.sum(branch * branch)
            result_sum = result_sum + jnp.sum(result * result)
    sums_out.ref[0:1, :] = lane_fill(branch_sum)
    sums_out.ref[1:2, :] = lane_fill(result_sum)
    sums_out.flush()
    put_top(top_out, tops)


def up_body(layer, count, scal, ins, outs):
    top_in, h_in, vecs_in, own_in, near_in, far_in, small_in = ins
    low_out, fac_out, g_out, slope_out, top_out = outs
    low_ref = low_out.ref
    rows, width = low_ref.shape
    size = rows // count
    bound = bound_of(top_in.all())
    first, second = halves(scal, width)
    tops = []
    for i in range(count):
        place = slice(i * size, (i + 1) * size)
        tangent = jnp.tanh(h_in.wait(i)[place, :] * (1.0 / bound))
        low = (bound * tangent).astype(BF16)
        low_ref[place, :] = low
        low_out.flush(i)
        fac_out.ref[place, :] = (1.0 - tangent * tangent).astype(BF16)
        fac_out.flush(i)
        for side in range(2):
            if side == 0:
                units = nn(low, own_in.all()[...]) + vec(vecs_in.all(), layer, B_UP)
            else:
                units = nn(low_ref[place, first], near_in.all()[...]) + nn(low_ref[place, second], far_in.all()[...])
                units = units + small_in.all()[3 * layer + 2 : 3 * layer + 3, :]
            area = 0.5 + 0.5 * lax.erf(units * (0.5**0.5))
            density = jnp.exp(-0.5 * units * units) * 0.3989422804014327
            active = units * area
            g_out.ref[side, place, :] = active
            slope_out.ref[side, place, :] = (area + units * density).astype(BF16)
            tops.append(largest(active))
        g_out.flush(i)
        slope_out.flush(i)
    put_top(top_out, tops)


def down_body(count, scal, ins, outs):
    top_in, g_in, slope_in, own_in, near_in, far_in = ins
    low_out, fac_out, f_out = outs
    low_ref = low_out.ref
    rows, width = f_out.ref.shape
    size = rows // count
    bound = bound_of(top_in.all())
    first, second = halves(scal, low_ref.shape[2])
    for i in range(count):
        place = slice(i * size, (i + 1) * size)
        tangent = jnp.tanh(g_in.wait(i)[:, place, :] * (1.0 / bound))
        low_ref[:, place, :] = (bound * tangent).astype(BF16)
        low_out.flush(i)
        slope = slope_in.wait(i)[:, place, :].astype(F32)
        fac_out.ref[:, place, :] = ((1.0 - tangent * tangent) * slope).astype(BF16)
        fac_out.flush(i)
        f_out.ref[place, :] = (
            nn(low_ref[0, place, :], own_in.all()[...])
            + nn(low_ref[1, place, first], near_in.all()[...])
            + nn(low_ref[1, place, second], far_in.all()[...])
        ).astype(BF16)
        f_out.flush(i)


def norm_back(grad, unit, inverse, gain):
    scaled = grad * gain
    return (
        scaled
        - jnp.mean(scaled, axis=1, keepdims=True)
        - unit * jnp.mean(scaled * unit, axis=1, keepdims=True)
    ) * inverse


def column_sums(values):
    return jnp.sum(values, axis=0, keepdims=True)


def ffn_back_body(layer, last_layer, count, scal, ins, outs):
    vecs_in, ins = ins[0], ins[1:]
    if last_layer:
        (h_in, self_in, recv_in, cot_in), ins = ins[:4], ins[4:]
        result_out, fsum_out = outs[-2:]
    else:
        (self_in, recv_in, infac_in, skip_in, unit_in, inv_in), ins = ins[:6], ins[6:]
    fac_in, down_in, dnear_in, dfar_in, up_in, unear_in, ufar_in = ins
    dz_out, df_out, du_out, dh_out, sums_out, usum_out = outs[:6]
    rows, width = dz_out.ref.shape
    size = rows // count
    vecs_ref = vecs_in.all()
    gain = vec(vecs_ref, layer, GAIN_TWO)
    first, second = halves(scal, width)
    du_ref = du_out.ref
    totals = None
    unit_totals = None
    branch_sum = 0.0
    for i in range(count):
        place = slice(i * size, (i + 1) * size)
        mine = i < count // 2
        both = self_in.wait(i)[place, :].astype(F32) + recv_in.wait(i)[place, :].astype(F32)
        if last_layer:
            branch = both + vec(vecs_ref, layer, B_DOWN)
            result, unit, inverse = norm_forward(h_in.wait(i)[place, :] + branch, gain, vec(vecs_ref, layer, SHIFT_TWO))
            grad = cot_in.wait(i)[place, :].astype(F32)
            if mine:
                result_out.ref[place, :] = result.astype(BF16)
                result_out.flush(i)
                branch_sum = branch_sum + jnp.sum(branch * branch)
        else:
            grad = both * infac_in.wait(i)[place, :].astype(F32) + skip_in.wait(i)[place, :]
            unit = unit_in.wait(i)[place, :].astype(F32)
            inverse = inv_in.wait(i)[place, 0:1]
        mixed = norm_back(grad, unit, inverse, gain)
        low = mixed.astype(BF16)
        dz_out.ref[place, :] = mixed
        dz_out.flush(i)
        df_out.ref[place, :] = low
        df_out.flush(i)
        if mine:
            new = [column_sums(v) for v in (grad * unit, grad, low.astype(F32))]
            totals = new if totals is None else [a + b for a, b in zip(totals, new)]
        fac_ref = fac_in.wait(i)
        du_ref[0, place, :] = (nt(low, down_in.all()[...]) * fac_ref[0, place, :].astype(F32)).astype(BF16)
        for part, load in ((first, dnear_in), (second, dfar_in)):
            du_ref[1, place, part] = (nt(low, load.all()[...]) * fac_ref[1, place, part].astype(F32)).astype(BF16)
        du_out.flush(i)
        for part, load in ((first, unear_in), (second, ufar_in)):
            dh_out.ref[place, part] = (
                nt(du_ref[0, place, :], up_in.all()[part, :]) + nt(du_ref[1, place, :], load.all()[...])
            ).astype(BF16)
        dh_out.flush(i)
        new = [column_sums(du_ref[side, place, :].astype(F32)) for side in range(2)]
        unit_totals = new if unit_totals is None else [a + b for a, b in zip(unit_totals, new)]
    for row, values in enumerate(totals):
        sums_out.ref[row : row + 1, :] = values
    for row, values in enumerate(unit_totals):
        usum_out.ref[row : row + 1, :] = values
    if last_layer:
        fsum_out.ref[...] = lane_fill(branch_sum)


def attn_back_body(layer, split, count, scal, ins, outs, da_scratch):
    (vecs_in, self_in, recv_in, hfac_in, skip_in, unit_in, inv_in, wout_in, cfac_in, rinv_in, ctx_in, qkv_in, e_in, wqkv_in,
     near_in, far_in) = ins
    dz_out, do_out, d_out, sums_out, hsum_out, da_out = outs[:6]
    rows, width = dz_out.ref.shape
    heads_width = qkv_in.ref.shape[3]
    size = rows // count
    first, second = halves(scal, width)
    gain = vec(vecs_in.all(), layer, GAIN_ONE)
    totals = None
    for i in range(count):
        place = slice(i * size, (i + 1) * size)
        grad = self_in.wait(i)[place, :].astype(F32) + recv_in.wait(i)[place, :].astype(F32)
        grad = grad * hfac_in.wait(i)[place, :].astype(F32) + skip_in.wait(i)[place, :]
        unit = unit_in.wait(i)[place, :].astype(F32)
        mixed = norm_back(grad, unit, inv_in.wait(i)[place, 0:1], gain)
        low = mixed.astype(BF16)
        dz_out.ref[place, :] = mixed
        dz_out.flush(i)
        do_out.ref[place, :] = low
        do_out.flush(i)
        if i < count // 2:
            new = [column_sums(v) for v in (grad * unit, grad, low.astype(F32))]
            totals = new if totals is None else [a + b for a, b in zip(totals, new)]
    for row, values in enumerate(totals):
        sums_out.ref[row : row + 1, :] = values
    do_ref, d_ref = do_out.ref, d_out.ref
    scale = HEAD_DIM ** (-0.5)
    left = lane_mask(rows, 0)
    for side in range(2):
        if side == 0:
            grad_ctx = nt(do_ref[...], wout_in.all()[...])
        else:
            grad_ctx = nt(do_ref[:, first], near_in.all()[3]) + nt(do_ref[:, second], far_in.all()[3])
        grad_ctx = grad_ctx * cfac_in.wait(side)[side].astype(F32)
        low = (grad_ctx * rinv_in.wait(side)[side]).astype(BF16)
        product = low.astype(F32) * ctx_in.wait(side)[side]
        qkv_ref, e_ref = qkv_in.wait(side), e_in.wait(side)
        results = []
        for h, (lo, hi, which) in enumerate(HEADS):
            inner = jnp.sum(only_head(product[:, lo:hi], which), axis=1, keepdims=True)
            values = only_head(qkv_ref[side, 2, :, lo:hi], which)
            weights = e_ref[side, h]
            grad_weights = nt(low[:, lo:hi], values)
            grad_scores = (weights.astype(F32) * (grad_weights - inner)).astype(BF16)
            dq = nn(grad_scores, qkv_ref[side, 1, :, lo:hi]) * scale
            dk = tn(grad_scores, qkv_ref[side, 0, :, lo:hi]) * scale
            dv = tn(weights, low[:, lo:hi])
            results.append((dq, dk, dv))
        for j in range(3):
            pair = jnp.where(left, results[0][j], results[1][j]).astype(BF16)
            last = results[2][j].astype(BF16)
            d_ref[side, :, j * heads_width : j * heads_width + 128] = pair
            d_ref[side, :, j * heads_width + 128 : (j + 1) * heads_width] = last
            if j != 1:
                at = slice(j // 2, j // 2 + 1)
                hsum_out.ref[side, at, 0:128] = column_sums(pair.astype(F32))
                hsum_out.ref[side, at, 128:192] = column_sums(last.astype(F32))
        d_out.flush(side)
        if side == 0:
            da_scratch[...] = nn(d_ref[0], merge(wqkv_in.all()[...]))
    for i in range(2):
        place = slice(i * rows // 2, (i + 1) * rows // 2)
        for part, load in ((first, near_in), (second, far_in)):
            total = (da_scratch[place, part] + nn(d_ref[1, place, :], merge(load.ref[0:3]))).astype(BF16)
            if split:
                outs[5 + i].ref[:, part] = total
            else:
                da_out.ref[place, part] = total
        if split:
            outs[5 + i].flush()
        else:
            da_out.flush(i)


def bands(bit_value, count, band):
    return [pl.ds(pl.multiple_of((2 * k + bit_value) * band, band), band) for k in range(count)]


def grad_body(with_ffn, with_attn, band, scal, ins, outs, scratch):
    if with_ffn:
        (df_in, gq_in, hq_in, du_in), ins = ins[:4], ins[4:]
    if with_attn:
        a_in, d_in, do_in, c_in = ins

    def y_first(side):
        at = 0
        if with_ffn:
            at = gq_in.ref.shape[2]
            scratch[:, 0:at] = tn(df_in.all()[...], gq_in.all()[side])
        if with_attn:
            width = c_in.ref.shape[2]
            scratch[:, at : at + width] = tn(a_in.all()[...], d_in.all()[side, :, 2 * width : 3 * width])
            scratch[:, at + width : at + 2 * width] = tn(do_in.all()[...], c_in.all()[side])

    def x_first(side, put):
        at = 0
        if with_ffn:
            at = hq_in.ref.shape[1]
            put(slice(0, at), tn(hq_in.all()[...], du_in.all()[side]).astype(BF16))
        if with_attn:
            width = c_in.ref.shape[2]
            put(slice(at, at + 2 * width), tn(a_in.all()[...], d_in.all()[side, :, 0 : 2 * width]).astype(BF16))

    if len(outs) == 2:
        for side, out in ((0, outs[0]), (1, outs[1])):

            def put(columns, values, out=out):
                out.ref[0, :, columns] = values

            x_first(side, put)
            y_first(side)
            out.ref[1] = scratch[...].astype(BF16)
        return
    own_out, oth_out, keep_out, send_out = outs
    count = keep_out.ref.shape[1] // band
    mine, away = bands(scal[Y], count, band), bands(1 - scal[Y], count, band)
    for side, out in ((1, oth_out), (0, own_out)):

        def put(columns, values, out=out):
            out.ref[:, columns] = values

        x_first(side, put)
        out.flush()
        y_first(side)
        for k in range(count):
            place = slice(k * band, (k + 1) * band)
            send_out.ref[side, place, :] = scratch[away[k], :].astype(BF16)
            keep_out.ref[side, place, :] = scratch[mine[k], :].astype(BF16)
        send_out.flush(side)
        keep_out.flush(side)


def second_kernel(band, scal, own_ref, recv_ref, keep_ref, got_ref, xkeep_ref, xsend_ref, yown_ref, yoth_ref, scratch):
    count = xkeep_ref.shape[0] // band
    scratch[...] = own_ref[...].astype(F32) + recv_ref[...].astype(F32)
    mine, away = bands(scal[Y], count, band), bands(1 - scal[Y], count, band)
    yoth_ref[...] = (keep_ref[1].astype(F32) + got_ref[1].astype(F32)).astype(BF16)
    yown_ref[...] = (keep_ref[0].astype(F32) + got_ref[0].astype(F32)).astype(BF16)
    for k in range(count):
        place = slice(k * band, (k + 1) * band)
        xsend_ref[place, :] = scratch[away[k], :].astype(BF16)
        xkeep_ref[place, :] = scratch[mine[k], :].astype(BF16)


def fold_kernel(band, bit, scal, *refs):
    keep_out, send_out, scratch = refs[-3:]
    count = keep_out.shape[1] // band
    if len(refs) == 7:
        scratch[0] = refs[0][...].astype(F32) + refs[1][...].astype(F32)
        scratch[1] = refs[2][...].astype(F32) + refs[3][...].astype(F32)
    else:
        scratch[...] = refs[0][...].astype(F32) + refs[1][...].astype(F32)
    mine = (scal[DP] // bit) % 2
    for k, (take, give) in enumerate(zip(bands(mine, count, band), bands(1 - mine, count, band))):
        place = slice(k * band, (k + 1) * band)
        keep_out[:, place, :] = scratch[:, take, :].astype(BF16)
        send_out[:, place, :] = scratch[:, give, :].astype(BF16)


def final_kernel(heads_width, scal, a_keep, a_recv, b_keep, b_recv, c_keep, c_recv, qkv_ref, out_ref, up_ref, down_ref):
    width = up_ref.shape[2]
    first = a_keep[...].astype(F32) + a_recv[...].astype(F32)
    up_ref[1] = first[0]
    down_ref[1] = first[1]
    second = b_keep[...].astype(F32) + b_recv[...].astype(F32)
    up_ref[0] = second[0, :, 0:width]
    down_ref[0] = second[1, :, 0:width]
    third = c_keep[...].astype(F32) + c_recv[...].astype(F32)
    for layer, part in ((1, second[:, :, width:]), (0, third)):
        qkv_ref[layer, 0] = part[0, :, 0:heads_width]
        qkv_ref[layer, 1] = part[0, :, heads_width : 2 * heads_width]
        qkv_ref[layer, 2] = part[1, :, 0:heads_width]
        out_ref[layer] = part[1, :, heads_width : 2 * heads_width]


def pack_kernel(tensor_size, heads_width, scal, *refs):
    refs, out_ref = refs[:-1], refs[-1]
    out_ref[...] = jnp.zeros(out_ref.shape, F32)
    shard = scal[SHARD]
    for layer in range(LAYERS):
        one_ref, two_ref, heads_ref, units_ref = refs[4 * layer : 4 * layer + 4]
        base = layer * (6 + 2 * tensor_size)
        for row in range(3):
            out_ref[base + row] = one_ref[row : row + 1, :]
            out_ref[base + 3 + row] = two_ref[row : row + 1, :]
        for side in range(2):
            place = shard if side == 0 else shard + 2 - 4 * ((shard // 2) % 2)
            out_ref[base + 6 + place, :, 0:heads_width] = heads_ref[side, 0:1, :]
            out_ref[base + 6 + place, :, 256 : 256 + heads_width] = heads_ref[side, 1:2, :]
            out_ref[base + 6 + tensor_size + place] = units_ref[side : side + 1, :]
    base = LAYERS * (6 + 2 * tensor_size)
    for i, ref in enumerate(refs[4 * LAYERS :]):
        out_ref[base, :, 128 * i : 128 * (i + 1)] = ref[0:1, :]


def total_kernel(scal, in_ref, out_ref):
    devices = out_ref.shape[0]
    total = jnp.sum(in_ref[...].reshape(devices, -1, in_ref.shape[2]), axis=0, keepdims=True)
    out_ref[...] = jnp.broadcast_to(total, out_ref.shape)


def unpack_kernel(tensor_size, heads_width, count, scal, in_ref, hb_ref, ob_ref, gain_ref, shift_ref, ub_ref, db_ref, rms_ref):
    shard = scal[SHARD]
    for layer in range(LAYERS):
        base = layer * (6 + 2 * tensor_size)
        for k in range(2):
            gain_ref[layer, k : k + 1, :] = in_ref[base + 3 * k]
            shift_ref[layer, k : k + 1, :] = in_ref[base + 3 * k + 1]
        ob_ref[layer : layer + 1, :] = in_ref[base + 2]
        db_ref[layer : layer + 1, :] = in_ref[base + 5]
        heads = in_ref[base + 6 + shard]
        hb_ref[layer, 0:1, :] = heads[:, 0:heads_width]
        hb_ref[layer, 1:2, :] = heads[:, 256 : 256 + heads_width]
        ub_ref[layer : layer + 1, :] = in_ref[base + 6 + tensor_size + shard]
    base = LAYERS * (6 + 2 * tensor_size)
    row = jnp.sqrt(in_ref[base] * (1.0 / count))
    for layer in range(LAYERS):
        for k in range(3):
            i = 3 * layer + k
            rms_ref[layer : layer + 1, k : k + 1] = row[:, 128 * i : 128 * i + 1]


def dx_kernel(scal, self_ref, recv_ref, fac_ref, skip_ref, out_ref):
    grad = self_ref[...].astype(F32) + recv_ref[...].astype(F32)
    out_ref[...] = grad * fac_ref[...].astype(F32) + skip_ref[...]


def body(
    hidden,
    long_lengths,
    short_lengths,
    w_qkv,
    bias_qv,
    w_out,
    bias_out,
    ln_gain,
    ln_bias,
    w_up,
    bias_up,
    w_down,
    bias_down,
    cotangent,
):
    own_rows, width = hidden.shape
    rows = 2 * own_rows
    heads_width = w_qkv.shape[-1]
    units = w_up.shape[-1]
    dp_size, tensor_size = lax.axis_size("dp"), lax.axis_size("tensor")
    devices = dp_size * tensor_size
    count_model = float(own_rows * devices * width)
    dp_index, tensor_index = lax.axis_index("dp"), lax.axis_index("tensor")
    core_pairs = [(i, i ^ 1) for i in range(tensor_size)]
    x_pairs = [(i, i ^ 2) for i in range(tensor_size)]
    core_swap = lambda v: lax.ppermute(v, "tensor", core_pairs)
    x_swap = lambda v: lax.ppermute(v, "tensor", x_pairs)
    dp_swap = lambda v, bit: lax.ppermute(v, "dp", [(i, i ^ bit) for i in range(dp_size)])
    over_ranks = lambda top: lax.all_to_all(top, BOTH, 0, 0)

    scal = jnp.concatenate(
        [
            jnp.stack([tensor_index // 2, dp_index % 2, tensor_index % 2, dp_index, tensor_index]).astype(jnp.int32),
            long_lengths,
            short_lengths,
        ]
    )
    w_qkv = jnp.swapaxes(w_qkv, 2, 3)

    def run(kernel, ins, outs, name, flops=0, scratch=(), after=()):
        arrays = [array for array, _ in ins] + list(after)
        moved = sum(a.size * a.dtype.itemsize for a, _ in ins) + sum(
            jax.ShapeDtypeStruct(s, d).size * jnp.dtype(d).itemsize for s, d in outs
        )

        def trimmed(scal_ref, *refs):
            kernel(scal_ref, *refs[: len(ins)], *refs[len(arrays) :])

        return pl.pallas_call(
            trimmed,
            grid_spec=pltpu.PrefetchScalarGridSpec(
                num_scalar_prefetch=1,
                grid=(1,),
                in_specs=[s for _, s in ins] + [pl.BlockSpec(memory_space=pl.ANY)] * len(after),
                out_specs=[pl.BlockSpec(s, lambda i, t, n=len(s): (0,) * n) for s, _ in outs],
                scratch_shapes=list(scratch),
            ),
            out_shape=[jax.ShapeDtypeStruct(s, d) for s, d in outs],
            name=name,
            cost_estimate=pl.CostEstimate(flops=int(flops), bytes_accessed=int(moved), transcendentals=0),
            compiler_params=pltpu.CompilerParams(vmem_limit_bytes=VMEM_LIMIT),
        )(scal, *arrays)

    flow = partial(stream, scal)
    spec = pl.BlockSpec
    full = lambda a: (a, spec(a.shape, lambda i, s: (0,) * len(a.shape)))
    top_rows = lambda a, n: (a, spec((n,) + a.shape[1:], lambda i, s: (0,) * len(a.shape)))
    top_shape = (devices, 1, 128)
    top_store = Store(top_shape, F32)

    vecs, small, top, input_sum = run(
        start_kernel,
        [full(a) for a in (hidden, bias_out, ln_gain, ln_bias, bias_down, bias_qv, bias_up)],
        [((LAYERS * VECS, width), F32), ((LAYERS * 3, units), F32), (top_shape, F32), ((1, 128), F32)],
        "start",
    )
    top = over_ranks(top)
    other_hidden = core_swap(hidden)

    def weight_halves(l, after):
        sends = run(
            halves_kernel,
            [
                (w_qkv, spec((None, 3, heads_width, width // 2), lambda i, s: (l, 0, 0, s[Y]))),
                (w_out, spec((None, heads_width, width // 2), lambda i, s: (l, 0, s[Y]))),
                (w_up, spec((None, width // 2, units), lambda i, s: (l, s[Y], 0))),
                (w_down, spec((None, units // 2, width), lambda i, s: (l, s[Y], 0))),
            ],
            [((4, heads_width, width // 2), BF16), ((width // 2, units), BF16), ((units // 2, width), BF16)],
            "halves",
            after=after,
        )
        near = [x_swap(v) for v in sends]
        return list(zip(near, [dp_swap(v, 1) for v in near]))

    weights = [weight_halves(0, (input_sum,))]
    small = x_swap(small)

    saved = []
    square_terms = []
    states = None
    for l in range(LAYERS):
        last = l == LAYERS - 1
        first = l == 0
        (att_near, att_far), (up_near, up_far), (down_near, down_far) = weights[l]
        low_in, fac_in, qkv, ctx, soft, rinv, top = flow(
            partial(attend_body, l, 2),
            [pair_in(hidden, other_hidden, 2) if first else rows_in(states, 2), whole_in(top), whole_in(vecs), layer_in(w_qkv, l),
             whole_in(att_near), whole_in(att_far), whole_in(small)],
            [rows_out((rows, width), BF16, 2), rows_out((rows, width), BF16, 2), per_side_out((2, 3, rows, heads_width), BF16),
             side_rows_out((2, rows, heads_width), F32, 0, 4), side_rows_out((2, 3, rows, rows), BF16, 1, 4),
             side_rows_out((2, rows, heads_width), F32, 0, 4), top_store],
            "attend",
            flops=12 * rows * rows * 128 * 8,
            scratch=[pltpu.VMEM((rows, rows), F32)],
        )
        if first:
            weights.append(weight_halves(1, (top,)))
        top = over_ranks(top)
        low_ctx, fac_ctx, part = flow(
            partial(out_body, 2),
            [whole_in(top), sides_in(ctx, 2), layer_in(w_out, l), whole_in(att_near), whole_in(att_far)],
            [sides_out((2, rows, heads_width), BF16, 2), sides_out((2, rows, heads_width), BF16, 2), rows_out((rows, width), BF16, 2)],
            "out_proj",
            flops=4 * rows * width * heads_width,
        )
        norm_stores = [rows_out((rows, width), F32, 4), rows_out((rows, width), BF16, 4), rows_out((rows, 128), F32, 4),
                       Store((2, 128), F32), top_store]
        middle, unit_one, inv_one, sums_one, top = flow(
            partial(norm_body, l, False, 4),
            [whole_in(vecs), pair_in(hidden, other_hidden, 4) if first else rows_in(states, 4), rows_in(part, 4),
             rows_in(core_swap(part), 4, True)],
            norm_stores,
            "norm_one",
        )
        top = over_ranks(top)
        low_mid, fac_mid, active, slope, top = flow(
            partial(up_body, l, 2),
            [whole_in(top), rows_in(middle, 2), whole_in(vecs), layer_in(w_up, l), whole_in(up_near), whole_in(up_far), whole_in(small)],
            [rows_out((rows, width), BF16, 2), rows_out((rows, width), BF16, 2), sides_out((2, rows, units), F32, 2),
             sides_out((2, rows, units), BF16, 2), top_store],
            "up_proj",
            flops=4 * rows * width * units,
        )
        top = over_ranks(top)
        low_act, fac_act, part = flow(
            partial(down_body, 2),
            [whole_in(top), sides_in(active, 2), sides_in(slope, 2), layer_in(w_down, l), whole_in(down_near), whole_in(down_far)],
            [sides_out((2, rows, units), BF16, 2), sides_out((2, rows, units), BF16, 2), rows_out((rows, width), BF16, 2)],
            "down_proj",
            flops=4 * rows * width * units,
        )
        square_terms += [input_sum, sums_one]
        keep = (low_in, fac_in, qkv, ctx, soft, rinv, low_ctx, fac_ctx, unit_one, inv_one, low_mid, fac_mid, low_act, fac_act)
        recv = core_swap(part)
        if not last:
            states, unit_two, inv_two, sums_two, top = flow(
                partial(norm_body, l, True, 4),
                [whole_in(vecs), rows_in(middle, 4), rows_in(part, 4), rows_in(recv, 4, True)],
                norm_stores,
                "norm_two",
            )
            square_terms.append(sums_two)
            input_sum = sums_two[1:2]
            top = over_ranks(top)
            keep += (unit_two, inv_two)
        saved.append(keep)

    other_cotangent = core_swap(cotangent)
    sums = [None] * LAYERS
    band = width // dp_size
    banded = band % 16 == 0

    def add_group(with_ffn, with_attn, ins, name, columns):
        half_width = width // 2
        if banded:
            stores = [Store((width, columns), BF16)] * 2 + [per_side_out((2, half_width, columns), BF16)] * 2
        else:
            stores = [per_side_out((2, width, columns), BF16)] * 2
        return flow(
            partial(grad_body, with_ffn, with_attn, band),
            [whole_in(a) for a in ins],
            stores,
            name,
            flops=4 * rows * width * columns * 2,
            scratch=[pltpu.VMEM((width, columns), F32)],
        )

    def fold_start(group):
        own, oth, keep, send = group
        return own, x_swap(oth), keep, dp_swap(send, 1)

    def fold_second(pending, after=()):
        columns = pending[0].shape[1]
        xkeep, xsend, yown, yoth = run(
            partial(second_kernel, band),
            [full(a) for a in pending],
            [((width // 2, columns), BF16)] * 4,
            "second",
            scratch=[pltpu.VMEM((width, columns), F32)],
            after=after,
        )
        return [xkeep, dp_swap(xsend, 1), yown, x_swap(yoth)]

    def fold_rest(ins):
        remaining = width // 2
        columns = ins[0].shape[-1]
        bit = 2
        while bit < dp_size:
            outs = run(
                partial(fold_kernel, band, bit),
                [full(a) for a in ins],
                [((2, remaining // 2, columns), BF16)] * 2,
                "fold",
                scratch=[pltpu.VMEM((2, remaining, columns), F32)],
            )
            ins = [outs[0], dp_swap(outs[1], bit)]
            remaining //= 2
            bit *= 2
        return ins

    grad_ins = []
    groups = []
    seconds = []
    for l in reversed(range(LAYERS)):
        (low_in, fac_in, qkv, ctx, soft, rinv, low_ctx, fac_ctx, unit_one, inv_one, low_mid, fac_mid, low_act, fac_act) = saved[l][:14]
        (att_near, att_far), (up_near, up_far), (down_near, down_far) = weights[l]
        last = l == LAYERS - 1
        if last:
            ins = [whole_in(vecs), rows_in(middle, 2), rows_in(part, 2), rows_in(recv, 2, True), pair_in(cotangent, other_cotangent, 2)]
            extra = [Store((own_rows, width), BF16), Store((1, 128), F32)]
        else:
            unit_two, inv_two = saved[l][14:]
            ins = [whole_in(vecs), rows_in(part, 2), rows_in(recv, 2, True), rows_in(fac, 2), rows_in(skip, 2), rows_in(unit_two, 2),
                   rows_in(inv_two, 2)]
            extra = []
        dz_two, df, du, part, sums_two, unit_sums, *more = flow(
            partial(ffn_back_body, l, last, 2),
            ins + [sides_in(fac_act, 2), layer_in(w_down, l), whole_in(down_near), whole_in(down_far), layer_in(w_up, l),
                   whole_in(up_near), whole_in(up_far)],
            [rows_out((rows, width), F32, 2), rows_out((rows, width), BF16, 2), sides_out((2, rows, units), BF16, 2),
             rows_out((rows, width), BF16, 2), Store((3, width), F32), Store((2, units), F32)] + extra,
            "ffn_back",
            flops=8 * rows * width * units,
        )
        if last:
            output = more[0]
            square_terms.append(more[1])
        recv = core_swap(part)
        hold = ()
        if banded and groups:
            seconds.append(fold_second(groups.pop(), (du,)))
            hold = (seconds[-1][0],)
        grad_ins = [df, low_act, low_mid, du] + grad_ins
        with_attn = len(grad_ins) > 4
        grads = add_group(True, with_attn, grad_ins, "grads", units + (2 * heads_width if with_attn else 0))
        if banded:
            groups.append(fold_start(grads))
        else:
            groups.append(grads)
        split = l == 0
        dz_one, do, dqkv, sums_one, head_sums, *parts = flow(
            partial(attn_back_body, l, split, 2),
            [whole_in(vecs), rows_in(part, 2), rows_in(recv, 2, True), rows_in(fac_mid, 2), rows_in(dz_two, 2), rows_in(unit_one, 2),
             rows_in(inv_one, 2), layer_in(w_out, l), per_side_in(fac_ctx), per_side_in(rinv), per_side_in(ctx), per_side_in(qkv),
             per_side_in(soft), layer_in(w_qkv, l), whole_in(att_near), whole_in(att_far)],
            [rows_out((rows, width), F32, 2), rows_out((rows, width), BF16, 2), per_side_out((2, rows, 3 * heads_width), BF16),
             Store((3, width), F32), Store((2, 2, heads_width), F32)]
            + ([Store((own_rows, width), BF16)] * 2 if split else [rows_out((rows, width), BF16, 2)]),
            "attn_back",
            flops=6 * rows * rows * 128 * 10,
            scratch=[pltpu.VMEM((rows, width), F32)],
            after=(grads[0],) + hold,
        )
        part = parts[0]
        recv = core_swap(parts[-1])
        fac, skip = fac_in, dz_one
        grad_ins = [low_in, dqkv, do, low_ctx]
        sums[l] = (sums_one, sums_two, head_sums, unit_sums)
    grads = add_group(False, True, grad_ins, "grads", 2 * heads_width)
    groups.append(fold_start(grads) if banded else grads)

    (grad_hidden,) = run(
        dx_kernel,
        [full(part), full(recv), top_rows(fac, own_rows), top_rows(skip, own_rows)],
        [((own_rows, width), F32)],
        "dx",
    )

    if banded:
        folded = []
        for ins in seconds + [fold_second(g) for g in groups]:
            folded += fold_rest(ins)
        grad_qkv, grad_out, grad_up, grad_down = run(
            partial(final_kernel, heads_width),
            [full(a) for a in folded],
            [((LAYERS, 3, band, heads_width), F32), ((LAYERS, band, heads_width), F32), ((LAYERS, band, units), F32),
             ((LAYERS, band, width), F32)],
            "final",
        )
    else:
        totals = []
        for own, oth in groups:
            both = own.astype(F32) + x_swap(oth).astype(F32)
            totals.append(lax.psum_scatter(both, "dp", scatter_dimension=1, tiled=True))
        one, two, three = totals
        grad_up = jnp.stack([two[0, :, :units], one[0]])
        grad_down = jnp.stack([two[1, :, :units], one[1]])
        attn = jnp.stack([three, two[:, :, units:]])
        cut = lambda side, at: attn[:, side, :, at * heads_width : (at + 1) * heads_width]
        grad_qkv = jnp.stack([cut(0, 0), cut(0, 1), cut(1, 0)], 1)
        grad_out = cut(1, 1)

    count_rows = LAYERS * (6 + 2 * tensor_size) + 1
    packed_rows = -(-count_rows // devices) * devices
    (packed,) = run(
        partial(pack_kernel, tensor_size, heads_width),
        [full(a) for l in range(LAYERS) for a in sums[l]] + [full(a) for a in square_terms],
        [((packed_rows, 1, width), F32)],
        "pack",
    )
    chunk = packed_rows // devices
    packed = over_ranks(packed.reshape(devices, chunk, width)).reshape(devices, chunk, width)
    (totals,) = run(total_kernel, [full(packed)], [((devices, chunk, width), F32)], "total")
    totals = over_ranks(totals).reshape(packed_rows, 1, width)
    head_bias, out_bias, gains, shifts, unit_bias, down_bias, rms = run(
        partial(unpack_kernel, tensor_size, heads_width, count_model),
        [full(totals)],
        [(s, F32) for s in ((LAYERS, 2, heads_width), (LAYERS, width), (LAYERS, 2, width), (LAYERS, 2, width), (LAYERS, units),
                            (LAYERS, width), (LAYERS, 3))],
        "unpack",
    )
    return (
        output,
        grad_hidden,
        grad_qkv,
        head_bias,
        jnp.swapaxes(grad_out, 1, 2),
        out_bias,
        gains,
        shifts,
        grad_up,
        unit_bias,
        jnp.swapaxes(grad_down, 1, 2),
        down_bias,
        rms,
    )


def solution(mesh):
    in_specs = (
        P(("dp", "tensor"), None),
        P("dp"),
        P("dp"),
        P(None, None, None, "tensor"),
        P(None, None, "tensor"),
        P(None, "tensor", None),
        P(),
        P(),
        P(),
        P(None, None, "tensor"),
        P(None, "tensor"),
        P(None, "tensor", None),
        P(),
        P(("dp", "tensor"), None),
    )
    out_specs = (
        P(("dp", "tensor"), None),
        P(("dp", "tensor"), None),
        P(None, None, "dp", "tensor"),
        P(None, None, "tensor"),
        P(None, "tensor", "dp"),
        P(),
        P(),
        P(),
        P(None, "dp", "tensor"),
        P(None, "tensor"),
        P(None, "tensor", "dp"),
        P(),
        P(),
    )
    return jax.shard_map(body, mesh=mesh, in_specs=in_specs, out_specs=out_specs, check_vma=False)
```

```python
from functools import partial

import jax
import jax.numpy as jnp
from jax import lax
from jax.experimental import pallas as pl
from jax.experimental.pallas import tpu as pltpu
from jax.sharding import PartitionSpec as P

HEAD_DIM = 64
LAYERS = 2
LONG_LEN = 512
SHORT_LEN = 128
LONG_DEV = 1
SHORT_DEV = 4

EPS = 1e-06
MASKED = -1e30
BOTH = ("dp", "tensor")
F32 = jnp.float32
BF16 = jnp.bfloat16
VMEM_LIMIT = 60 * 1024 * 1024
HEAVY = 10**15
LIGHT = {"halves", "norm_one", "norm_two", "up_proj"}

X, Y, CORE, DP, SHARD, LENGTHS = range(6)


def nt(left, right):
    return lax.dot_general(left, right, (((1,), (1,)), ((), ())), preferred_element_type=F32)


def nn(left, right):
    return jnp.dot(left, right, preferred_element_type=F32)


def tn(left, right):
    return lax.dot_general(left, right, (((0,), (0,)), ((), ())), preferred_element_type=F32)


def merge(values):
    return values.reshape(values.shape[0] * values.shape[1], values.shape[2])


def bound_of(top_ref):
    return jnp.max(top_ref[...]) * 0.25 + EPS


def halves(scal, width):
    part = width // 2
    near = scal[Y]
    first = pl.ds(pl.multiple_of(near * part, part), part)
    second = pl.ds(pl.multiple_of((1 - near) * part, part), part)
    return first, second


class Load:
    def __init__(self, shape, dtype, pieces):
        self.shape, self.dtype, self.pieces = tuple(shape), dtype, pieces


class Store:
    def __init__(self, shape, dtype, pieces=((),)):
        self.shape, self.dtype, self.pieces = tuple(shape), dtype, pieces


def view(ref, index):
    return ref.at[index] if index else ref


class Arriving:
    def __init__(self, ref, copies):
        self.ref, self.copies, self.waited = ref, copies, set()

    def wait(self, piece):
        if piece not in self.waited:
            self.copies[piece].wait()
            self.waited.add(piece)
        return self.ref

    def all(self):
        for piece in range(len(self.copies)):
            self.wait(piece)
        return self.ref


class Leaving:
    def __init__(self, ref, copies):
        self.ref, self.copies, self.started = ref, copies, set()

    def flush(self, piece=0):
        self.copies[piece].start()
        self.started.add(piece)


def stream(scal, body, loads, stores, name, scratch=()):
    arrays = []

    def slot(array):
        for i, known in enumerate(arrays):
            if known is array:
                return i
        arrays.append(array)
        return len(arrays) - 1

    plan = [[(slot(a), src, dst) for a, src, dst in load.pieces] for load in loads]
    first_out = len(arrays)
    n_in = sum(len(p) for p in plan)
    n_out = sum(len(st.pieces) for st in stores)

    def kernel(scal_ref, *refs):
        sources = refs[: len(arrays)]
        targets = refs[first_out : first_out + len(stores)]
        at = first_out + len(stores)
        vin, at = refs[at : at + len(loads)], at + len(loads)
        vout, at = refs[at : at + len(stores)], at + len(stores)
        extra, (sem_in, sem_out) = refs[at:-2], refs[-2:]
        count = 0
        arriving = []
        for pieces, ref in zip(plan, vin):
            copies = []
            for i, src, dst in pieces:
                copies.append(pltpu.make_async_copy(view(sources[i], src), view(ref, dst), sem_in.at[count]))
                count += 1
            arriving.append(Arriving(ref, copies))
        for piece in range(max(len(p) for p in plan)):
            for a in arriving:
                if piece < len(a.copies):
                    a.copies[piece].start()
        count = 0
        leaving = []
        for st, ref, target in zip(stores, vout, targets):
            copies = []
            for index in st.pieces:
                copies.append(pltpu.make_async_copy(view(ref, index), view(target, index), sem_out.at[count]))
                count += 1
            leaving.append(Leaving(ref, copies))
        body(scal_ref, arriving, leaving, *extra)
        for a in arriving:
            a.all()
        for out in leaving:
            for piece, copy in enumerate(out.copies):
                if piece not in out.started:
                    copy.start()
        for out in leaving:
            for copy in out.copies:
                copy.wait()

    anywhere = pl.BlockSpec(memory_space=pl.ANY)
    return pl.pallas_call(
        kernel,
        in_specs=[pl.BlockSpec(memory_space=pltpu.SMEM)] + [anywhere] * first_out,
        out_specs=[anywhere] * len(stores),
        out_shape=[jax.ShapeDtypeStruct(st.shape, st.dtype) for st in stores],
        scratch_shapes=[pltpu.VMEM(x.shape, x.dtype) for x in list(loads) + list(stores)]
        + list(scratch)
        + [pltpu.SemaphoreType.DMA((n_in,)), pltpu.SemaphoreType.DMA((n_out,))],
        name=name,
        cost_estimate=pl.CostEstimate(flops=0 if name in LIGHT else HEAVY, bytes_accessed=1, transcendentals=0),
        compiler_params=pltpu.CompilerParams(vmem_limit_bytes=VMEM_LIMIT),
    )(scal, *arrays)


ALL = slice(None)


def span(i, size):
    return pl.ds(i * size, size)


def whole_in(a):
    return Load(a.shape, a.dtype, [(a, (), ())])


def layer_in(a, layer):
    return Load(a.shape[1:], a.dtype, [(a, (layer,), ())])


def rows_in(a, count, swap=False):
    size = a.shape[0] // count
    turn = count // 2 if swap else 0
    return Load(a.shape, a.dtype, [(a, (span((i + turn) % count, size),), (span(i, size),)) for i in range(count)])


def pair_in(mine, other, count):
    rows, width = mine.shape
    size = 2 * rows // count
    half = count // 2
    return Load(
        (2 * rows, width),
        mine.dtype,
        [((mine if i < half else other), (span(i % half, size),), (span(i, size),)) for i in range(count)],
    )


def sides_in(a, count):
    size = a.shape[1] // count
    return Load(a.shape, a.dtype, [(a, (ALL, span(i, size)), (ALL, span(i, size))) for i in range(count)])


def side_rows_in(parts, count):
    size = parts[0].shape[1] // count
    sources = [(a, i) for a in parts for i in range(a.shape[0])]
    return Load(
        (2,) + parts[0].shape[1:],
        parts[0].dtype,
        [(a, (s, span(i, size)), (side, span(i, size))) for i in range(count) for side, (a, s) in enumerate(sources)],
    )


def per_side_in(parts):
    pieces = [(a, (i,)) for a in parts for i in range(a.shape[0])]
    return Load((2,) + parts[0].shape[1:], parts[0].dtype, [(a, src, (i,)) for i, (a, src) in enumerate(pieces)])


def rows_out(shape, dtype, count):
    size = shape[0] // count
    return Store(shape, dtype, [(span(i, size),) for i in range(count)])


def sides_out(shape, dtype, count):
    size = shape[1] // count
    return Store(shape, dtype, [(ALL, span(i, size)) for i in range(count)])


def side_rows_out(shape, dtype, lead, count):
    size = shape[1 + lead] // count
    return Store(shape, dtype, [(s,) + (ALL,) * lead + (span(i, size),) for s in range(shape[0]) for i in range(count)])


def per_side_out(shape, dtype):
    return Store(shape, dtype, [(i,) for i in range(shape[0])])


B_OUT, GAIN_ONE, SHIFT_ONE, B_DOWN, GAIN_TWO, SHIFT_TWO, B_Q, B_V, B_UP, VECS = range(10)


def vec(ref, layer, row, width=None):
    at = layer * VECS + row
    return ref[at : at + 1, :] if width is None else ref[at : at + 1, 0:width]


def start_kernel(scal, hidden_ref, bout_ref, gain_ref, shift_ref, bdown_ref, bqv_ref, bup_ref, vecs_ref, small_ref, top_ref, sums_ref):
    heads_width = bqv_ref.shape[2]
    vecs_ref[...] = jnp.zeros(vecs_ref.shape, F32)
    small_ref[...] = jnp.zeros(small_ref.shape, F32)
    for layer in range(LAYERS):
        base = layer * VECS
        one = slice(layer, layer + 1)
        vecs_ref[base + B_OUT : base + B_OUT + 1, :] = bout_ref[one, :]
        vecs_ref[base + B_DOWN : base + B_DOWN + 1, :] = bdown_ref[one, :]
        vecs_ref[base + GAIN_ONE : base + GAIN_ONE + 1, :] = gain_ref[layer, 0:1, :]
        vecs_ref[base + GAIN_TWO : base + GAIN_TWO + 1, :] = gain_ref[layer, 1:2, :]
        vecs_ref[base + SHIFT_ONE : base + SHIFT_ONE + 1, :] = shift_ref[layer, 0:1, :]
        vecs_ref[base + SHIFT_TWO : base + SHIFT_TWO + 1, :] = shift_ref[layer, 1:2, :]
        for ref, at in ((vecs_ref, base + B_Q), (small_ref, 3 * layer)):
            ref[at : at + 1, 0:heads_width] = bqv_ref[layer, 0:1, :]
            ref[at + 1 : at + 2, 0:heads_width] = bqv_ref[layer, 1:2, :]
            ref[at + 2 : at + 3, :] = bup_ref[one, :]
    values = hidden_ref[...].astype(F32)
    top_ref[...] = jnp.full(top_ref.shape, jnp.max(jnp.abs(values)), F32)
    sums_ref[...] = jnp.full((1, 128), jnp.sum(values * values), F32)


def halves_kernel(scal, wqkv_ref, wout_ref, wup_ref, wdown_ref, att_ref, up_ref, down_ref):
    att_ref[0:3] = wqkv_ref[...]
    att_ref[3] = wout_ref[...]
    up_ref[...] = wup_ref[...]
    down_ref[...] = wdown_ref[...]


def row_ids(scal, slots, half_rows):
    rows = 2 * half_rows
    slot = slots + half_rows * scal[CORE]
    slot = jnp.where(slot >= rows, slot - rows, slot) + scal[X] * rows
    short = slot - LONG_DEV * LONG_LEN
    is_long = short < 0
    row = jnp.where(is_long, slot // LONG_LEN, LONG_DEV + short // SHORT_LEN)
    place = jnp.where(is_long, slot % LONG_LEN, short % SHORT_LEN)
    length = jnp.zeros_like(row)
    for i in range(LONG_DEV + SHORT_DEV):
        length = jnp.where(row == i, scal[LENGTHS + i], length)
    return row, place < length


HEADS = ((0, 128, 0), (0, 128, 1), (128, 192, None))


def lane_mask(rows, which):
    lane = lax.broadcasted_iota(jnp.int32, (rows, 128), 1)
    return (lane < HEAD_DIM) if which == 0 else (lane >= HEAD_DIM)


def only_head(values, which):
    if which is None:
        return values
    return jnp.where(lane_mask(values.shape[0], which), values, jnp.zeros_like(values))


def largest(values):
    return jnp.max(jnp.abs(values))


def put_top(out, tops):
    top = tops[0]
    for other in tops[1:]:
        top = jnp.maximum(top, other)
    out.ref[...] = jnp.full(out.ref.shape, top, F32)
    out.flush()


def attend_body(layer, count, sides, scal, ins, outs, bias_ref):
    if 0 in sides:
        x_in, top_in, vecs_in, own_in, ins = *ins[:4], ins[4:]
        low_out, fac_out, outs = *outs[:2], outs[2:]
        low_ref = low_out.ref
    else:
        low_in, ins = ins[0], ins[1:]
        low_ref = low_in.all()
    if 1 in sides:
        near_in, far_in, small_in, ins = *ins[:3], ins[3:]
    qkv_out, ctx_out, e_out, rinv_out, top_out = outs
    qkv_ref, ctx_ref, e_ref, rinv_ref = (o.ref for o in (qkv_out, ctx_out, e_out, rinv_out))
    rows, width = low_ref.shape
    heads_width = qkv_ref.shape[3]
    first, second = halves(scal, width)
    q_row, _ = row_ids(scal, lax.broadcasted_iota(jnp.int32, (rows, 1), 0), rows // 2)
    k_row, k_live = row_ids(scal, lax.broadcasted_iota(jnp.int32, (1, rows), 1), rows // 2)
    k_row = jnp.where(k_live, k_row, -1)
    bias_ref[...] = jnp.where(q_row == k_row, 0.0, MASKED)
    if 0 in sides:
        bound = bound_of(top_in.all())
        size = rows // count
        vecs_ref = vecs_in.all()
        for i in range(count):
            place = slice(i * size, (i + 1) * size)
            tangent = jnp.tanh(x_in.wait(i)[place, :].astype(F32) * (1.0 / bound))
            low = (bound * tangent).astype(BF16)
            low_ref[place, :] = low
            low_out.flush(i)
            fac_out.ref[place, :] = (1.0 - tangent * tangent).astype(BF16)
            fac_out.flush(i)
            own_ref = own_in.all()
            for j in range(3):
                values = nt(low, own_ref[j])
                if j != 1:
                    values = values + vec(vecs_ref, layer, B_Q + j // 2, heads_width)
                qkv_ref[0, j, place, :] = values.astype(BF16)
        qkv_out.flush(0)
    scale = HEAD_DIM ** (-0.5)
    chunk = 128
    chunks = rows // chunk
    tops = []
    for at, side in enumerate(sides):
        if side == 1:
            near_ref, far_ref, small_ref = near_in.all(), far_in.all(), small_in.all()
            for j in range(3):
                values = nt(low_ref[:, first], near_ref[j]) + nt(low_ref[:, second], far_ref[j])
                if j != 1:
                    row = 3 * layer + j // 2
                    values = values + small_ref[row : row + 1, 0:heads_width]
                qkv_ref[at, j] = values.astype(BF16)
            qkv_out.flush(at)
        heads = []
        for h, (lo, hi, which) in enumerate(HEADS):
            keys = only_head(qkv_ref[at, 1, :, lo:hi], which)
            heads.append((h, lo, hi, which, keys, qkv_ref[at, 2, :, lo:hi]))
        left = lane_mask(chunk, 0)
        for i in range(chunks):
            place = slice(i * chunk, (i + 1) * chunk)
            done = []
            for h, lo, hi, which, keys, vals in heads:
                scores = nt(qkv_ref[at, 0, place, lo:hi], keys) * scale + bias_ref[place, :]
                weights = jnp.exp(scores - jnp.max(scores, axis=1, keepdims=True))
                inverse = 1.0 / jnp.sum(weights, axis=1, keepdims=True)
                low = weights.astype(BF16)
                e_ref[at, h, place, :] = low
                done.append((nn(low, vals) * inverse, inverse))
            pair = jnp.where(left, done[0][0], done[1][0])
            ctx_ref[at, place, 0:128] = pair
            ctx_ref[at, place, 128:192] = done[2][0]
            tops += [largest(pair), largest(done[2][0])]
            rinv_ref[at, place, 0:128] = jnp.where(left, done[0][1], done[1][1])
            rinv_ref[at, place, 128:192] = jnp.broadcast_to(done[2][1], (chunk, HEAD_DIM))
            for out in (e_out, ctx_out, rinv_out):
                out.flush(at * chunks + i)
    tops += [jnp.max(load.all()[...]) for load in ins]
    put_top(top_out, tops)


def out_body(scal, ins, outs):
    top_in, ctx_in, own_in, near_in, far_in = ins
    c_out, fac_out, *o_outs = outs
    bound = bound_of(top_in.all())
    size, width = o_outs[0].ref.shape
    for i, o_out in enumerate(o_outs):
        place = slice(i * size, (i + 1) * size)
        ctx_in.wait(2 * i)
        tangent = jnp.tanh(ctx_in.wait(2 * i + 1)[:, place, :] * (1.0 / bound))
        low = (bound * tangent).astype(BF16)
        c_out.ref[:, place, :] = low
        c_out.flush(i)
        fac_out.ref[:, place, :] = (1.0 - tangent * tangent).astype(BF16)
        fac_out.flush(i)
        own_ref = own_in.all()
        for part, load in zip(halves(scal, width), (near_in, far_in)):
            o_out.ref[:, part] = (nn(low[0], own_ref[:, part]) + nn(low[1], load.all()[3])).astype(BF16)
        o_out.flush()


def norm_forward(mixed, gain, shift):
    centred = mixed - jnp.mean(mixed, axis=1, keepdims=True)
    inverse = lax.rsqrt(jnp.mean(centred * centred, axis=1, keepdims=True) + EPS)
    unit = centred * inverse
    return unit * gain + shift, unit, inverse


def lane_fill(value):
    return jnp.full((1, 128), value, F32)


def norm_body(layer, second, count, scal, ins, outs):
    vecs_in, x_in, self_in, recv_in = ins
    h_out, unit_out, inv_out, sums_out, top_out = outs
    rows, width = h_out.ref.shape
    size = rows // count
    vecs_ref = vecs_in.all()
    bias = vec(vecs_ref, layer, B_DOWN if second else B_OUT)
    gain = vec(vecs_ref, layer, GAIN_TWO if second else GAIN_ONE)
    shift = vec(vecs_ref, layer, SHIFT_TWO if second else SHIFT_ONE)
    tops, branch_sum, result_sum = [], 0.0, 0.0
    for i in range(count):
        place = slice(i * size, (i + 1) * size)
        branch = self_in.wait(i)[place, :].astype(F32) + recv_in.wait(i)[place, :].astype(F32) + bias
        result, unit, inverse = norm_forward(x_in.wait(i)[place, :].astype(F32) + branch, gain, shift)
        h_out.ref[place, :] = result
        h_out.flush(i)
        unit_out.ref[place, :] = unit.astype(unit_out.ref.dtype)
        unit_out.flush(i)
        inv_out.ref[place, :] = jnp.broadcast_to(inverse, (size, 128))
        inv_out.flush(i)
        tops.append(largest(result))
        if i < count // 2:
            branch_sum = branch_sum + jnp.sum(branch * branch)
            result_sum = result_sum + jnp.sum(result * result)
    sums_out.ref[0:1, :] = lane_fill(branch_sum)
    sums_out.ref[1:2, :] = lane_fill(result_sum)
    sums_out.flush()
    put_top(top_out, tops)


def up_body(layer, count, scal, ins, outs):
    top_in, h_in, vecs_in, own_in, near_in, far_in, small_in = ins
    low_out, fac_out, g_out, slope_out, top_out = outs
    low_ref = low_out.ref
    rows, width = low_ref.shape
    size = rows // count
    bound = bound_of(top_in.all())
    first, second = halves(scal, width)
    tops = []
    for i in range(count):
        place = slice(i * size, (i + 1) * size)
        tangent = jnp.tanh(h_in.wait(i)[place, :] * (1.0 / bound))
        low = (bound * tangent).astype(BF16)
        low_ref[place, :] = low
        low_out.flush(i)
        fac_out.ref[place, :] = (1.0 - tangent * tangent).astype(BF16)
        fac_out.flush(i)
        for side in range(2):
            if side == 0:
                units = nn(low, own_in.all()[...]) + vec(vecs_in.all(), layer, B_UP)
            else:
                units = nn(low_ref[place, first], near_in.all()[...]) + nn(low_ref[place, second], far_in.all()[...])
                units = units + small_in.all()[3 * layer + 2 : 3 * layer + 3, :]
            area = 0.5 + 0.5 * lax.erf(units * (0.5**0.5))
            density = jnp.exp(-0.5 * units * units) * 0.3989422804014327
            active = units * area
            g_out.ref[side, place, :] = active
            slope_out.ref[side, place, :] = (area + units * density).astype(BF16)
            tops.append(largest(active))
        g_out.flush(i)
        slope_out.flush(i)
    put_top(top_out, tops)


def down_body(scal, ins, outs):
    top_in, g_in, slope_in, own_in, near_in, far_in = ins
    low_out, fac_out, *f_outs = outs
    low_ref = low_out.ref
    size = f_outs[0].ref.shape[0]
    bound = bound_of(top_in.all())
    first, second = halves(scal, low_ref.shape[2])
    for i, f_out in enumerate(f_outs):
        place = slice(i * size, (i + 1) * size)
        tangent = jnp.tanh(g_in.wait(i)[:, place, :] * (1.0 / bound))
        low_ref[:, place, :] = (bound * tangent).astype(BF16)
        low_out.flush(i)
        slope = slope_in.wait(i)[:, place, :].astype(F32)
        fac_out.ref[:, place, :] = ((1.0 - tangent * tangent) * slope).astype(BF16)
        fac_out.flush(i)
        f_out.ref[...] = (
            nn(low_ref[0, place, :], own_in.all()[...])
            + nn(low_ref[1, place, first], near_in.all()[...])
            + nn(low_ref[1, place, second], far_in.all()[...])
        ).astype(BF16)
        f_out.flush()


def norm_back(grad, unit, inverse, gain):
    scaled = grad * gain
    return (
        scaled
        - jnp.mean(scaled, axis=1, keepdims=True)
        - unit * jnp.mean(scaled * unit, axis=1, keepdims=True)
    ) * inverse


def column_sums(values):
    return jnp.sum(values, axis=0, keepdims=True)


def ffn_back_body(layer, last_layer, count, scal, ins, outs):
    vecs_in, ins = ins[0], ins[1:]
    if last_layer:
        (h_in, self_in, recv_in, cot_in), ins = ins[:4], ins[4:]
        result_out, fsum_out = outs[-2:]
    else:
        (self_in, recv_in, infac_in, skip_in, unit_in, inv_in), ins = ins[:6], ins[6:]
    fac_in, down_in, dnear_in, dfar_in, up_in, unear_in, ufar_in = ins
    dz_out, df_out, du_out, dh_out, sums_out, usum_out = outs[:6]
    rows, width = dz_out.ref.shape
    size = rows // count
    vecs_ref = vecs_in.all()
    gain = vec(vecs_ref, layer, GAIN_TWO)
    first, second = halves(scal, width)
    du_ref = du_out.ref
    totals = None
    unit_totals = None
    branch_sum = 0.0
    for i in range(count):
        place = slice(i * size, (i + 1) * size)
        mine = i < count // 2
        both = self_in.wait(i)[place, :].astype(F32) + recv_in.wait(i)[place, :].astype(F32)
        if last_layer:
            branch = both + vec(vecs_ref, layer, B_DOWN)
            result, unit, inverse = norm_forward(h_in.wait(i)[place, :] + branch, gain, vec(vecs_ref, layer, SHIFT_TWO))
            grad = cot_in.wait(i)[place, :].astype(F32)
            if mine:
                result_out.ref[place, :] = result.astype(BF16)
                result_out.flush(i)
                branch_sum = branch_sum + jnp.sum(branch * branch)
        else:
            grad = both * infac_in.wait(i)[place, :].astype(F32) + skip_in.wait(i)[place, :]
            unit = unit_in.wait(i)[place, :].astype(F32)
            inverse = inv_in.wait(i)[place, 0:1]
        mixed = norm_back(grad, unit, inverse, gain)
        low = mixed.astype(BF16)
        dz_out.ref[place, :] = mixed
        dz_out.flush(i)
        df_out.ref[place, :] = low
        df_out.flush(i)
        if mine:
            new = [column_sums(v) for v in (grad * unit, grad, low.astype(F32))]
            totals = new if totals is None else [a + b for a, b in zip(totals, new)]
        fac_ref = fac_in.wait(i)
        du_ref[0, place, :] = (nt(low, down_in.all()[...]) * fac_ref[0, place, :].astype(F32)).astype(BF16)
        for part, load in ((first, dnear_in), (second, dfar_in)):
            du_ref[1, place, part] = (nt(low, load.all()[...]) * fac_ref[1, place, part].astype(F32)).astype(BF16)
        du_out.flush(i)
        for part, load in ((first, unear_in), (second, ufar_in)):
            dh_out.ref[place, part] = (
                nt(du_ref[0, place, :], up_in.all()[part, :]) + nt(du_ref[1, place, :], load.all()[...])
            ).astype(BF16)
        dh_out.flush(i)
        new = [column_sums(du_ref[side, place, :].astype(F32)) for side in range(2)]
        unit_totals = new if unit_totals is None else [a + b for a, b in zip(unit_totals, new)]
    for row, values in enumerate(totals):
        sums_out.ref[row : row + 1, :] = values
    for row, values in enumerate(unit_totals):
        usum_out.ref[row : row + 1, :] = values
    if last_layer:
        fsum_out.ref[...] = lane_fill(branch_sum)


def attn_back_body(layer, split, count, scal, ins, outs, da_scratch):
    (vecs_in, self_in, recv_in, hfac_in, skip_in, unit_in, inv_in, wout_in, cfac_in, rinv_in, ctx_in, qkv_in, e_in, wqkv_in,
     near_in, far_in) = ins
    dz_out, do_out, d_out, sums_out, hsum_out, da_out = outs[:6]
    rows, width = dz_out.ref.shape
    heads_width = qkv_in.ref.shape[3]
    size = rows // count
    first, second = halves(scal, width)
    gain = vec(vecs_in.all(), layer, GAIN_ONE)
    totals = None
    for i in range(count):
        place = slice(i * size, (i + 1) * size)
        grad = self_in.wait(i)[place, :].astype(F32) + recv_in.wait(i)[place, :].astype(F32)
        grad = grad * hfac_in.wait(i)[place, :].astype(F32) + skip_in.wait(i)[place, :]
        unit = unit_in.wait(i)[place, :].astype(F32)
        mixed = norm_back(grad, unit, inv_in.wait(i)[place, 0:1], gain)
        low = mixed.astype(BF16)
        dz_out.ref[place, :] = mixed
        dz_out.flush(i)
        do_out.ref[place, :] = low
        do_out.flush(i)
        if i < count // 2:
            new = [column_sums(v) for v in (grad * unit, grad, low.astype(F32))]
            totals = new if totals is None else [a + b for a, b in zip(totals, new)]
    for row, values in enumerate(totals):
        sums_out.ref[row : row + 1, :] = values
    do_ref, d_ref = do_out.ref, d_out.ref
    scale = HEAD_DIM ** (-0.5)
    left = lane_mask(rows, 0)
    for side in range(2):
        if side == 0:
            grad_ctx = nt(do_ref[...], wout_in.all()[...])
        else:
            grad_ctx = nt(do_ref[:, first], near_in.all()[3]) + nt(do_ref[:, second], far_in.all()[3])
        grad_ctx = grad_ctx * cfac_in.wait(side)[side].astype(F32)
        low = (grad_ctx * rinv_in.wait(side)[side]).astype(BF16)
        product = low.astype(F32) * ctx_in.wait(side)[side]
        qkv_ref, e_ref = qkv_in.wait(side), e_in.wait(side)
        results = []
        for h, (lo, hi, which) in enumerate(HEADS):
            inner = jnp.sum(only_head(product[:, lo:hi], which), axis=1, keepdims=True)
            values = only_head(qkv_ref[side, 2, :, lo:hi], which)
            weights = e_ref[side, h]
            grad_weights = nt(low[:, lo:hi], values)
            grad_scores = (weights.astype(F32) * (grad_weights - inner)).astype(BF16)
            dq = nn(grad_scores, qkv_ref[side, 1, :, lo:hi]) * scale
            dk = tn(grad_scores, qkv_ref[side, 0, :, lo:hi]) * scale
            dv = tn(weights, low[:, lo:hi])
            results.append((dq, dk, dv))
        for j in range(3):
            pair = jnp.where(left, results[0][j], results[1][j]).astype(BF16)
            last = results[2][j].astype(BF16)
            d_ref[side, :, j * heads_width : j * heads_width + 128] = pair
            d_ref[side, :, j * heads_width + 128 : (j + 1) * heads_width] = last
            if j != 1:
                at = slice(j // 2, j // 2 + 1)
                hsum_out.ref[side, at, 0:128] = column_sums(pair.astype(F32))
                hsum_out.ref[side, at, 128:192] = column_sums(last.astype(F32))
        d_out.flush(side)
        if side == 0:
            da_scratch[...] = nn(d_ref[0], merge(wqkv_in.all()[...]))
    for i in range(2):
        place = slice(i * rows // 2, (i + 1) * rows // 2)
        for part, load in ((first, near_in), (second, far_in)):
            total = (da_scratch[place, part] + nn(d_ref[1, place, :], merge(load.ref[0:3]))).astype(BF16)
            if split:
                outs[5 + i].ref[:, part] = total
            else:
                da_out.ref[place, part] = total
        if split:
            outs[5 + i].flush()
        else:
            da_out.flush(i)


def bands(bit_value, count, band):
    return [pl.ds(pl.multiple_of((2 * k + bit_value) * band, band), band) for k in range(count)]


def cut_bands(scratch, mine, away, keep_ref, send_ref, band):
    for k, (take, give) in enumerate(zip(mine, away)):
        place = slice(k * band, (k + 1) * band)
        send_ref[place, :] = scratch[give, :].astype(BF16)
        keep_ref[place, :] = scratch[take, :].astype(BF16)


def grad_body(kind, bit, band, scal, ins, outs, scratch):
    if kind == "ffn":
        df_in, gq_in, hq_in, du_in = ins
        columns = hq_in.ref.shape[1]
        x_first = lambda side: tn(hq_in.all()[...], du_in.all()[side])

        def y_first(side, put):
            put(slice(None), tn(df_in.all()[...], gq_in.all()[side]))

    else:
        a_in, d_in, do_in, c_in = ins
        width = c_in.ref.shape[2]
        columns = 2 * width
        x_first = lambda side: tn(a_in.all()[...], d_in.all()[side, :, 0:columns])

        def y_first(side, put):
            put(slice(0, width), tn(a_in.all()[...], d_in.all()[side, :, columns : 3 * width]))
            put(slice(width, columns), tn(do_in.all()[...], c_in.all()[side]))

    if bit is None:
        for side, out in ((0, outs[0]), (1, outs[1])):

            def put(at, values):
                out.ref[1, :, at] = values.astype(BF16)

            out.ref[0] = x_first(side).astype(BF16)
            y_first(side, put)
        return

    def put(at, values):
        scratch[:, at] = values

    keep_out, send_out = outs[-2:]
    value = (scal[DP] // bit) % 2
    count = keep_out.ref.shape[-2] // band
    mine, away = bands(value, count, band), bands(1 - value, count, band)
    if len(outs) == 4:
        own_out, oth_out = outs[:2]
        for side, out in ((1, oth_out), (0, own_out)):
            out.ref[...] = x_first(side).astype(BF16)
            out.flush()
            y_first(side, put)
            cut_bands(scratch, mine, away, keep_out.ref.at[side], send_out.ref.at[side], band)
            send_out.flush(side)
            keep_out.flush(side)
        return
    for side in range(2):
        scratch[...] = x_first(side)
        cut_bands(scratch, mine, away, keep_out.ref.at[side, 0], send_out.ref.at[side, 0], band)
        y_first(side, put)
        cut_bands(scratch, mine, away, keep_out.ref.at[side, 1], send_out.ref.at[side, 1], band)
        send_out.flush(side)
        keep_out.flush(side)


def second_kernel(band, scal, own_ref, recv_ref, keep_ref, got_ref, xkeep_ref, xsend_ref, yown_ref, yoth_ref, scratch):
    count = xkeep_ref.shape[0] // band
    scratch[...] = own_ref[...].astype(F32) + recv_ref[...].astype(F32)
    mine, away = bands(scal[Y], count, band), bands(1 - scal[Y], count, band)
    yoth_ref[...] = (keep_ref[1].astype(F32) + got_ref[1].astype(F32)).astype(BF16)
    yown_ref[...] = (keep_ref[0].astype(F32) + got_ref[0].astype(F32)).astype(BF16)
    cut_bands(scratch, mine, away, xkeep_ref, xsend_ref, band)


def fold_kernel(band, bit, scal, *refs):
    refs, (keep_out, send_out, scratch) = refs[:-3], refs[-3:]
    lead = scratch.shape[0]
    if len(refs) == 4:
        scratch[0] = refs[0][...].astype(F32) + refs[1][...].astype(F32)
        scratch[1] = refs[2][...].astype(F32) + refs[3][...].astype(F32)
    else:
        scratch[...] = refs[0][...].astype(F32) + refs[1][...].astype(F32)
    count = keep_out.shape[1] // band
    value = (scal[DP] // bit) % 2
    mine, away = bands(value, count, band), bands(1 - value, count, band)
    for part in range(lead):
        cut_bands(scratch.at[part], mine, away, keep_out.at[part], send_out.at[part], band)


def final_kernel(heads_width, scal, *refs):
    (ffn_one, attn_one, ffn_zero, attn_zero), outs = [refs[2 * i : 2 * i + 2] for i in range(4)], refs[8:]
    qkv_ref, out_ref, up_ref, down_ref = outs
    for layer, (keep_ref, recv_ref) in ((1, ffn_one), (0, ffn_zero)):
        up_ref[layer] = keep_ref[0].astype(F32) + recv_ref[0].astype(F32)
        down_ref[layer] = keep_ref[1].astype(F32) + recv_ref[1].astype(F32)
    for layer, (keep_ref, recv_ref) in ((1, attn_one), (0, attn_zero)):
        for part in range(2):
            total = keep_ref[part].astype(F32) + recv_ref[part].astype(F32)
            qkv_ref[layer, 2 * part] = total[:, 0:heads_width]
            if part == 0:
                qkv_ref[layer, 1] = total[:, heads_width : 2 * heads_width]
            else:
                out_ref[layer] = total[:, heads_width : 2 * heads_width]


def pack_kernel(tensor_size, heads_width, scal, *refs):
    refs, out_ref = refs[:-1], refs[-1]
    out_ref[...] = jnp.zeros(out_ref.shape, F32)
    shard = scal[SHARD]
    for layer in range(LAYERS):
        one_ref, two_ref, heads_ref, units_ref = refs[4 * layer : 4 * layer + 4]
        base = layer * (6 + 2 * tensor_size)
        for row in range(3):
            out_ref[base + row] = one_ref[row : row + 1, :]
            out_ref[base + 3 + row] = two_ref[row : row + 1, :]
        for side in range(2):
            place = shard if side == 0 else shard + 2 - 4 * ((shard // 2) % 2)
            out_ref[base + 6 + place, :, 0:heads_width] = heads_ref[side, 0:1, :]
            out_ref[base + 6 + place, :, 256 : 256 + heads_width] = heads_ref[side, 1:2, :]
            out_ref[base + 6 + tensor_size + place] = units_ref[side : side + 1, :]
    base = LAYERS * (6 + 2 * tensor_size)
    for i, ref in enumerate(refs[4 * LAYERS :]):
        out_ref[base, :, 128 * i : 128 * (i + 1)] = ref[0:1, :]


def total_kernel(scal, in_ref, out_ref):
    devices = out_ref.shape[0]
    total = jnp.sum(in_ref[...].reshape(devices, -1, in_ref.shape[2]), axis=0, keepdims=True)
    out_ref[...] = jnp.broadcast_to(total, out_ref.shape)


def unpack_kernel(tensor_size, heads_width, count, scal, in_ref, hb_ref, ob_ref, gain_ref, shift_ref, ub_ref, db_ref, rms_ref):
    shard = scal[SHARD]
    for layer in range(LAYERS):
        base = layer * (6 + 2 * tensor_size)
        for k in range(2):
            gain_ref[layer, k : k + 1, :] = in_ref[base + 3 * k]
            shift_ref[layer, k : k + 1, :] = in_ref[base + 3 * k + 1]
        ob_ref[layer : layer + 1, :] = in_ref[base + 2]
        db_ref[layer : layer + 1, :] = in_ref[base + 5]
        heads = in_ref[base + 6 + shard]
        hb_ref[layer, 0:1, :] = heads[:, 0:heads_width]
        hb_ref[layer, 1:2, :] = heads[:, 256 : 256 + heads_width]
        ub_ref[layer : layer + 1, :] = in_ref[base + 6 + tensor_size + shard]
    base = LAYERS * (6 + 2 * tensor_size)
    row = jnp.sqrt(in_ref[base] * (1.0 / count))
    for layer in range(LAYERS):
        for k in range(3):
            i = 3 * layer + k
            rms_ref[layer : layer + 1, k : k + 1] = row[:, 128 * i : 128 * i + 1]


def dx_kernel(scal, self_ref, recv_ref, fac_ref, skip_ref, out_ref):
    grad = self_ref[...].astype(F32) + recv_ref[...].astype(F32)
    out_ref[...] = grad * fac_ref[...].astype(F32) + skip_ref[...]


def body(
    hidden,
    long_lengths,
    short_lengths,
    w_qkv,
    bias_qv,
    w_out,
    bias_out,
    ln_gain,
    ln_bias,
    w_up,
    bias_up,
    w_down,
    bias_down,
    cotangent,
):
    own_rows, width = hidden.shape
    rows = 2 * own_rows
    heads_width = w_qkv.shape[-1]
    units = w_up.shape[-1]
    dp_size, tensor_size = lax.axis_size("dp"), lax.axis_size("tensor")
    devices = dp_size * tensor_size
    count_model = float(own_rows * devices * width)
    dp_index, tensor_index = lax.axis_index("dp"), lax.axis_index("tensor")
    core_pairs = [(i, i ^ 1) for i in range(tensor_size)]
    x_pairs = [(i, i ^ 2) for i in range(tensor_size)]
    core_swap = lambda v: lax.ppermute(v, "tensor", core_pairs)
    x_swap = lambda v: lax.ppermute(v, "tensor", x_pairs)
    dp_swap = lambda v, bit: lax.ppermute(v, "dp", [(i, i ^ bit) for i in range(dp_size)])
    over_ranks = lambda top: lax.all_to_all(top, BOTH, 0, 0)

    scal = jnp.concatenate(
        [
            jnp.stack([tensor_index // 2, dp_index % 2, tensor_index % 2, dp_index, tensor_index]).astype(jnp.int32),
            long_lengths,
            short_lengths,
        ]
    )
    w_qkv = jnp.swapaxes(w_qkv, 2, 3)

    chain = [scal]

    def ordered(outs):
        small = min(outs, key=lambda a: a.size)
        chain[0] = lax.optimization_barrier((scal, small))[0]
        return outs

    def run(kernel, ins, outs, name, scratch=()):
        return ordered(
            pl.pallas_call(
                kernel,
                grid_spec=pltpu.PrefetchScalarGridSpec(
                    num_scalar_prefetch=1,
                    grid=(1,),
                    in_specs=[s for _, s in ins],
                    out_specs=[pl.BlockSpec(s, lambda i, t, n=len(s): (0,) * n) for s, _ in outs],
                    scratch_shapes=list(scratch),
                ),
                out_shape=[jax.ShapeDtypeStruct(s, d) for s, d in outs],
                name=name,
                cost_estimate=pl.CostEstimate(flops=0 if name in LIGHT else HEAVY, bytes_accessed=1, transcendentals=0),
                compiler_params=pltpu.CompilerParams(vmem_limit_bytes=VMEM_LIMIT),
            )(chain[0], *[array for array, _ in ins])
        )

    def flow(*args, **named):
        return ordered(stream(chain[0], *args, **named))

    def tie(value, token):
        return lax.optimization_barrier((value, token))[0]

    def settle(*arrived):
        chain[0] = lax.optimization_barrier((chain[0],) + arrived)[0]

    spec = pl.BlockSpec
    full = lambda a: (a, spec(a.shape, lambda i, s: (0,) * len(a.shape)))
    top_rows = lambda a, n: (a, spec((n,) + a.shape[1:], lambda i, s: (0,) * len(a.shape)))
    top_shape = (devices, 1, 128)
    top_store = Store(top_shape, F32)

    def weight_halves(l):
        return run(
            halves_kernel,
            [
                (w_qkv, spec((None, 3, heads_width, width // 2), lambda i, s: (l, 0, 0, s[Y]))),
                (w_out, spec((None, heads_width, width // 2), lambda i, s: (l, 0, s[Y]))),
                (w_up, spec((None, width // 2, units), lambda i, s: (l, s[Y], 0))),
                (w_down, spec((None, units // 2, width), lambda i, s: (l, s[Y], 0))),
            ],
            [((4, heads_width, width // 2), BF16), ((width // 2, units), BF16), ((units // 2, width), BF16)],
            "halves",
        )

    sends = weight_halves(0)
    vecs, small, top, input_sum = run(
        start_kernel,
        [full(a) for a in (hidden, bias_out, ln_gain, ln_bias, bias_down, bias_qv, bias_up)],
        [((LAYERS * VECS, width), F32), ((LAYERS * 3, units), F32), (top_shape, F32), ((1, 128), F32)],
        "start",
    )
    top = over_ranks(top)
    other_hidden = core_swap(hidden)
    small = x_swap(small)
    near = [[x_swap(sends[0]), x_swap(tie(sends[1], (top, small))), None], [None] * 3]
    far = [[dp_swap(tie(near[0][0], top), 1), None, None], [None] * 3]
    other_cotangent = core_swap(cotangent)

    saved = []
    square_terms = []
    states = None
    for l in range(LAYERS):
        last = l == LAYERS - 1
        first = l == 0
        attend_stores = lambda n: [
            per_side_out((n, 3, rows, heads_width), BF16),
            side_rows_out((n, rows, heads_width), F32, 0, 4),
            side_rows_out((n, 3, rows, rows), BF16, 1, 4),
            side_rows_out((n, rows, heads_width), F32, 0, 4),
            top_store,
        ]
        low_stores = [rows_out((rows, width), BF16, 2), rows_out((rows, width), BF16, 2)]
        own_loads = [whole_in(top), whole_in(vecs), layer_in(w_qkv, l)]
        scores = [pltpu.VMEM((rows, rows), F32)]
        if first:
            low_in, fac_in, *parts, own_top = flow(
                partial(attend_body, l, 2, (0,)),
                [pair_in(hidden, other_hidden, 2)] + own_loads,
                low_stores + attend_stores(1),
                "attend_own",
                scratch=scores,
            )
            next_sends = weight_halves(1)
            settle(near[0][1], other_cotangent)
            near[0][2] = x_swap(tie(sends[2], next_sends[0]))
            far[0][1] = dp_swap(tie(near[0][1], next_sends[0]), 1)
            *more, top = flow(
                partial(attend_body, l, 2, (1,)),
                [whole_in(low_in), whole_in(near[l][0]), whole_in(far[l][0]), whole_in(small), whole_in(own_top)],
                attend_stores(1),
                "attend_oth",
                scratch=scores,
            )
            qkv, ctx, soft, rinv = zip(parts, more)
        else:
            low_in, fac_in, *parts, top = flow(
                partial(attend_body, l, 2, (0, 1)),
                [rows_in(states, 2)] + own_loads + [whole_in(near[l][0]), whole_in(far[l][0]), whole_in(small)],
                low_stores + attend_stores(2),
                "attend",
                scratch=scores,
            )
            qkv, ctx, soft, rinv = [(v,) for v in parts]
        if first:
            top = over_ranks(tie(top, (near[0][2], far[0][1])))
            near[1][0] = x_swap(tie(next_sends[0], top))
            far[0][2] = dp_swap(tie(near[0][2], top), 1)
            window = (near[1][0], far[0][2])
        else:
            top = over_ranks(tie(top, (near[1][2], far[1][1])))
            far[1][2] = dp_swap(tie(near[1][2], top), 1)
            window = (far[1][2],)
        att_near, up_near, down_near = near[l]
        att_far, up_far, down_far = far[l]
        low_ctx, fac_ctx, *parts = flow(
            out_body,
            [whole_in(top), side_rows_in(ctx, 2), layer_in(w_out, l), whole_in(att_near), whole_in(att_far)],
            [sides_out((2, rows, heads_width), BF16, 2), sides_out((2, rows, heads_width), BF16, 2)] + [Store((own_rows, width), BF16)] * 2,
            "out_proj",
        )
        norm_stores = [rows_out((rows, width), F32, 4), rows_out((rows, width), BF16, 4), rows_out((rows, 128), F32, 4),
                       Store((2, 128), F32), top_store]
        middle, unit_one, inv_one, sums_one, top = flow(
            partial(norm_body, l, False, 4),
            [whole_in(vecs), pair_in(hidden, other_hidden, 4) if first else rows_in(states, 4), pair_in(*parts, 4),
             pair_in(*[core_swap(v) for v in parts[::-1]], 4)],
            norm_stores,
            "norm_one",
        )
        top = over_ranks(tie(top, window))
        low_mid, fac_mid, active, slope, top = flow(
            partial(up_body, l, 2),
            [whole_in(top), rows_in(middle, 2), whole_in(vecs), layer_in(w_up, l), whole_in(up_near), whole_in(up_far), whole_in(small)],
            [rows_out((rows, width), BF16, 2), rows_out((rows, width), BF16, 2), sides_out((2, rows, units), F32, 2),
             sides_out((2, rows, units), BF16, 2), top_store],
            "up_proj",
        )
        top = over_ranks(top)
        if first:
            near[1][1] = x_swap(tie(next_sends[1], top))
            far[1][0] = dp_swap(tie(near[1][0], top), 1)
        low_act, fac_act, *parts = flow(
            down_body,
            [whole_in(top), sides_in(active, 2), sides_in(slope, 2), layer_in(w_down, l), whole_in(down_near), whole_in(down_far)],
            [sides_out((2, rows, units), BF16, 2), sides_out((2, rows, units), BF16, 2)] + [Store((own_rows, width), BF16)] * 2,
            "down_proj",
        )
        square_terms += [input_sum, sums_one]
        keep = (low_in, fac_in, qkv, ctx, soft, rinv, low_ctx, fac_ctx, unit_one, inv_one, low_mid, fac_mid, low_act, fac_act)
        recvs = [core_swap(v) for v in parts[::-1]]
        if not last:
            states, unit_two, inv_two, sums_two, top = flow(
                partial(norm_body, l, True, 4),
                [whole_in(vecs), rows_in(middle, 4), pair_in(*parts, 4), pair_in(*recvs, 4)],
                norm_stores,
                "norm_two",
            )
            square_terms.append(sums_two)
            input_sum = sums_two[1:2]
            top = over_ranks(tie(top, (near[1][1], far[1][0])))
            near[1][2] = x_swap(tie(next_sends[2], top))
            far[1][1] = dp_swap(tie(near[1][1], top), 1)
            keep += (unit_two, inv_two)
        saved.append(keep)

    sums = [None] * LAYERS
    band = width // dp_size
    banded = band % 16 == 0

    half_width = width // 2

    def grad_group(kind, ins, columns, bit):
        cut = band * 2 if bit == 2 else band
        if not banded:
            stores = [per_side_out((2, width, columns), BF16)] * 2
            bit = None
        elif bit == 1:
            stores = [Store((width, columns), BF16)] * 2 + [per_side_out((2, half_width, columns), BF16)] * 2
        else:
            stores = [per_side_out((2, 2, half_width, columns), BF16)] * 2
        return flow(
            partial(grad_body, kind, bit, cut),
            [whole_in(a) for a in ins],
            stores,
            kind + "_grad",
            scratch=[pltpu.VMEM((width, columns), F32)],
        )

    def begin(group, token):
        own, oth, keep, send = group
        return own, x_swap(tie(oth, token)), keep, dp_swap(tie(send, token), 1)

    def second(pending):
        columns = pending[0].shape[1]
        return run(
            partial(second_kernel, band),
            [full(a) for a in pending],
            [((half_width, columns), BF16)] * 4,
            "second",
            scratch=[pltpu.VMEM((width, columns), F32)],
        )

    def crossed(outs, token):
        xkeep, xsend, yown, yoth = outs
        return xkeep, dp_swap(tie(xsend, token), 1), yown, x_swap(tie(yoth, token))

    def fold(ins, bit):
        remaining, columns = ins[0].shape[-2:]
        lead = 2 if len(ins) == 4 else ins[0].shape[0]
        return run(
            partial(fold_kernel, band, bit),
            [full(a) for a in ins],
            [((lead, remaining // 2, columns), BF16)] * 2,
            "fold",
            scratch=[pltpu.VMEM((lead, remaining, columns), F32)],
        )

    def sent(outs, bit, token):
        return outs[0], dp_swap(tie(outs[1], token), bit)

    count_rows = LAYERS * (6 + 2 * tensor_size) + 1
    packed_rows = -(-count_rows // devices) * devices
    chunk = packed_rows // devices

    def packed_sums():
        (packed,) = run(
            partial(pack_kernel, tensor_size, heads_width),
            [full(a) for l in range(LAYERS) for a in sums[l]] + [full(a) for a in square_terms],
            [((packed_rows, 1, width), F32)],
            "pack",
        )
        return over_ranks(packed.reshape(devices, chunk, width)).reshape(devices, chunk, width)

    def total_sums(packed):
        (totals,) = run(total_kernel, [full(packed)], [((devices, chunk, width), F32)], "total")
        return over_ranks(totals).reshape(packed_rows, 1, width)

    def unpacked_sums(totals):
        return run(
            partial(unpack_kernel, tensor_size, heads_width, count_model),
            [full(totals)],
            [(s, F32) for s in ((LAYERS, 2, heads_width), (LAYERS, width), (LAYERS, 2, width), (LAYERS, 2, width), (LAYERS, units),
                                (LAYERS, width), (LAYERS, 3))],
            "unpack",
        )

    def ffn_back(l, ins, extra):
        return flow(
            partial(ffn_back_body, l, l == LAYERS - 1, 2),
            ins + [sides_in(saved[l][13], 2), layer_in(w_down, l), whole_in(near[l][2]), whole_in(far[l][2]), layer_in(w_up, l),
                   whole_in(near[l][1]), whole_in(far[l][1])],
            [rows_out((rows, width), F32, 2), rows_out((rows, width), BF16, 2), sides_out((2, rows, units), BF16, 2),
             rows_out((rows, width), BF16, 2), Store((3, width), F32), Store((2, units), F32)] + extra,
            "ffn_back",
        )

    def attn_back(l, part, recv, dz_two, split):
        (low_in, fac_in, qkv, ctx, soft, rinv, low_ctx, fac_ctx, unit_one, inv_one, low_mid, fac_mid) = saved[l][:12]
        return flow(
            partial(attn_back_body, l, split, 2),
            [whole_in(vecs), rows_in(part, 2), rows_in(recv, 2, True), rows_in(fac_mid, 2), rows_in(dz_two, 2), rows_in(unit_one, 2),
             rows_in(inv_one, 2), layer_in(w_out, l), per_side_in((fac_ctx,)), per_side_in(rinv), per_side_in(ctx), per_side_in(qkv),
             per_side_in(soft), layer_in(w_qkv, l), whole_in(near[l][0]), whole_in(far[l][0])],
            [rows_out((rows, width), F32, 2), rows_out((rows, width), BF16, 2), per_side_out((2, rows, 3 * heads_width), BF16),
             Store((3, width), F32), Store((2, 2, heads_width), F32)]
            + ([Store((own_rows, width), BF16)] * 2 if split else [rows_out((rows, width), BF16, 2)]),
            "attn_back",
            scratch=[pltpu.VMEM((rows, width), F32)],
        )

    attn_columns = 2 * heads_width
    ins = [whole_in(vecs), rows_in(middle, 2), pair_in(*parts, 2), pair_in(*recvs, 2), pair_in(cotangent, other_cotangent, 2)]
    dz_two, df, du, part, sums_two, unit_sums, output, branch_sum = ffn_back(
        1, ins, [Store((own_rows, width), BF16), Store((1, 128), F32)]
    )
    square_terms.append(branch_sum)
    recv = core_swap(part)
    ffn_one = grad_group("ffn", [df, saved[1][12], saved[1][10], du], units, 1)
    if banded:
        ffn_one = begin(ffn_one, scal)
    dz_one, do, dqkv, sums_one, head_sums, part = attn_back(1, part, recv, dz_two, False)
    recv = core_swap(part)
    sums[1] = (sums_one, sums_two, head_sums, unit_sums)
    attn_one = grad_group("attn", [saved[1][0], dqkv, do, saved[1][6]], attn_columns, 1)
    if banded:
        attn_one = begin(attn_one, scal)
    ins = [whole_in(vecs), rows_in(part, 2), rows_in(recv, 2, True), rows_in(saved[1][1], 2), rows_in(dz_one, 2),
           rows_in(saved[0][14], 2), rows_in(saved[0][15], 2)]
    dz_two, df, du, part, sums_two, unit_sums = ffn_back(0, ins, [])
    recv = core_swap(part)
    if banded:
        ffn_one = second(ffn_one)
        ffn_one = crossed(ffn_one, scal)
    ffn_zero = grad_group("ffn", [df, saved[0][12], saved[0][10], du], units, 1)
    if banded:
        attn_one = second(attn_one)
        ffn_zero = begin(ffn_zero, attn_one[0])
        settle(ffn_one[1], ffn_one[3])
        ffn_one = fold(ffn_one, 2)
        ffn_one = sent(ffn_one, 2, scal)
    dz_one, do, dqkv, sums_one, head_sums, part, away = attn_back(0, part, recv, dz_two, True)
    recv = core_swap(away)
    sums[0] = (sums_one, sums_two, head_sums, unit_sums)
    attn_zero = grad_group("attn", [saved[0][0], dqkv, do, saved[0][6]], attn_columns, 1)
    (grad_hidden,) = run(
        dx_kernel,
        [full(part), full(recv), top_rows(saved[0][1], own_rows), top_rows(dz_one, own_rows)],
        [((own_rows, width), F32)],
        "dx",
    )
    if banded:
        attn_one = crossed(attn_one, grad_hidden)
        ffn_one = fold(ffn_one, 4)
        ffn_one = sent(ffn_one, 4, scal)
        ffn_zero = second(ffn_zero)
        ffn_zero = crossed(ffn_zero, scal)
        attn_one = fold(attn_one, 2)
        attn_zero = begin(attn_zero, attn_one[0])
    packed = packed_sums()
    if banded:
        attn_one = sent(attn_one, 2, ffn_one[1])
        ffn_zero = fold(ffn_zero, 2)
        ffn_zero = sent(ffn_zero, 2, scal)
        attn_one = fold(attn_one, 4)
        attn_one = sent(attn_one, 4, scal)
        attn_zero = second(attn_zero)
        attn_zero = crossed(attn_zero, scal)
        totals = total_sums(packed)
        ffn_zero = fold(ffn_zero, 4)
        ffn_zero = sent(ffn_zero, 4, scal)
        attn_zero = fold(attn_zero, 2)
        attn_zero = sent(attn_zero, 2, scal)
        attn_zero = fold(attn_zero, 4)
        attn_zero = sent(attn_zero, 4, scal)
        small_outs = unpacked_sums(totals)
        grad_qkv, grad_out, grad_up, grad_down = run(
            partial(final_kernel, heads_width),
            [full(a) for pair in (ffn_one, attn_one, ffn_zero, attn_zero) for a in pair],
            [((LAYERS, 3, band, heads_width), F32), ((LAYERS, band, heads_width), F32), ((LAYERS, band, units), F32),
             ((LAYERS, band, width), F32)],
            "final",
        )
    else:
        small_outs = unpacked_sums(total_sums(packed))
        totals = []
        for own, oth in (ffn_zero, ffn_one, attn_zero, attn_one):
            both = own.astype(F32) + x_swap(oth).astype(F32)
            totals.append(lax.psum_scatter(both, "dp", scatter_dimension=1, tiled=True))
        grad_up = jnp.stack([totals[0][0], totals[1][0]])
        grad_down = jnp.stack([totals[0][1], totals[1][1]])
        attn = jnp.stack(totals[2:])
        cut = lambda side, at: attn[:, side, :, at * heads_width : (at + 1) * heads_width]
        grad_qkv = jnp.stack([cut(0, 0), cut(0, 1), cut(1, 0)], 1)
        grad_out = cut(1, 1)

    head_bias, out_bias, gains, shifts, unit_bias, down_bias, rms = small_outs
    return (
        output,
        grad_hidden,
        grad_qkv,
        head_bias,
        jnp.swapaxes(grad_out, 1, 2),
        out_bias,
        gains,
        shifts,
        grad_up,
        unit_bias,
        jnp.swapaxes(grad_down, 1, 2),
        down_bias,
        rms,
    )


def solution(mesh):
    in_specs = (
        P(("dp", "tensor"), None),
        P("dp"),
        P("dp"),
        P(None, None, None, "tensor"),
        P(None, None, "tensor"),
        P(None, "tensor", None),
        P(),
        P(),
        P(),
        P(None, None, "tensor"),
        P(None, "tensor"),
        P(None, "tensor", None),
        P(),
        P(("dp", "tensor"), None),
    )
    out_specs = (
        P(("dp", "tensor"), None),
        P(("dp", "tensor"), None),
        P(None, None, "dp", "tensor"),
        P(None, None, "tensor"),
        P(None, "tensor", "dp"),
        P(),
        P(),
        P(),
        P(None, "dp", "tensor"),
        P(None, "tensor"),
        P(None, "tensor", "dp"),
        P(),
        P(),
    )
    return jax.shard_map(body, mesh=mesh, in_specs=in_specs, out_specs=out_specs, check_vma=False)
```

```python
from functools import partial

import jax
import jax.numpy as jnp
from jax import lax
from jax.experimental import pallas as pl
from jax.experimental.pallas import tpu as pltpu
from jax.sharding import PartitionSpec as P

HEAD_DIM = 64
LAYERS = 2
LONG_LEN = 512
SHORT_LEN = 128
LONG_DEV = 1
SHORT_DEV = 4

EPS = 1e-06
MASKED = -1e30
BOTH = ("dp", "tensor")
F32 = jnp.float32
BF16 = jnp.bfloat16
VMEM_LIMIT = 60 * 1024 * 1024
HEAVY = 10**15
LIGHT = {"halves", "norm_one", "norm_two", "up_proj", "second", "fold"}

X, Y, CORE, DP, SHARD, LENGTHS = range(6)


def nt(left, right):
    return lax.dot_general(left, right, (((1,), (1,)), ((), ())), preferred_element_type=F32)


def nn(left, right):
    return jnp.dot(left, right, preferred_element_type=F32)


def tn(left, right):
    return lax.dot_general(left, right, (((0,), (0,)), ((), ())), preferred_element_type=F32)


def merge(values):
    return values.reshape(values.shape[0] * values.shape[1], values.shape[2])


def bound_of(top_ref):
    return jnp.max(top_ref[...]) * 0.25 + EPS


def halves(scal, width):
    part = width // 2
    near = scal[Y]
    first = pl.ds(pl.multiple_of(near * part, part), part)
    second = pl.ds(pl.multiple_of((1 - near) * part, part), part)
    return first, second


class Load:
    def __init__(self, shape, dtype, pieces):
        self.shape, self.dtype, self.pieces = tuple(shape), dtype, pieces


class Store:
    def __init__(self, shape, dtype, pieces=((),)):
        self.shape, self.dtype, self.pieces = tuple(shape), dtype, pieces


def view(ref, index):
    return ref.at[index] if index else ref


class Arriving:
    def __init__(self, ref, copies):
        self.ref, self.copies, self.waited = ref, copies, set()

    def wait(self, piece):
        if piece not in self.waited:
            self.copies[piece].wait()
            self.waited.add(piece)
        return self.ref

    def all(self):
        for piece in range(len(self.copies)):
            self.wait(piece)
        return self.ref


class Leaving:
    def __init__(self, ref, copies):
        self.ref, self.copies, self.started = ref, copies, set()

    def flush(self, piece=0):
        self.copies[piece].start()
        self.started.add(piece)


def stream(scal, body, loads, stores, name, scratch=()):
    arrays = []

    def slot(array):
        for i, known in enumerate(arrays):
            if known is array:
                return i
        arrays.append(array)
        return len(arrays) - 1

    plan = [[(slot(a), src, dst) for a, src, dst in load.pieces] for load in loads]
    first_out = len(arrays)
    n_in = sum(len(p) for p in plan)
    n_out = sum(len(st.pieces) for st in stores)

    def kernel(scal_ref, *refs):
        sources = refs[: len(arrays)]
        targets = refs[first_out : first_out + len(stores)]
        at = first_out + len(stores)
        vin, at = refs[at : at + len(loads)], at + len(loads)
        vout, at = refs[at : at + len(stores)], at + len(stores)
        extra, (sem_in, sem_out) = refs[at:-2], refs[-2:]
        count = 0
        arriving = []
        for pieces, ref in zip(plan, vin):
            copies = []
            for i, src, dst in pieces:
                copies.append(pltpu.make_async_copy(view(sources[i], src), view(ref, dst), sem_in.at[count]))
                count += 1
            arriving.append(Arriving(ref, copies))
        for piece in range(max(len(p) for p in plan)):
            for a in arriving:
                if piece < len(a.copies):
                    a.copies[piece].start()
        count = 0
        leaving = []
        for st, ref, target in zip(stores, vout, targets):
            copies = []
            for index in st.pieces:
                copies.append(pltpu.make_async_copy(view(ref, index), view(target, index), sem_out.at[count]))
                count += 1
            leaving.append(Leaving(ref, copies))
        body(scal_ref, arriving, leaving, *extra)
        for a in arriving:
            a.all()
        for out in leaving:
            for piece, copy in enumerate(out.copies):
                if piece not in out.started:
                    copy.start()
        for out in leaving:
            for copy in out.copies:
                copy.wait()

    anywhere = pl.BlockSpec(memory_space=pl.ANY)
    return pl.pallas_call(
        kernel,
        in_specs=[pl.BlockSpec(memory_space=pltpu.SMEM)] + [anywhere] * first_out,
        out_specs=[anywhere] * len(stores),
        out_shape=[jax.ShapeDtypeStruct(st.shape, st.dtype) for st in stores],
        scratch_shapes=[pltpu.VMEM(x.shape, x.dtype) for x in list(loads) + list(stores)]
        + list(scratch)
        + [pltpu.SemaphoreType.DMA((n_in,)), pltpu.SemaphoreType.DMA((n_out,))],
        name=name,
        cost_estimate=pl.CostEstimate(flops=0 if name in LIGHT else HEAVY, bytes_accessed=1, transcendentals=0),
        compiler_params=pltpu.CompilerParams(vmem_limit_bytes=VMEM_LIMIT),
    )(scal, *arrays)


ALL = slice(None)


def span(i, size):
    return pl.ds(i * size, size)


def whole_in(a):
    return Load(a.shape, a.dtype, [(a, (), ())])


def layer_in(a, layer):
    return Load(a.shape[1:], a.dtype, [(a, (layer,), ())])


def rows_in(a, count, swap=False):
    size = a.shape[0] // count
    turn = count // 2 if swap else 0
    return Load(a.shape, a.dtype, [(a, (span((i + turn) % count, size),), (span(i, size),)) for i in range(count)])


def pair_in(mine, other, count):
    rows, width = mine.shape
    size = 2 * rows // count
    half = count // 2
    return Load(
        (2 * rows, width),
        mine.dtype,
        [((mine if i < half else other), (span(i % half, size),), (span(i, size),)) for i in range(count)],
    )


def sides_in(a, count):
    size = a.shape[1] // count
    return Load(a.shape, a.dtype, [(a, (ALL, span(i, size)), (ALL, span(i, size))) for i in range(count)])


def side_rows_in(parts, count):
    size = parts[0].shape[1] // count
    sources = [(a, i) for a in parts for i in range(a.shape[0])]
    return Load(
        (2,) + parts[0].shape[1:],
        parts[0].dtype,
        [(a, (s, span(i, size)), (side, span(i, size))) for i in range(count) for side, (a, s) in enumerate(sources)],
    )


def per_side_in(parts):
    pieces = [(a, (i,)) for a in parts for i in range(a.shape[0])]
    return Load((2,) + parts[0].shape[1:], parts[0].dtype, [(a, src, (i,)) for i, (a, src) in enumerate(pieces)])


def rows_out(shape, dtype, count):
    size = shape[0] // count
    return Store(shape, dtype, [(span(i, size),) for i in range(count)])


def sides_out(shape, dtype, count):
    size = shape[1] // count
    return Store(shape, dtype, [(ALL, span(i, size)) for i in range(count)])


def side_rows_out(shape, dtype, lead, count):
    size = shape[1 + lead] // count
    return Store(shape, dtype, [(s,) + (ALL,) * lead + (span(i, size),) for s in range(shape[0]) for i in range(count)])


def per_side_out(shape, dtype):
    return Store(shape, dtype, [(i,) for i in range(shape[0])])


B_OUT, GAIN_ONE, SHIFT_ONE, B_DOWN, GAIN_TWO, SHIFT_TWO, B_Q, B_V, B_UP, VECS = range(10)


def vec(ref, layer, row, width=None):
    at = layer * VECS + row
    return ref[at : at + 1, :] if width is None else ref[at : at + 1, 0:width]


def start_kernel(scal, hidden_ref, bout_ref, gain_ref, shift_ref, bdown_ref, bqv_ref, bup_ref, vecs_ref, small_ref, top_ref, sums_ref):
    heads_width = bqv_ref.shape[2]
    vecs_ref[...] = jnp.zeros(vecs_ref.shape, F32)
    small_ref[...] = jnp.zeros(small_ref.shape, F32)
    for layer in range(LAYERS):
        base = layer * VECS
        one = slice(layer, layer + 1)
        vecs_ref[base + B_OUT : base + B_OUT + 1, :] = bout_ref[one, :]
        vecs_ref[base + B_DOWN : base + B_DOWN + 1, :] = bdown_ref[one, :]
        vecs_ref[base + GAIN_ONE : base + GAIN_ONE + 1, :] = gain_ref[layer, 0:1, :]
        vecs_ref[base + GAIN_TWO : base + GAIN_TWO + 1, :] = gain_ref[layer, 1:2, :]
        vecs_ref[base + SHIFT_ONE : base + SHIFT_ONE + 1, :] = shift_ref[layer, 0:1, :]
        vecs_ref[base + SHIFT_TWO : base + SHIFT_TWO + 1, :] = shift_ref[layer, 1:2, :]
        for ref, at in ((vecs_ref, base + B_Q), (small_ref, 3 * layer)):
            ref[at : at + 1, 0:heads_width] = bqv_ref[layer, 0:1, :]
            ref[at + 1 : at + 2, 0:heads_width] = bqv_ref[layer, 1:2, :]
            ref[at + 2 : at + 3, :] = bup_ref[one, :]
    values = hidden_ref[...].astype(F32)
    top_ref[...] = jnp.full(top_ref.shape, jnp.max(jnp.abs(values)), F32)
    sums_ref[...] = jnp.full((1, 128), jnp.sum(values * values), F32)


def halves_kernel(scal, wqkv_ref, wout_ref, wup_ref, wdown_ref, att_ref, up_ref, down_ref):
    att_ref[0:3] = wqkv_ref[...]
    att_ref[3] = wout_ref[...]
    up_ref[...] = wup_ref[...]
    down_ref[...] = wdown_ref[...]


def row_ids(scal, slots, half_rows):
    rows = 2 * half_rows
    slot = slots + half_rows * scal[CORE]
    slot = jnp.where(slot >= rows, slot - rows, slot) + scal[X] * rows
    short = slot - LONG_DEV * LONG_LEN
    is_long = short < 0
    row = jnp.where(is_long, slot // LONG_LEN, LONG_DEV + short // SHORT_LEN)
    place = jnp.where(is_long, slot % LONG_LEN, short % SHORT_LEN)
    length = jnp.zeros_like(row)
    for i in range(LONG_DEV + SHORT_DEV):
        length = jnp.where(row == i, scal[LENGTHS + i], length)
    return row, jnp.where(place < length, 1, 0)


HEADS = ((0, 128, 0), (0, 128, 1), (128, 192, None))


def lane_mask(rows, which):
    lane = lax.broadcasted_iota(jnp.int32, (rows, 128), 1)
    return (lane < HEAD_DIM) if which == 0 else (lane >= HEAD_DIM)


def only_head(values, which):
    if which is None:
        return values
    return jnp.where(lane_mask(values.shape[0], which), values, jnp.zeros_like(values))


def largest(values):
    return jnp.max(jnp.abs(values))


def put_top(out, tops):
    top = tops[0]
    for other in tops[1:]:
        top = jnp.maximum(top, other)
    out.ref[...] = jnp.full(out.ref.shape, top, F32)
    out.flush()


def attend_body(layer, count, sides, scal, ins, outs, qcode_ref, kcode_ref, qlast_ref, klast_ref):
    if 0 in sides:
        x_in, top_in, vecs_in, own_in, ins = *ins[:4], ins[4:]
        low_out, fac_out, outs = *outs[:2], outs[2:]
        low_ref = low_out.ref
    else:
        low_in, ins = ins[0], ins[1:]
        low_ref = low_in.all()
    if 1 in sides:
        near_in, far_in, small_in, ins = *ins[:3], ins[3:]
    qkv_out, ctx_out, e_out, rinv_out, top_out = outs
    qkv_ref, ctx_ref, e_ref, rinv_ref = (o.ref for o in (qkv_out, ctx_out, e_out, rinv_out))
    rows, width = low_ref.shape
    heads_width = qkv_ref.shape[3]
    first, second = halves(scal, width)
    row, live = row_ids(scal, lax.broadcasted_iota(jnp.int32, (rows, 1), 0), rows // 2)
    code_lane = lax.broadcasted_iota(jnp.int32, (rows, 128), 1) % HEAD_DIM
    qcode_ref[...] = jnp.where(code_lane == row, 1.0, 0.0).astype(BF16)
    hidden_to = (code_lane < LONG_DEV + SHORT_DEV) & ((code_lane != row) | (live == 0))
    kcode_ref[...] = jnp.where(hidden_to, MASKED, 0.0).astype(BF16)
    qlast_ref[...] = qcode_ref[...]
    klast_ref[...] = kcode_ref[...]
    scale = HEAD_DIM ** (-0.5)
    if 0 in sides:
        bound = bound_of(top_in.all())
        size = rows // count
        vecs_ref = vecs_in.all()
        for i in range(count):
            place = slice(i * size, (i + 1) * size)
            tangent = jnp.tanh(x_in.wait(i)[place, :].astype(F32) * (1.0 / bound))
            low = (bound * tangent).astype(BF16)
            low_ref[place, :] = low
            low_out.flush(i)
            fac_out.ref[place, :] = (1.0 - tangent * tangent).astype(BF16)
            fac_out.flush(i)
            own_ref = own_in.all()
            for j in range(3):
                values = nt(low, own_ref[j])
                if j != 1:
                    values = values + vec(vecs_ref, layer, B_Q + j // 2, heads_width)
                qkv_ref[0, j, place, :] = (values * scale if j == 0 else values).astype(BF16)
        qkv_out.flush(0)
    chunk = 512
    chunks = rows // chunk
    tops = []
    for at, side in enumerate(sides):
        if side == 1:
            near_ref, far_ref, small_ref = near_in.all(), far_in.all(), small_in.all()
            for j in range(3):
                values = nt(low_ref[:, first], near_ref[j]) + nt(low_ref[:, second], far_ref[j])
                if j != 1:
                    row = 3 * layer + j // 2
                    values = values + small_ref[row : row + 1, 0:heads_width]
                qkv_ref[at, j] = (values * scale if j == 0 else values).astype(BF16)
            qkv_out.flush(at)
        qlast_ref[:, 0:HEAD_DIM] = qkv_ref[at, 0, :, 128:192]
        klast_ref[:, 0:HEAD_DIM] = qkv_ref[at, 1, :, 128:192]
        heads = []
        for h, (lo, hi, which) in enumerate(HEADS):
            if which is None:
                keys = klast_ref[...]
            else:
                keys = jnp.where(lane_mask(rows, which), qkv_ref[at, 1, :, lo:hi], kcode_ref[...])
            heads.append((h, lo, hi, which, keys, qkv_ref[at, 2, :, lo:hi]))
        left = lane_mask(chunk, 0)
        for i in range(chunks):
            place = slice(i * chunk, (i + 1) * chunk)
            done = []
            for h, lo, hi, which, keys, vals in heads:
                if which is None:
                    asking = qlast_ref[place, :]
                else:
                    asking = jnp.where(lane_mask(chunk, which), qkv_ref[at, 0, place, lo:hi], qcode_ref[place, :])
                scores = nt(asking, keys)
                weights = jnp.exp(scores - jnp.max(scores, axis=1, keepdims=True))
                inverse = 1.0 / jnp.sum(weights, axis=1, keepdims=True)
                low = weights.astype(BF16)
                e_ref[at, h, place, :] = low
                done.append((nn(low, vals) * inverse, inverse))
            pair = jnp.where(left, done[0][0], done[1][0])
            ctx_ref[at, place, 0:128] = pair
            ctx_ref[at, place, 128:192] = done[2][0]
            tops += [largest(pair), largest(done[2][0])]
            rinv_ref[at, place, 0:128] = jnp.where(left, done[0][1], done[1][1])
            rinv_ref[at, place, 128:192] = jnp.broadcast_to(done[2][1], (chunk, HEAD_DIM))
            for out in (e_out, ctx_out, rinv_out):
                out.flush(at * chunks + i)
    tops += [jnp.max(load.all()[...]) for load in ins]
    put_top(top_out, tops)


def out_body(scal, ins, outs):
    top_in, ctx_in, own_in, near_in, far_in = ins
    c_out, fac_out, *o_outs = outs
    bound = bound_of(top_in.all())
    size, width = o_outs[0].ref.shape
    for i, o_out in enumerate(o_outs):
        place = slice(i * size, (i + 1) * size)
        ctx_in.wait(2 * i)
        tangent = jnp.tanh(ctx_in.wait(2 * i + 1)[:, place, :] * (1.0 / bound))
        low = (bound * tangent).astype(BF16)
        c_out.ref[:, place, :] = low
        c_out.flush(i)
        fac_out.ref[:, place, :] = (1.0 - tangent * tangent).astype(BF16)
        fac_out.flush(i)
        own_ref = own_in.all()
        for part, load in zip(halves(scal, width), (near_in, far_in)):
            o_out.ref[:, part] = (nn(low[0], own_ref[:, part]) + nn(low[1], load.all()[3])).astype(BF16)
        o_out.flush()


def norm_forward(mixed, gain, shift):
    centred = mixed - jnp.mean(mixed, axis=1, keepdims=True)
    inverse = lax.rsqrt(jnp.mean(centred * centred, axis=1, keepdims=True) + EPS)
    unit = centred * inverse
    return unit * gain + shift, unit, inverse


def lane_fill(value):
    return jnp.full((1, 128), value, F32)


def norm_body(layer, second, count, scal, ins, outs):
    vecs_in, x_in, self_in, recv_in = ins
    h_out, unit_out, inv_out, sums_out, top_out = outs
    rows, width = h_out.ref.shape
    size = rows // count
    vecs_ref = vecs_in.all()
    bias = vec(vecs_ref, layer, B_DOWN if second else B_OUT)
    gain = vec(vecs_ref, layer, GAIN_TWO if second else GAIN_ONE)
    shift = vec(vecs_ref, layer, SHIFT_TWO if second else SHIFT_ONE)
    tops, branch_sum, result_sum = [], 0.0, 0.0
    for i in range(count):
        place = slice(i * size, (i + 1) * size)
        branch = self_in.wait(i)[place, :].astype(F32) + recv_in.wait(i)[place, :].astype(F32) + bias
        result, unit, inverse = norm_forward(x_in.wait(i)[place, :].astype(F32) + branch, gain, shift)
        h_out.ref[place, :] = result
        h_out.flush(i)
        unit_out.ref[place, :] = unit.astype(unit_out.ref.dtype)
        unit_out.flush(i)
        inv_out.ref[place, :] = jnp.broadcast_to(inverse, (size, 128))
        inv_out.flush(i)
        tops.append(largest(result))
        if i < count // 2:
            branch_sum = branch_sum + jnp.sum(branch * branch)
            result_sum = result_sum + jnp.sum(result * result)
    sums_out.ref[0:1, :] = lane_fill(branch_sum)
    sums_out.ref[1:2, :] = lane_fill(result_sum)
    sums_out.flush()
    put_top(top_out, tops)


def up_body(layer, count, scal, ins, outs):
    top_in, h_in, vecs_in, own_in, near_in, far_in, small_in = ins
    low_out, fac_out, g_out, slope_out, top_out = outs
    low_ref = low_out.ref
    rows, width = low_ref.shape
    size = rows // count
    bound = bound_of(top_in.all())
    first, second = halves(scal, width)
    tops = []
    for i in range(count):
        place = slice(i * size, (i + 1) * size)
        tangent = jnp.tanh(h_in.wait(i)[place, :] * (1.0 / bound))
        low = (bound * tangent).astype(BF16)
        low_ref[place, :] = low
        low_out.flush(i)
        fac_out.ref[place, :] = (1.0 - tangent * tangent).astype(BF16)
        fac_out.flush(i)
        for side in range(2):
            if side == 0:
                units = nn(low, own_in.all()[...]) + vec(vecs_in.all(), layer, B_UP)
            else:
                units = nn(low_ref[place, first], near_in.all()[...]) + nn(low_ref[place, second], far_in.all()[...])
                units = units + small_in.all()[3 * layer + 2 : 3 * layer + 3, :]
            area = 0.5 + 0.5 * lax.erf(units * (0.5**0.5))
            density = jnp.exp(-0.5 * units * units) * 0.3989422804014327
            active = units * area
            g_out.ref[side, place, :] = active
            slope_out.ref[side, place, :] = (area + units * density).astype(BF16)
            tops.append(largest(active))
        g_out.flush(i)
        slope_out.flush(i)
    put_top(top_out, tops)


def down_body(scal, ins, outs):
    top_in, g_in, slope_in, own_in, near_in, far_in = ins
    low_out, fac_out, *f_outs = outs
    low_ref = low_out.ref
    size = f_outs[0].ref.shape[0]
    bound = bound_of(top_in.all())
    first, second = halves(scal, low_ref.shape[2])
    for i, f_out in enumerate(f_outs):
        place = slice(i * size, (i + 1) * size)
        tangent = jnp.tanh(g_in.wait(i)[:, place, :] * (1.0 / bound))
        low_ref[:, place, :] = (bound * tangent).astype(BF16)
        low_out.flush(i)
        slope = slope_in.wait(i)[:, place, :].astype(F32)
        fac_out.ref[:, place, :] = ((1.0 - tangent * tangent) * slope).astype(BF16)
        fac_out.flush(i)
        f_out.ref[...] = (
            nn(low_ref[0, place, :], own_in.all()[...])
            + nn(low_ref[1, place, first], near_in.all()[...])
            + nn(low_ref[1, place, second], far_in.all()[...])
        ).astype(BF16)
        f_out.flush()


def norm_back(grad, unit, inverse, gain):
    scaled = grad * gain
    return (
        scaled
        - jnp.mean(scaled, axis=1, keepdims=True)
        - unit * jnp.mean(scaled * unit, axis=1, keepdims=True)
    ) * inverse


def column_sums(values):
    return jnp.sum(values, axis=0, keepdims=True)


def ffn_back_body(layer, last_layer, count, scal, ins, outs):
    vecs_in, ins = ins[0], ins[1:]
    if last_layer:
        (h_in, self_in, recv_in, cot_in), ins = ins[:4], ins[4:]
        result_out, fsum_out = outs[-2:]
    else:
        (self_in, recv_in, infac_in, skip_in, unit_in, inv_in), ins = ins[:6], ins[6:]
    fac_in, down_in, dnear_in, dfar_in, up_in, unear_in, ufar_in = ins
    dz_out, df_out, du_out, dh_out, sums_out, usum_out = outs[:6]
    rows, width = dz_out.ref.shape
    size = rows // count
    vecs_ref = vecs_in.all()
    gain = vec(vecs_ref, layer, GAIN_TWO)
    first, second = halves(scal, width)
    du_ref = du_out.ref
    totals = None
    unit_totals = None
    branch_sum = 0.0
    for i in range(count):
        place = slice(i * size, (i + 1) * size)
        mine = i < count // 2
        both = self_in.wait(i)[place, :].astype(F32) + recv_in.wait(i)[place, :].astype(F32)
        if last_layer:
            branch = both + vec(vecs_ref, layer, B_DOWN)
            result, unit, inverse = norm_forward(h_in.wait(i)[place, :] + branch, gain, vec(vecs_ref, layer, SHIFT_TWO))
            grad = cot_in.wait(i)[place, :].astype(F32)
            if mine:
                result_out.ref[place, :] = result.astype(BF16)
                result_out.flush(i)
                branch_sum = branch_sum + jnp.sum(branch * branch)
        else:
            grad = both * infac_in.wait(i)[place, :].astype(F32) + skip_in.wait(i)[place, :]
            unit = unit_in.wait(i)[place, :].astype(F32)
            inverse = inv_in.wait(i)[place, 0:1]
        mixed = norm_back(grad, unit, inverse, gain)
        low = mixed.astype(BF16)
        dz_out.ref[place, :] = mixed
        dz_out.flush(i)
        df_out.ref[place, :] = low
        df_out.flush(i)
        if mine:
            new = [column_sums(v) for v in (grad * unit, grad, low.astype(F32))]
            totals = new if totals is None else [a + b for a, b in zip(totals, new)]
        fac_ref = fac_in.wait(i)
        du_ref[0, place, :] = (nt(low, down_in.all()[...]) * fac_ref[0, place, :].astype(F32)).astype(BF16)
        for part, load in ((first, dnear_in), (second, dfar_in)):
            du_ref[1, place, part] = (nt(low, load.all()[...]) * fac_ref[1, place, part].astype(F32)).astype(BF16)
        du_out.flush(i)
        for part, load in ((first, unear_in), (second, ufar_in)):
            dh_out.ref[place, part] = (
                nt(du_ref[0, place, :], up_in.all()[part, :]) + nt(du_ref[1, place, :], load.all()[...])
            ).astype(BF16)
        dh_out.flush(i)
        new = [column_sums(du_ref[side, place, :].astype(F32)) for side in range(2)]
        unit_totals = new if unit_totals is None else [a + b for a, b in zip(unit_totals, new)]
    for row, values in enumerate(totals):
        sums_out.ref[row : row + 1, :] = values
    for row, values in enumerate(unit_totals):
        usum_out.ref[row : row + 1, :] = values
    if last_layer:
        fsum_out.ref[...] = lane_fill(branch_sum)


def attn_back_body(layer, split, count, scal, ins, outs, da_scratch):
    (vecs_in, self_in, recv_in, hfac_in, skip_in, unit_in, inv_in, wout_in, cfac_in, rinv_in, ctx_in, qkv_in, e_in, wqkv_in,
     near_in, far_in) = ins
    dz_out, do_out, d_out, sums_out, hsum_out, da_out = outs[:6]
    rows, width = dz_out.ref.shape
    heads_width = qkv_in.ref.shape[3]
    size = rows // count
    first, second = halves(scal, width)
    gain = vec(vecs_in.all(), layer, GAIN_ONE)
    totals = None
    for i in range(count):
        place = slice(i * size, (i + 1) * size)
        grad = self_in.wait(i)[place, :].astype(F32) + recv_in.wait(i)[place, :].astype(F32)
        grad = grad * hfac_in.wait(i)[place, :].astype(F32) + skip_in.wait(i)[place, :]
        unit = unit_in.wait(i)[place, :].astype(F32)
        mixed = norm_back(grad, unit, inv_in.wait(i)[place, 0:1], gain)
        low = mixed.astype(BF16)
        dz_out.ref[place, :] = mixed
        dz_out.flush(i)
        do_out.ref[place, :] = low
        do_out.flush(i)
        if i < count // 2:
            new = [column_sums(v) for v in (grad * unit, grad, low.astype(F32))]
            totals = new if totals is None else [a + b for a, b in zip(totals, new)]
    for row, values in enumerate(totals):
        sums_out.ref[row : row + 1, :] = values
    do_ref, d_ref = do_out.ref, d_out.ref
    scale = HEAD_DIM ** (-0.5)
    left = lane_mask(rows, 0)
    for side in range(2):
        if side == 0:
            grad_ctx = nt(do_ref[...], wout_in.all()[...])
        else:
            grad_ctx = nt(do_ref[:, first], near_in.all()[3]) + nt(do_ref[:, second], far_in.all()[3])
        grad_ctx = grad_ctx * cfac_in.wait(side)[side].astype(F32)
        low = (grad_ctx * rinv_in.wait(side)[side]).astype(BF16)
        product = low.astype(F32) * ctx_in.wait(side)[side]
        qkv_ref, e_ref = qkv_in.wait(side), e_in.wait(side)
        results = []
        for h, (lo, hi, which) in enumerate(HEADS):
            inner = jnp.sum(only_head(product[:, lo:hi], which), axis=1, keepdims=True)
            values = only_head(qkv_ref[side, 2, :, lo:hi], which)
            weights = e_ref[side, h]
            grad_weights = nt(low[:, lo:hi], values)
            grad_scores = (weights.astype(F32) * (grad_weights - inner)).astype(BF16)
            dq = nn(grad_scores, qkv_ref[side, 1, :, lo:hi]) * scale
            dk = tn(qkv_ref[side, 0, :, lo:hi], grad_scores).T
            dv = tn(low[:, lo:hi], weights).T
            results.append((dq, dk, dv))
        for j in range(3):
            pair = jnp.where(left, results[0][j], results[1][j]).astype(BF16)
            last = results[2][j].astype(BF16)
            d_ref[side, :, j * heads_width : j * heads_width + 128] = pair
            d_ref[side, :, j * heads_width + 128 : (j + 1) * heads_width] = last
            if j != 1:
                at = slice(j // 2, j // 2 + 1)
                hsum_out.ref[side, at, 0:128] = column_sums(pair.astype(F32))
                hsum_out.ref[side, at, 128:192] = column_sums(last.astype(F32))
        d_out.flush(side)
        if side == 0:
            da_scratch[...] = nn(d_ref[0], merge(wqkv_in.all()[...]))
    for i in range(2):
        place = slice(i * rows // 2, (i + 1) * rows // 2)
        for part, load in ((first, near_in), (second, far_in)):
            total = (da_scratch[place, part] + nn(d_ref[1, place, :], merge(load.ref[0:3]))).astype(BF16)
            if split:
                outs[5 + i].ref[:, part] = total
            else:
                da_out.ref[place, part] = total
        if split:
            outs[5 + i].flush()
        else:
            da_out.flush(i)


def bands(bit_value, count, band):
    return [pl.ds(pl.multiple_of((2 * k + bit_value) * band, band), band) for k in range(count)]


def cut_bands(scratch, mine, away, keep_ref, send_ref, band):
    for k, (take, give) in enumerate(zip(mine, away)):
        place = slice(k * band, (k + 1) * band)
        send_ref[place, :] = scratch[give, :].astype(BF16)
        keep_ref[place, :] = scratch[take, :].astype(BF16)


def grad_body(kind, bit, band, scal, ins, outs, scratch):
    if kind == "ffn":
        df_in, gq_in, hq_in, du_in = ins
        columns = hq_in.ref.shape[1]
        x_first = lambda side: tn(hq_in.all()[...], du_in.all()[side])

        def y_first(side, put):
            put(slice(None), tn(df_in.all()[...], gq_in.all()[side]))

    else:
        a_in, d_in, do_in, c_in = ins
        width = c_in.ref.shape[2]
        columns = 2 * width
        x_first = lambda side: tn(a_in.all()[...], d_in.all()[side, :, 0:columns])

        def y_first(side, put):
            put(slice(0, width), tn(a_in.all()[...], d_in.all()[side, :, columns : 3 * width]))
            put(slice(width, columns), tn(do_in.all()[...], c_in.all()[side]))

    if bit is None:
        for side, out in ((0, outs[0]), (1, outs[1])):

            def put(at, values):
                out.ref[1, :, at] = values.astype(BF16)

            out.ref[0] = x_first(side).astype(BF16)
            y_first(side, put)
        return

    def put(at, values):
        scratch[:, at] = values

    keep_out, send_out = outs[-2:]
    value = (scal[DP] // bit) % 2
    count = keep_out.ref.shape[-2] // band
    mine, away = bands(value, count, band), bands(1 - value, count, band)
    if len(outs) == 4:
        own_out, oth_out = outs[:2]
        for side, out in ((1, oth_out), (0, own_out)):
            out.ref[...] = x_first(side).astype(BF16)
            out.flush()
            y_first(side, put)
            cut_bands(scratch, mine, away, keep_out.ref.at[side], send_out.ref.at[side], band)
            send_out.flush(side)
            keep_out.flush(side)
        return
    for side in range(2):
        scratch[...] = x_first(side)
        cut_bands(scratch, mine, away, keep_out.ref.at[side, 0], send_out.ref.at[side, 0], band)
        y_first(side, put)
        cut_bands(scratch, mine, away, keep_out.ref.at[side, 1], send_out.ref.at[side, 1], band)
        send_out.flush(side)
        keep_out.flush(side)


def second_kernel(band, scal, own_ref, recv_ref, keep_ref, got_ref, xkeep_ref, xsend_ref, yown_ref, yoth_ref, scratch):
    count = xkeep_ref.shape[0] // band
    scratch[...] = own_ref[...].astype(F32) + recv_ref[...].astype(F32)
    mine, away = bands(scal[Y], count, band), bands(1 - scal[Y], count, band)
    yoth_ref[...] = (keep_ref[1].astype(F32) + got_ref[1].astype(F32)).astype(BF16)
    yown_ref[...] = (keep_ref[0].astype(F32) + got_ref[0].astype(F32)).astype(BF16)
    cut_bands(scratch, mine, away, xkeep_ref, xsend_ref, band)


def fold_kernel(band, bit, scal, *refs):
    refs, (keep_out, send_out, scratch) = refs[:-3], refs[-3:]
    lead = scratch.shape[0]
    if len(refs) == 4:
        scratch[0] = refs[0][...].astype(F32) + refs[1][...].astype(F32)
        scratch[1] = refs[2][...].astype(F32) + refs[3][...].astype(F32)
    else:
        scratch[...] = refs[0][...].astype(F32) + refs[1][...].astype(F32)
    count = keep_out.shape[1] // band
    value = (scal[DP] // bit) % 2
    mine, away = bands(value, count, band), bands(1 - value, count, band)
    for part in range(lead):
        cut_bands(scratch.at[part], mine, away, keep_out.at[part], send_out.at[part], band)


def final_kernel(heads_width, scal, *refs):
    (ffn_one, attn_one, ffn_zero, attn_zero), outs = [refs[2 * i : 2 * i + 2] for i in range(4)], refs[8:]
    qkv_ref, out_ref, up_ref, down_ref = outs
    for layer, (keep_ref, recv_ref) in ((1, ffn_one), (0, ffn_zero)):
        up_ref[layer] = keep_ref[0].astype(F32) + recv_ref[0].astype(F32)
        down_ref[layer] = keep_ref[1].astype(F32) + recv_ref[1].astype(F32)
    for layer, (keep_ref, recv_ref) in ((1, attn_one), (0, attn_zero)):
        for part in range(2):
            total = keep_ref[part].astype(F32) + recv_ref[part].astype(F32)
            qkv_ref[layer, 2 * part] = total[:, 0:heads_width]
            if part == 0:
                qkv_ref[layer, 1] = total[:, heads_width : 2 * heads_width]
            else:
                out_ref[layer] = total[:, heads_width : 2 * heads_width].T


def pack_kernel(tensor_size, heads_width, scal, *refs):
    refs, out_ref = refs[:-1], refs[-1]
    out_ref[...] = jnp.zeros(out_ref.shape, F32)
    shard = scal[SHARD]
    for layer in range(LAYERS):
        one_ref, two_ref, heads_ref, units_ref = refs[4 * layer : 4 * layer + 4]
        base = layer * (6 + 2 * tensor_size)
        for row in range(3):
            out_ref[base + row] = one_ref[row : row + 1, :]
            out_ref[base + 3 + row] = two_ref[row : row + 1, :]
        for side in range(2):
            place = shard if side == 0 else shard + 2 - 4 * ((shard // 2) % 2)
            out_ref[base + 6 + place, :, 0:heads_width] = heads_ref[side, 0:1, :]
            out_ref[base + 6 + place, :, 256 : 256 + heads_width] = heads_ref[side, 1:2, :]
            out_ref[base + 6 + tensor_size + place] = units_ref[side : side + 1, :]
    base = LAYERS * (6 + 2 * tensor_size)
    for i, ref in enumerate(refs[4 * LAYERS :]):
        out_ref[base, :, 128 * i : 128 * (i + 1)] = ref[0:1, :]


def total_kernel(scal, in_ref, out_ref):
    devices = out_ref.shape[0]
    total = jnp.sum(in_ref[...].reshape(devices, -1, in_ref.shape[2]), axis=0, keepdims=True)
    out_ref[...] = jnp.broadcast_to(total, out_ref.shape)


def unpack_kernel(tensor_size, heads_width, count, scal, in_ref, hb_ref, ob_ref, gain_ref, shift_ref, ub_ref, db_ref, rms_ref):
    shard = scal[SHARD]
    for layer in range(LAYERS):
        base = layer * (6 + 2 * tensor_size)
        for k in range(2):
            gain_ref[layer, k : k + 1, :] = in_ref[base + 3 * k]
            shift_ref[layer, k : k + 1, :] = in_ref[base + 3 * k + 1]
        ob_ref[layer : layer + 1, :] = in_ref[base + 2]
        db_ref[layer : layer + 1, :] = in_ref[base + 5]
        heads = in_ref[base + 6 + shard]
        hb_ref[layer, 0:1, :] = heads[:, 0:heads_width]
        hb_ref[layer, 1:2, :] = heads[:, 256 : 256 + heads_width]
        ub_ref[layer : layer + 1, :] = in_ref[base + 6 + tensor_size + shard]
    base = LAYERS * (6 + 2 * tensor_size)
    row = jnp.sqrt(in_ref[base] * (1.0 / count))
    for layer in range(LAYERS):
        for k in range(3):
            i = 3 * layer + k
            rms_ref[layer : layer + 1, k : k + 1] = row[:, 128 * i : 128 * i + 1]


def dx_kernel(scal, self_ref, recv_ref, fac_ref, skip_ref, out_ref):
    grad = self_ref[...].astype(F32) + recv_ref[...].astype(F32)
    out_ref[...] = grad * fac_ref[...].astype(F32) + skip_ref[...]


def body(
    hidden,
    long_lengths,
    short_lengths,
    w_qkv,
    bias_qv,
    w_out,
    bias_out,
    ln_gain,
    ln_bias,
    w_up,
    bias_up,
    w_down,
    bias_down,
    cotangent,
):
    own_rows, width = hidden.shape
    rows = 2 * own_rows
    heads_width = w_qkv.shape[-1]
    units = w_up.shape[-1]
    dp_size, tensor_size = lax.axis_size("dp"), lax.axis_size("tensor")
    devices = dp_size * tensor_size
    count_model = float(own_rows * devices * width)
    dp_index, tensor_index = lax.axis_index("dp"), lax.axis_index("tensor")
    core_pairs = [(i, i ^ 1) for i in range(tensor_size)]
    x_pairs = [(i, i ^ 2) for i in range(tensor_size)]
    core_swap = lambda v: lax.ppermute(v, "tensor", core_pairs)
    x_swap = lambda v: lax.ppermute(v, "tensor", x_pairs)
    dp_swap = lambda v, bit: lax.ppermute(v, "dp", [(i, i ^ bit) for i in range(dp_size)])
    over_ranks = lambda top: lax.all_to_all(top, BOTH, 0, 0)

    scal = jnp.concatenate(
        [
            jnp.stack([tensor_index // 2, dp_index % 2, tensor_index % 2, dp_index, tensor_index]).astype(jnp.int32),
            long_lengths,
            short_lengths,
        ]
    )
    w_qkv = jnp.swapaxes(w_qkv, 2, 3)

    chain = [scal]

    def ordered(outs):
        small = min(outs, key=lambda a: a.size)
        chain[0] = lax.optimization_barrier((scal, small))[0]
        return outs

    def run(kernel, ins, outs, name, scratch=()):
        return ordered(
            pl.pallas_call(
                kernel,
                grid_spec=pltpu.PrefetchScalarGridSpec(
                    num_scalar_prefetch=1,
                    grid=(1,),
                    in_specs=[s for _, s in ins],
                    out_specs=[pl.BlockSpec(s, lambda i, t, n=len(s): (0,) * n) for s, _ in outs],
                    scratch_shapes=list(scratch),
                ),
                out_shape=[jax.ShapeDtypeStruct(s, d) for s, d in outs],
                name=name,
                cost_estimate=pl.CostEstimate(flops=0 if name in LIGHT else HEAVY, bytes_accessed=1, transcendentals=0),
                compiler_params=pltpu.CompilerParams(vmem_limit_bytes=VMEM_LIMIT),
            )(chain[0], *[array for array, _ in ins])
        )

    def flow(*args, **named):
        return ordered(stream(chain[0], *args, **named))

    def tie(value, token):
        return lax.optimization_barrier((value, token))[0]

    def settle(*arrived):
        chain[0] = lax.optimization_barrier((chain[0],) + arrived)[0]

    spec = pl.BlockSpec
    full = lambda a: (a, spec(a.shape, lambda i, s: (0,) * len(a.shape)))
    top_rows = lambda a, n: (a, spec((n,) + a.shape[1:], lambda i, s: (0,) * len(a.shape)))
    top_shape = (devices, 1, 128)
    top_store = Store(top_shape, F32)

    def weight_halves(l):
        return run(
            halves_kernel,
            [
                (w_qkv, spec((None, 3, heads_width, width // 2), lambda i, s: (l, 0, 0, s[Y]))),
                (w_out, spec((None, heads_width, width // 2), lambda i, s: (l, 0, s[Y]))),
                (w_up, spec((None, width // 2, units), lambda i, s: (l, s[Y], 0))),
                (w_down, spec((None, units // 2, width), lambda i, s: (l, s[Y], 0))),
            ],
            [((4, heads_width, width // 2), BF16), ((width // 2, units), BF16), ((units // 2, width), BF16)],
            "halves",
        )

    sends = weight_halves(0)
    vecs, small, top, input_sum = run(
        start_kernel,
        [full(a) for a in (hidden, bias_out, ln_gain, ln_bias, bias_down, bias_qv, bias_up)],
        [((LAYERS * VECS, width), F32), ((LAYERS * 3, units), F32), (top_shape, F32), ((1, 128), F32)],
        "start",
    )
    top = over_ranks(top)
    other_hidden = core_swap(hidden)
    small = x_swap(small)
    near = [[x_swap(sends[0]), x_swap(tie(sends[1], (top, small))), None], [None] * 3]
    far = [[dp_swap(tie(near[0][0], top), 1), None, None], [None] * 3]
    other_cotangent = core_swap(cotangent)

    saved = []
    square_terms = []
    states = None
    for l in range(LAYERS):
        last = l == LAYERS - 1
        first = l == 0
        attend_stores = lambda n: [
            per_side_out((n, 3, rows, heads_width), BF16),
            side_rows_out((n, rows, heads_width), F32, 0, 512 // 512),
            side_rows_out((n, 3, rows, rows), BF16, 1, 4),
            side_rows_out((n, rows, heads_width), F32, 0, 512 // 512),
            top_store,
        ]
        low_stores = [rows_out((rows, width), BF16, 2), rows_out((rows, width), BF16, 2)]
        own_loads = [whole_in(top), whole_in(vecs), layer_in(w_qkv, l)]
        scores = [pltpu.VMEM((rows, 128), BF16)] * 4
        if first:
            low_in, fac_in, *parts, own_top = flow(
                partial(attend_body, l, 2, (0,)),
                [pair_in(hidden, other_hidden, 2)] + own_loads,
                low_stores + attend_stores(1),
                "attend_own",
                scratch=scores,
            )
            next_sends = weight_halves(1)
            settle(near[0][1], other_cotangent)
            near[0][2] = x_swap(tie(sends[2], next_sends[0]))
            far[0][1] = dp_swap(tie(near[0][1], next_sends[0]), 1)
            *more, top = flow(
                partial(attend_body, l, 2, (1,)),
                [whole_in(low_in), whole_in(near[l][0]), whole_in(far[l][0]), whole_in(small), whole_in(own_top)],
                attend_stores(1),
                "attend_oth",
                scratch=scores,
            )
            qkv, ctx, soft, rinv = zip(parts, more)
        else:
            low_in, fac_in, *parts, top = flow(
                partial(attend_body, l, 2, (0, 1)),
                [rows_in(states, 2)] + own_loads + [whole_in(near[l][0]), whole_in(far[l][0]), whole_in(small)],
                low_stores + attend_stores(2),
                "attend",
                scratch=scores,
            )
            qkv, ctx, soft, rinv = [(v,) for v in parts]
        if first:
            top = over_ranks(tie(top, (near[0][2], far[0][1])))
            near[1][0] = x_swap(tie(next_sends[0], top))
            far[0][2] = dp_swap(tie(near[0][2], top), 1)
            window = (near[1][0], far[0][2])
        else:
            top = over_ranks(tie(top, (near[1][2], far[1][1])))
            far[1][2] = dp_swap(tie(near[1][2], top), 1)
            window = (far[1][2],)
        att_near, up_near, down_near = near[l]
        att_far, up_far, down_far = far[l]
        low_ctx, fac_ctx, *parts = flow(
            out_body,
            [whole_in(top), side_rows_in(ctx, 2), layer_in(w_out, l), whole_in(att_near), whole_in(att_far)],
            [sides_out((2, rows, heads_width), BF16, 2), sides_out((2, rows, heads_width), BF16, 2)] + [Store((own_rows, width), BF16)] * 2,
            "out_proj",
        )
        norm_stores = [rows_out((rows, width), F32, 4), rows_out((rows, width), BF16, 4), rows_out((rows, 128), F32, 4),
                       Store((2, 128), F32), top_store]
        middle, unit_one, inv_one, sums_one, top = flow(
            partial(norm_body, l, False, 4),
            [whole_in(vecs), pair_in(hidden, other_hidden, 4) if first else rows_in(states, 4), pair_in(*parts, 4),
             pair_in(*[core_swap(v) for v in parts[::-1]], 4)],
            norm_stores,
            "norm_one",
        )
        top = over_ranks(tie(top, window))
        low_mid, fac_mid, active, slope, top = flow(
            partial(up_body, l, 2),
            [whole_in(top), rows_in(middle, 2), whole_in(vecs), layer_in(w_up, l), whole_in(up_near), whole_in(up_far), whole_in(small)],
            [rows_out((rows, width), BF16, 2), rows_out((rows, width), BF16, 2), sides_out((2, rows, units), F32, 2),
             sides_out((2, rows, units), BF16, 2), top_store],
            "up_proj",
        )
        top = over_ranks(top)
        if first:
            near[1][1] = x_swap(tie(next_sends[1], top))
            far[1][0] = dp_swap(tie(near[1][0], top), 1)
        low_act, fac_act, *parts = flow(
            down_body,
            [whole_in(top), sides_in(active, 2), sides_in(slope, 2), layer_in(w_down, l), whole_in(down_near), whole_in(down_far)],
            [sides_out((2, rows, units), BF16, 2), sides_out((2, rows, units), BF16, 2)] + [Store((own_rows, width), BF16)] * 2,
            "down_proj",
        )
        square_terms += [input_sum, sums_one]
        keep = (low_in, fac_in, qkv, ctx, soft, rinv, low_ctx, fac_ctx, unit_one, inv_one, low_mid, fac_mid, low_act, fac_act)
        recvs = [core_swap(v) for v in parts[::-1]]
        if not last:
            states, unit_two, inv_two, sums_two, top = flow(
                partial(norm_body, l, True, 4),
                [whole_in(vecs), rows_in(middle, 4), pair_in(*parts, 4), pair_in(*recvs, 4)],
                norm_stores,
                "norm_two",
            )
            square_terms.append(sums_two)
            input_sum = sums_two[1:2]
            top = over_ranks(tie(top, (near[1][1], far[1][0])))
            near[1][2] = x_swap(tie(next_sends[2], top))
            far[1][1] = dp_swap(tie(near[1][1], top), 1)
            keep += (unit_two, inv_two)
        saved.append(keep)

    sums = [None] * LAYERS
    band = width // dp_size
    banded = band % 16 == 0

    half_width = width // 2

    def grad_group(kind, ins, columns, bit):
        cut = band * 2 if bit == 2 else band
        if not banded:
            stores = [per_side_out((2, width, columns), BF16)] * 2
            bit = None
        elif bit == 1:
            stores = [Store((width, columns), BF16)] * 2 + [per_side_out((2, half_width, columns), BF16)] * 2
        else:
            stores = [per_side_out((2, 2, half_width, columns), BF16)] * 2
        return flow(
            partial(grad_body, kind, bit, cut),
            [whole_in(a) for a in ins],
            stores,
            kind + "_grad",
            scratch=[pltpu.VMEM((width, columns), F32)],
        )

    def begin(group, token):
        own, oth, keep, send = group
        return own, x_swap(tie(oth, token)), keep, dp_swap(tie(send, token), 1)

    def second(pending):
        columns = pending[0].shape[1]
        return run(
            partial(second_kernel, band),
            [full(a) for a in pending],
            [((half_width, columns), BF16)] * 4,
            "second",
            scratch=[pltpu.VMEM((width, columns), F32)],
        )

    def crossed(outs, token):
        xkeep, xsend, yown, yoth = outs
        return xkeep, dp_swap(tie(xsend, token), 1), yown, x_swap(tie(yoth, token))

    def fold(ins, bit):
        remaining, columns = ins[0].shape[-2:]
        lead = 2 if len(ins) == 4 else ins[0].shape[0]
        return run(
            partial(fold_kernel, band, bit),
            [full(a) for a in ins],
            [((lead, remaining // 2, columns), BF16)] * 2,
            "fold",
            scratch=[pltpu.VMEM((lead, remaining, columns), F32)],
        )

    def sent(outs, bit, token):
        return outs[0], dp_swap(tie(outs[1], token), bit)

    count_rows = LAYERS * (6 + 2 * tensor_size) + 1
    packed_rows = -(-count_rows // devices) * devices
    chunk = packed_rows // devices

    def packed_sums():
        (packed,) = run(
            partial(pack_kernel, tensor_size, heads_width),
            [full(a) for l in range(LAYERS) for a in sums[l]] + [full(a) for a in square_terms],
            [((packed_rows, 1, width), F32)],
            "pack",
        )
        return over_ranks(packed.reshape(devices, chunk, width)).reshape(devices, chunk, width)

    def total_sums(packed):
        (totals,) = run(total_kernel, [full(packed)], [((devices, chunk, width), F32)], "total")
        return over_ranks(totals).reshape(packed_rows, 1, width)

    def unpacked_sums(totals):
        return run(
            partial(unpack_kernel, tensor_size, heads_width, count_model),
            [full(totals)],
            [(s, F32) for s in ((LAYERS, 2, heads_width), (LAYERS, width), (LAYERS, 2, width), (LAYERS, 2, width), (LAYERS, units),
                                (LAYERS, width), (LAYERS, 3))],
            "unpack",
        )

    def ffn_back(l, ins, extra):
        return flow(
            partial(ffn_back_body, l, l == LAYERS - 1, 2),
            ins + [sides_in(saved[l][13], 2), layer_in(w_down, l), whole_in(near[l][2]), whole_in(far[l][2]), layer_in(w_up, l),
                   whole_in(near[l][1]), whole_in(far[l][1])],
            [rows_out((rows, width), F32, 2), rows_out((rows, width), BF16, 2), sides_out((2, rows, units), BF16, 2),
             rows_out((rows, width), BF16, 2), Store((3, width), F32), Store((2, units), F32)] + extra,
            "ffn_back",
        )

    def attn_back(l, part, recv, dz_two, split):
        (low_in, fac_in, qkv, ctx, soft, rinv, low_ctx, fac_ctx, unit_one, inv_one, low_mid, fac_mid) = saved[l][:12]
        return flow(
            partial(attn_back_body, l, split, 2),
            [whole_in(vecs), rows_in(part, 2), rows_in(recv, 2, True), rows_in(fac_mid, 2), rows_in(dz_two, 2), rows_in(unit_one, 2),
             rows_in(inv_one, 2), layer_in(w_out, l), per_side_in((fac_ctx,)), per_side_in(rinv), per_side_in(ctx), per_side_in(qkv),
             per_side_in(soft), layer_in(w_qkv, l), whole_in(near[l][0]), whole_in(far[l][0])],
            [rows_out((rows, width), F32, 2), rows_out((rows, width), BF16, 2), per_side_out((2, rows, 3 * heads_width), BF16),
             Store((3, width), F32), Store((2, 2, heads_width), F32)]
            + ([Store((own_rows, width), BF16)] * 2 if split else [rows_out((rows, width), BF16, 2)]),
            "attn_back",
            scratch=[pltpu.VMEM((rows, width), F32)],
        )

    attn_columns = 2 * heads_width
    ins = [whole_in(vecs), rows_in(middle, 2), pair_in(*parts, 2), pair_in(*recvs, 2), pair_in(cotangent, other_cotangent, 2)]
    dz_two, df, du, part, sums_two, unit_sums, output, branch_sum = ffn_back(
        1, ins, [Store((own_rows, width), BF16), Store((1, 128), F32)]
    )
    square_terms.append(branch_sum)
    recv = core_swap(part)
    ffn_one = grad_group("ffn", [df, saved[1][12], saved[1][10], du], units, 1)
    if banded:
        ffn_one = begin(ffn_one, scal)
    dz_one, do, dqkv, sums_one, head_sums, part = attn_back(1, part, recv, dz_two, False)
    recv = core_swap(part)
    sums[1] = (sums_one, sums_two, head_sums, unit_sums)
    attn_one = grad_group("attn", [saved[1][0], dqkv, do, saved[1][6]], attn_columns, 1)
    if banded:
        attn_one = begin(attn_one, scal)
    ins = [whole_in(vecs), rows_in(part, 2), rows_in(recv, 2, True), rows_in(saved[1][1], 2), rows_in(dz_one, 2),
           rows_in(saved[0][14], 2), rows_in(saved[0][15], 2)]
    dz_two, df, du, part, sums_two, unit_sums = ffn_back(0, ins, [])
    recv = core_swap(part)
    if banded:
        ffn_one = second(ffn_one)
        ffn_one = crossed(ffn_one, scal)
    ffn_zero = grad_group("ffn", [df, saved[0][12], saved[0][10], du], units, 1)
    if banded:
        attn_one = second(attn_one)
        ffn_zero = begin(ffn_zero, attn_one[0])
        settle(ffn_one[1], ffn_one[3])
        ffn_one = fold(ffn_one, 2)
        ffn_one = sent(ffn_one, 2, scal)
    dz_one, do, dqkv, sums_one, head_sums, part, away = attn_back(0, part, recv, dz_two, True)
    recv = core_swap(away)
    sums[0] = (sums_one, sums_two, head_sums, unit_sums)
    attn_zero = grad_group("attn", [saved[0][0], dqkv, do, saved[0][6]], attn_columns, 1)
    (grad_hidden,) = run(
        dx_kernel,
        [full(part), full(recv), top_rows(saved[0][1], own_rows), top_rows(dz_one, own_rows)],
        [((own_rows, width), F32)],
        "dx",
    )
    if banded:
        attn_one = crossed(attn_one, grad_hidden)
        ffn_one = fold(ffn_one, 4)
        ffn_one = sent(ffn_one, 4, scal)
        ffn_zero = second(ffn_zero)
        ffn_zero = crossed(ffn_zero, scal)
        attn_one = fold(attn_one, 2)
        attn_zero = begin(attn_zero, attn_one[0])
    packed = packed_sums()
    if banded:
        attn_one = sent(attn_one, 2, ffn_one[1])
        ffn_zero = fold(ffn_zero, 2)
        ffn_zero = sent(ffn_zero, 2, scal)
        attn_one = fold(attn_one, 4)
        attn_one = sent(attn_one, 4, scal)
        attn_zero = second(attn_zero)
        attn_zero = crossed(attn_zero, scal)
        totals = total_sums(packed)
        ffn_zero = fold(ffn_zero, 4)
        ffn_zero = sent(ffn_zero, 4, scal)
        attn_zero = fold(attn_zero, 2)
        attn_zero = sent(attn_zero, 2, scal)
        attn_zero = fold(attn_zero, 4)
        attn_zero = sent(attn_zero, 4, scal)
        small_outs = unpacked_sums(totals)
        grad_qkv, grad_out, grad_up, grad_down = run(
            partial(final_kernel, heads_width),
            [full(a) for pair in (ffn_one, attn_one, ffn_zero, attn_zero) for a in pair],
            [((LAYERS, 3, band, heads_width), F32), ((LAYERS, heads_width, band), F32), ((LAYERS, band, units), F32),
             ((LAYERS, band, width), F32)],
            "final",
        )
    else:
        small_outs = unpacked_sums(total_sums(packed))
        totals = []
        for own, oth in (ffn_zero, ffn_one, attn_zero, attn_one):
            both = own.astype(F32) + x_swap(oth).astype(F32)
            totals.append(lax.psum_scatter(both, "dp", scatter_dimension=1, tiled=True))
        grad_up = jnp.stack([totals[0][0], totals[1][0]])
        grad_down = jnp.stack([totals[0][1], totals[1][1]])
        attn = jnp.stack(totals[2:])
        cut = lambda side, at: attn[:, side, :, at * heads_width : (at + 1) * heads_width]
        grad_qkv = jnp.stack([cut(0, 0), cut(0, 1), cut(1, 0)], 1)
        grad_out = jnp.swapaxes(cut(1, 1), 1, 2)

    head_bias, out_bias, gains, shifts, unit_bias, down_bias, rms = small_outs
    return (
        output,
        grad_hidden,
        grad_qkv,
        head_bias,
        grad_out,
        out_bias,
        gains,
        shifts,
        grad_up,
        unit_bias,
        jnp.swapaxes(grad_down, 1, 2),
        down_bias,
        rms,
    )


def solution(mesh):
    in_specs = (
        P(("dp", "tensor"), None),
        P("dp"),
        P("dp"),
        P(None, None, None, "tensor"),
        P(None, None, "tensor"),
        P(None, "tensor", None),
        P(),
        P(),
        P(),
        P(None, None, "tensor"),
        P(None, "tensor"),
        P(None, "tensor", None),
        P(),
        P(("dp", "tensor"), None),
    )
    out_specs = (
        P(("dp", "tensor"), None),
        P(("dp", "tensor"), None),
        P(None, None, "dp", "tensor"),
        P(None, None, "tensor"),
        P(None, "tensor", "dp"),
        P(),
        P(),
        P(),
        P(None, "dp", "tensor"),
        P(None, "tensor"),
        P(None, "tensor", "dp"),
        P(),
        P(),
    )
    return jax.shard_map(body, mesh=mesh, in_specs=in_specs, out_specs=out_specs, check_vma=False)
```

```python
from functools import partial

import jax
import jax.numpy as jnp
from jax import lax
from jax.experimental import pallas as pl
from jax.experimental.pallas import tpu as pltpu
from jax.sharding import PartitionSpec as P

HEAD_DIM = 64
LAYERS = 2
LONG_LEN = 512
SHORT_LEN = 128
LONG_DEV = 1
SHORT_DEV = 4

EPS = 1e-06
MASKED = -1e30
BOTH = ("dp", "tensor")
F32 = jnp.float32
BF16 = jnp.bfloat16
VMEM_LIMIT = 60 * 1024 * 1024
HEAVY = 10**15
LIGHT = {"halves", "norm_one", "norm_two", "up_proj", "second", "fold"}

X, Y, CORE, DP, SHARD, LENGTHS = range(6)


def nt(left, right):
    return lax.dot_general(left, right, (((1,), (1,)), ((), ())), preferred_element_type=F32)


def nn(left, right):
    return jnp.dot(left, right, preferred_element_type=F32)


def tn(left, right):
    return lax.dot_general(left, right, (((0,), (0,)), ((), ())), preferred_element_type=F32)


def merge(values):
    return values.reshape(values.shape[0] * values.shape[1], values.shape[2])


def bound_of(top_ref):
    return jnp.max(top_ref[...]) * 0.25 + EPS


def halves(scal, width):
    part = width // 2
    near = scal[Y]
    first = pl.ds(pl.multiple_of(near * part, part), part)
    second = pl.ds(pl.multiple_of((1 - near) * part, part), part)
    return first, second


class Load:
    def __init__(self, shape, dtype, pieces):
        self.shape, self.dtype, self.pieces = tuple(shape), dtype, pieces


class Store:
    def __init__(self, shape, dtype, pieces=((),)):
        self.shape, self.dtype, self.pieces = tuple(shape), dtype, pieces


def view(ref, index):
    return ref.at[index] if index else ref


class Arriving:
    def __init__(self, ref, copies):
        self.ref, self.copies, self.waited = ref, copies, set()

    def wait(self, piece):
        if piece not in self.waited:
            self.copies[piece].wait()
            self.waited.add(piece)
        return self.ref

    def all(self):
        for piece in range(len(self.copies)):
            self.wait(piece)
        return self.ref


class Leaving:
    def __init__(self, ref, copies):
        self.ref, self.copies, self.started = ref, copies, set()

    def flush(self, piece=0):
        self.copies[piece].start()
        self.started.add(piece)


def stream(scal, body, loads, stores, name, scratch=()):
    arrays = []

    def slot(array):
        for i, known in enumerate(arrays):
            if known is array:
                return i
        arrays.append(array)
        return len(arrays) - 1

    plan = [[(slot(a), src, dst) for a, src, dst in load.pieces] for load in loads]
    first_out = len(arrays)
    n_in = sum(len(p) for p in plan)
    n_out = sum(len(st.pieces) for st in stores)

    def kernel(scal_ref, *refs):
        sources = refs[: len(arrays)]
        targets = refs[first_out : first_out + len(stores)]
        at = first_out + len(stores)
        vin, at = refs[at : at + len(loads)], at + len(loads)
        vout, at = refs[at : at + len(stores)], at + len(stores)
        extra, (sem_in, sem_out) = refs[at:-2], refs[-2:]
        count = 0
        arriving = []
        for pieces, ref in zip(plan, vin):
            copies = []
            for i, src, dst in pieces:
                copies.append(pltpu.make_async_copy(view(sources[i], src), view(ref, dst), sem_in.at[count]))
                count += 1
            arriving.append(Arriving(ref, copies))
        for piece in range(max(len(p) for p in plan)):
            for a in arriving:
                if piece < len(a.copies):
                    a.copies[piece].start()
        count = 0
        leaving = []
        for st, ref, target in zip(stores, vout, targets):
            copies = []
            for index in st.pieces:
                copies.append(pltpu.make_async_copy(view(ref, index), view(target, index), sem_out.at[count]))
                count += 1
            leaving.append(Leaving(ref, copies))
        body(scal_ref, arriving, leaving, *extra)
        for a in arriving:
            a.all()
        for out in leaving:
            for piece, copy in enumerate(out.copies):
                if piece not in out.started:
                    copy.start()
        for out in leaving:
            for copy in out.copies:
                copy.wait()

    anywhere = pl.BlockSpec(memory_space=pl.ANY)
    return pl.pallas_call(
        kernel,
        in_specs=[pl.BlockSpec(memory_space=pltpu.SMEM)] + [anywhere] * first_out,
        out_specs=[anywhere] * len(stores),
        out_shape=[jax.ShapeDtypeStruct(st.shape, st.dtype) for st in stores],
        scratch_shapes=[pltpu.VMEM(x.shape, x.dtype) for x in list(loads) + list(stores)]
        + list(scratch)
        + [pltpu.SemaphoreType.DMA((n_in,)), pltpu.SemaphoreType.DMA((n_out,))],
        name=name,
        cost_estimate=pl.CostEstimate(flops=0 if name in LIGHT else HEAVY, bytes_accessed=1, transcendentals=0),
        compiler_params=pltpu.CompilerParams(vmem_limit_bytes=VMEM_LIMIT),
    )(scal, *arrays)


ALL = slice(None)


def span(i, size):
    return pl.ds(i * size, size)


def whole_in(a):
    return Load(a.shape, a.dtype, [(a, (), ())])


def layer_in(a, layer):
    return Load(a.shape[1:], a.dtype, [(a, (layer,), ())])


def rows_in(a, count, swap=False):
    size = a.shape[0] // count
    turn = count // 2 if swap else 0
    return Load(a.shape, a.dtype, [(a, (span((i + turn) % count, size),), (span(i, size),)) for i in range(count)])


def pair_in(mine, other, count):
    rows, width = mine.shape
    size = 2 * rows // count
    half = count // 2
    return Load(
        (2 * rows, width),
        mine.dtype,
        [((mine if i < half else other), (span(i % half, size),), (span(i, size),)) for i in range(count)],
    )


def sides_in(a, count):
    size = a.shape[1] // count
    return Load(a.shape, a.dtype, [(a, (ALL, span(i, size)), (ALL, span(i, size))) for i in range(count)])


def side_rows_in(parts, count):
    size = parts[0].shape[1] // count
    sources = [(a, i) for a in parts for i in range(a.shape[0])]
    return Load(
        (2,) + parts[0].shape[1:],
        parts[0].dtype,
        [(a, (s, span(i, size)), (side, span(i, size))) for i in range(count) for side, (a, s) in enumerate(sources)],
    )


def per_side_in(parts):
    pieces = [(a, (i,)) for a in parts for i in range(a.shape[0])]
    return Load((2,) + parts[0].shape[1:], parts[0].dtype, [(a, src, (i,)) for i, (a, src) in enumerate(pieces)])


def rows_out(shape, dtype, count):
    size = shape[0] // count
    return Store(shape, dtype, [(span(i, size),) for i in range(count)])


def sides_out(shape, dtype, count):
    size = shape[1] // count
    return Store(shape, dtype, [(ALL, span(i, size)) for i in range(count)])


def side_rows_out(shape, dtype, lead, count):
    size = shape[1 + lead] // count
    return Store(shape, dtype, [(s,) + (ALL,) * lead + (span(i, size),) for s in range(shape[0]) for i in range(count)])


def per_side_out(shape, dtype):
    return Store(shape, dtype, [(i,) for i in range(shape[0])])


B_OUT, GAIN_ONE, SHIFT_ONE, B_DOWN, GAIN_TWO, SHIFT_TWO, B_Q, B_V, B_UP, VECS = range(10)


def vec(ref, layer, row, width=None):
    at = layer * VECS + row
    return ref[at : at + 1, :] if width is None else ref[at : at + 1, 0:width]


def start_kernel(scal, hidden_ref, bout_ref, gain_ref, shift_ref, bdown_ref, bqv_ref, bup_ref, vecs_ref, small_ref, top_ref, sums_ref):
    heads_width = bqv_ref.shape[2]
    vecs_ref[...] = jnp.zeros(vecs_ref.shape, F32)
    small_ref[...] = jnp.zeros(small_ref.shape, F32)
    for layer in range(LAYERS):
        base = layer * VECS
        one = slice(layer, layer + 1)
        vecs_ref[base + B_OUT : base + B_OUT + 1, :] = bout_ref[one, :]
        vecs_ref[base + B_DOWN : base + B_DOWN + 1, :] = bdown_ref[one, :]
        vecs_ref[base + GAIN_ONE : base + GAIN_ONE + 1, :] = gain_ref[layer, 0:1, :]
        vecs_ref[base + GAIN_TWO : base + GAIN_TWO + 1, :] = gain_ref[layer, 1:2, :]
        vecs_ref[base + SHIFT_ONE : base + SHIFT_ONE + 1, :] = shift_ref[layer, 0:1, :]
        vecs_ref[base + SHIFT_TWO : base + SHIFT_TWO + 1, :] = shift_ref[layer, 1:2, :]
        for ref, at in ((vecs_ref, base + B_Q), (small_ref, 3 * layer)):
            ref[at : at + 1, 0:heads_width] = bqv_ref[layer, 0:1, :]
            ref[at + 1 : at + 2, 0:heads_width] = bqv_ref[layer, 1:2, :]
            ref[at + 2 : at + 3, :] = bup_ref[one, :]
    values = hidden_ref[...].astype(F32)
    top_ref[...] = jnp.full(top_ref.shape, jnp.max(jnp.abs(values)), F32)
    sums_ref[...] = jnp.full((1, 128), jnp.sum(values * values), F32)


def halves_kernel(scal, wqkv_ref, wout_ref, wup_ref, wdown_ref, att_ref, up_ref, down_ref):
    att_ref[0:3] = wqkv_ref[...]
    att_ref[3] = wout_ref[...]
    up_ref[...] = wup_ref[...]
    down_ref[...] = wdown_ref[...]


def row_ids(scal, slots, half_rows):
    rows = 2 * half_rows
    slot = slots + half_rows * scal[CORE]
    slot = jnp.where(slot >= rows, slot - rows, slot) + scal[X] * rows
    short = slot - LONG_DEV * LONG_LEN
    is_long = short < 0
    row = jnp.where(is_long, slot // LONG_LEN, LONG_DEV + short // SHORT_LEN)
    place = jnp.where(is_long, slot % LONG_LEN, short % SHORT_LEN)
    length = jnp.zeros_like(row)
    for i in range(LONG_DEV + SHORT_DEV):
        length = jnp.where(row == i, scal[LENGTHS + i], length)
    return row, jnp.where(place < length, 1, 0)


HEADS = ((0, 128, 0), (0, 128, 1), (128, 192, None))


def lane_mask(rows, which):
    lane = lax.broadcasted_iota(jnp.int32, (rows, 128), 1)
    return (lane < HEAD_DIM) if which == 0 else (lane >= HEAD_DIM)


def only_head(values, which):
    if which is None:
        return values
    return jnp.where(lane_mask(values.shape[0], which), values, jnp.zeros_like(values))


def largest(values):
    return jnp.max(jnp.abs(values))


def put_top(out, tops):
    top = tops[0]
    for other in tops[1:]:
        top = jnp.maximum(top, other)
    out.ref[...] = jnp.full(out.ref.shape, top, F32)
    out.flush()


def attend_body(layer, count, sides, scal, ins, outs, qcode_ref, kcode_ref, qlast_ref, klast_ref):
    if 0 in sides:
        x_in, top_in, vecs_in, own_in, ins = *ins[:4], ins[4:]
        low_out, fac_out, outs = *outs[:2], outs[2:]
        low_ref = low_out.ref
    else:
        low_in, ins = ins[0], ins[1:]
        low_ref = low_in.all()
    if 1 in sides:
        near_in, far_in, small_in, ins = *ins[:3], ins[3:]
    qkv_out, ctx_out, e_out, rinv_out, top_out = outs
    qkv_ref, ctx_ref, e_ref, rinv_ref = (o.ref for o in (qkv_out, ctx_out, e_out, rinv_out))
    rows, width = low_ref.shape
    heads_width = qkv_ref.shape[3]
    first, second = halves(scal, width)
    row, live = row_ids(scal, lax.broadcasted_iota(jnp.int32, (rows, 1), 0), rows // 2)
    code_lane = lax.broadcasted_iota(jnp.int32, (rows, 128), 1) % HEAD_DIM
    qcode_ref[...] = jnp.where(code_lane == row, 1.0, 0.0).astype(BF16)
    hidden_to = (code_lane < LONG_DEV + SHORT_DEV) & ((code_lane != row) | (live == 0))
    kcode_ref[...] = jnp.where(hidden_to, MASKED, 0.0).astype(BF16)
    qlast_ref[...] = qcode_ref[...]
    klast_ref[...] = kcode_ref[...]
    scale = HEAD_DIM ** (-0.5)
    if 0 in sides:
        bound = bound_of(top_in.all())
        size = rows // count
        vecs_ref = vecs_in.all()
        for i in range(count):
            place = slice(i * size, (i + 1) * size)
            tangent = jnp.tanh(x_in.wait(i)[place, :].astype(F32) * (1.0 / bound))
            low = (bound * tangent).astype(BF16)
            low_ref[place, :] = low
            low_out.flush(i)
            fac_out.ref[place, :] = (1.0 - tangent * tangent).astype(BF16)
            fac_out.flush(i)
            own_ref = own_in.all()
            for j in range(3):
                values = nt(low, own_ref[j])
                if j != 1:
                    values = values + vec(vecs_ref, layer, B_Q + j // 2, heads_width)
                qkv_ref[0, j, place, :] = (values * scale if j == 0 else values).astype(BF16)
        qkv_out.flush(0)
    chunk = 512
    chunks = rows // chunk
    tops = []
    for at, side in enumerate(sides):
        if side == 1:
            near_ref, far_ref, small_ref = near_in.all(), far_in.all(), small_in.all()
            for j in range(3):
                values = nt(low_ref[:, first], near_ref[j]) + nt(low_ref[:, second], far_ref[j])
                if j != 1:
                    row = 3 * layer + j // 2
                    values = values + small_ref[row : row + 1, 0:heads_width]
                qkv_ref[at, j] = (values * scale if j == 0 else values).astype(BF16)
            qkv_out.flush(at)
        qlast_ref[:, 0:HEAD_DIM] = qkv_ref[at, 0, :, 128:192]
        klast_ref[:, 0:HEAD_DIM] = qkv_ref[at, 1, :, 128:192]
        heads = []
        for h, (lo, hi, which) in enumerate(HEADS):
            if which is None:
                keys = klast_ref[...]
            else:
                keys = jnp.where(lane_mask(rows, which), qkv_ref[at, 1, :, lo:hi], kcode_ref[...])
            heads.append((h, lo, hi, which, keys, qkv_ref[at, 2, :, lo:hi]))
        left = lane_mask(chunk, 0)
        for i in range(chunks):
            place = slice(i * chunk, (i + 1) * chunk)
            done = []
            for h, lo, hi, which, keys, vals in heads:
                if which is None:
                    asking = qlast_ref[place, :]
                else:
                    asking = jnp.where(lane_mask(chunk, which), qkv_ref[at, 0, place, lo:hi], qcode_ref[place, :])
                scores = nt(asking, keys)
                weights = jnp.exp(scores - jnp.max(scores, axis=1, keepdims=True))
                inverse = 1.0 / jnp.sum(weights, axis=1, keepdims=True)
                low = weights.astype(BF16)
                e_ref[at, h, place, :] = low
                done.append((nn(low, vals) * inverse, inverse))
            pair = jnp.where(left, done[0][0], done[1][0])
            ctx_ref[at, place, 0:128] = pair
            ctx_ref[at, place, 128:192] = done[2][0]
            tops += [largest(pair), largest(done[2][0])]
            rinv_ref[at, place, 0:128] = jnp.where(left, done[0][1], done[1][1])
            rinv_ref[at, place, 128:192] = jnp.broadcast_to(done[2][1], (chunk, HEAD_DIM))
            for out in (e_out, ctx_out, rinv_out):
                out.flush(at * chunks + i)
    tops += [jnp.max(load.all()[...]) for load in ins]
    put_top(top_out, tops)


def out_body(scal, ins, outs):
    top_in, ctx_in, own_in, near_in, far_in = ins
    c_out, fac_out, *o_outs = outs
    bound = bound_of(top_in.all())
    size, width = o_outs[0].ref.shape
    for i, o_out in enumerate(o_outs):
        place = slice(i * size, (i + 1) * size)
        ctx_in.wait(2 * i)
        tangent = jnp.tanh(ctx_in.wait(2 * i + 1)[:, place, :] * (1.0 / bound))
        low = (bound * tangent).astype(BF16)
        c_out.ref[:, place, :] = low
        c_out.flush(i)
        fac_out.ref[:, place, :] = (1.0 - tangent * tangent).astype(BF16)
        fac_out.flush(i)
        own_ref = own_in.all()
        for part, load in zip(halves(scal, width), (near_in, far_in)):
            o_out.ref[:, part] = (nn(low[0], own_ref[:, part]) + nn(low[1], load.all()[3])).astype(BF16)
        o_out.flush()


def norm_forward(mixed, gain, shift):
    centred = mixed - jnp.mean(mixed, axis=1, keepdims=True)
    inverse = lax.rsqrt(jnp.mean(centred * centred, axis=1, keepdims=True) + EPS)
    unit = centred * inverse
    return unit * gain + shift, unit, inverse


def lane_fill(value):
    return jnp.full((1, 128), value, F32)


def norm_body(layer, second, count, scal, ins, outs):
    vecs_in, x_in, self_in, recv_in = ins
    h_out, unit_out, inv_out, sums_out, top_out = outs
    rows, width = h_out.ref.shape
    size = rows // count
    vecs_ref = vecs_in.all()
    bias = vec(vecs_ref, layer, B_DOWN if second else B_OUT)
    gain = vec(vecs_ref, layer, GAIN_TWO if second else GAIN_ONE)
    shift = vec(vecs_ref, layer, SHIFT_TWO if second else SHIFT_ONE)
    tops, branch_sum, result_sum = [], 0.0, 0.0
    for i in range(count):
        place = slice(i * size, (i + 1) * size)
        branch = self_in.wait(i)[place, :].astype(F32) + recv_in.wait(i)[place, :].astype(F32) + bias
        result, unit, inverse = norm_forward(x_in.wait(i)[place, :].astype(F32) + branch, gain, shift)
        h_out.ref[place, :] = result
        h_out.flush(i)
        unit_out.ref[place, :] = unit.astype(unit_out.ref.dtype)
        unit_out.flush(i)
        inv_out.ref[place, :] = jnp.broadcast_to(inverse, (size, 128))
        inv_out.flush(i)
        tops.append(largest(result))
        if i < count // 2:
            branch_sum = branch_sum + jnp.sum(branch * branch)
            result_sum = result_sum + jnp.sum(result * result)
    sums_out.ref[0:1, :] = lane_fill(branch_sum)
    sums_out.ref[1:2, :] = lane_fill(result_sum)
    sums_out.flush()
    put_top(top_out, tops)


def up_body(layer, count, scal, ins, outs):
    top_in, h_in, vecs_in, own_in, near_in, far_in, small_in = ins
    low_out, fac_out, g_out, slope_out, top_out = outs
    low_ref = low_out.ref
    rows, width = low_ref.shape
    size = rows // count
    bound = bound_of(top_in.all())
    first, second = halves(scal, width)
    tops = []
    for i in range(count):
        place = slice(i * size, (i + 1) * size)
        tangent = jnp.tanh(h_in.wait(i)[place, :] * (1.0 / bound))
        low = (bound * tangent).astype(BF16)
        low_ref[place, :] = low
        low_out.flush(i)
        fac_out.ref[place, :] = (1.0 - tangent * tangent).astype(BF16)
        fac_out.flush(i)
        for side in range(2):
            if side == 0:
                units = nn(low, own_in.all()[...]) + vec(vecs_in.all(), layer, B_UP)
            else:
                units = nn(low_ref[place, first], near_in.all()[...]) + nn(low_ref[place, second], far_in.all()[...])
                units = units + small_in.all()[3 * layer + 2 : 3 * layer + 3, :]
            area = 0.5 + 0.5 * lax.erf(units * (0.5**0.5))
            density = jnp.exp(-0.5 * units * units) * 0.3989422804014327
            active = units * area
            g_out.ref[side, place, :] = active
            slope_out.ref[side, place, :] = (area + units * density).astype(BF16)
            tops.append(largest(active))
        g_out.flush(i)
        slope_out.flush(i)
    put_top(top_out, tops)


def down_body(scal, ins, outs):
    top_in, g_in, slope_in, own_in, near_in, far_in = ins
    low_out, fac_out, *f_outs = outs
    low_ref = low_out.ref
    size = f_outs[0].ref.shape[0]
    bound = bound_of(top_in.all())
    first, second = halves(scal, low_ref.shape[2])
    for i, f_out in enumerate(f_outs):
        place = slice(i * size, (i + 1) * size)
        tangent = jnp.tanh(g_in.wait(i)[:, place, :] * (1.0 / bound))
        low_ref[:, place, :] = (bound * tangent).astype(BF16)
        low_out.flush(i)
        slope = slope_in.wait(i)[:, place, :].astype(F32)
        fac_out.ref[:, place, :] = ((1.0 - tangent * tangent) * slope).astype(BF16)
        fac_out.flush(i)
        f_out.ref[...] = (
            nn(low_ref[0, place, :], own_in.all()[...])
            + nn(low_ref[1, place, first], near_in.all()[...])
            + nn(low_ref[1, place, second], far_in.all()[...])
        ).astype(BF16)
        f_out.flush()


def norm_back(grad, unit, inverse, gain):
    scaled = grad * gain
    return (
        scaled
        - jnp.mean(scaled, axis=1, keepdims=True)
        - unit * jnp.mean(scaled * unit, axis=1, keepdims=True)
    ) * inverse


def column_sums(values):
    return jnp.sum(values, axis=0, keepdims=True)


def ffn_back_body(layer, last_layer, count, scal, ins, outs):
    vecs_in, ins = ins[0], ins[1:]
    if last_layer:
        (h_in, self_in, recv_in, cot_in), ins = ins[:4], ins[4:]
        result_out, fsum_out = outs[-2:]
    else:
        (self_in, recv_in, infac_in, skip_in, unit_in, inv_in), ins = ins[:6], ins[6:]
    fac_in, down_in, dnear_in, dfar_in, up_in, unear_in, ufar_in = ins
    dz_out, df_out, du_out, dh_out, sums_out, usum_out = outs[:6]
    rows, width = dz_out.ref.shape
    size = rows // count
    vecs_ref = vecs_in.all()
    gain = vec(vecs_ref, layer, GAIN_TWO)
    first, second = halves(scal, width)
    du_ref = du_out.ref
    totals = None
    unit_totals = None
    branch_sum = 0.0
    for i in range(count):
        place = slice(i * size, (i + 1) * size)
        mine = i < count // 2
        both = self_in.wait(i)[place, :].astype(F32) + recv_in.wait(i)[place, :].astype(F32)
        if last_layer:
            branch = both + vec(vecs_ref, layer, B_DOWN)
            result, unit, inverse = norm_forward(h_in.wait(i)[place, :] + branch, gain, vec(vecs_ref, layer, SHIFT_TWO))
            grad = cot_in.wait(i)[place, :].astype(F32)
            if mine:
                result_out.ref[place, :] = result.astype(BF16)
                result_out.flush(i)
                branch_sum = branch_sum + jnp.sum(branch * branch)
        else:
            grad = both * infac_in.wait(i)[place, :].astype(F32) + skip_in.wait(i)[place, :]
            unit = unit_in.wait(i)[place, :].astype(F32)
            inverse = inv_in.wait(i)[place, 0:1]
        mixed = norm_back(grad, unit, inverse, gain)
        low = mixed.astype(BF16)
        dz_out.ref[place, :] = mixed
        dz_out.flush(i)
        df_out.ref[place, :] = low
        df_out.flush(i)
        if mine:
            new = [column_sums(v) for v in (grad * unit, grad, low.astype(F32))]
            totals = new if totals is None else [a + b for a, b in zip(totals, new)]
        fac_ref = fac_in.wait(i)
        du_ref[0, place, :] = (nt(low, down_in.all()[...]) * fac_ref[0, place, :].astype(F32)).astype(BF16)
        for part, load in ((first, dnear_in), (second, dfar_in)):
            du_ref[1, place, part] = (nt(low, load.all()[...]) * fac_ref[1, place, part].astype(F32)).astype(BF16)
        du_out.flush(i)
        for part, load in ((first, unear_in), (second, ufar_in)):
            dh_out.ref[place, part] = (
                nt(du_ref[0, place, :], up_in.all()[part, :]) + nt(du_ref[1, place, :], load.all()[...])
            ).astype(BF16)
        dh_out.flush(i)
        new = [column_sums(du_ref[side, place, :].astype(F32)) for side in range(2)]
        unit_totals = new if unit_totals is None else [a + b for a, b in zip(unit_totals, new)]
    for row, values in enumerate(totals):
        sums_out.ref[row : row + 1, :] = values
    for row, values in enumerate(unit_totals):
        usum_out.ref[row : row + 1, :] = values
    if last_layer:
        fsum_out.ref[...] = lane_fill(branch_sum)


def attn_back_body(layer, split, count, scal, ins, outs, da_scratch):
    (vecs_in, self_in, recv_in, hfac_in, skip_in, unit_in, inv_in, wout_in, cfac_in, rinv_in, ctx_in, qkv_in, e_in, wqkv_in,
     near_in, far_in) = ins
    dz_out, do_out, d_out, sums_out, hsum_out, da_out = outs[:6]
    rows, width = dz_out.ref.shape
    heads_width = qkv_in.ref.shape[3]
    size = rows // count
    first, second = halves(scal, width)
    gain = vec(vecs_in.all(), layer, GAIN_ONE)
    totals = None
    for i in range(count):
        place = slice(i * size, (i + 1) * size)
        grad = self_in.wait(i)[place, :].astype(F32) + recv_in.wait(i)[place, :].astype(F32)
        grad = grad * hfac_in.wait(i)[place, :].astype(F32) + skip_in.wait(i)[place, :]
        unit = unit_in.wait(i)[place, :].astype(F32)
        mixed = norm_back(grad, unit, inv_in.wait(i)[place, 0:1], gain)
        low = mixed.astype(BF16)
        dz_out.ref[place, :] = mixed
        dz_out.flush(i)
        do_out.ref[place, :] = low
        do_out.flush(i)
        if i < count // 2:
            new = [column_sums(v) for v in (grad * unit, grad, low.astype(F32))]
            totals = new if totals is None else [a + b for a, b in zip(totals, new)]
    for row, values in enumerate(totals):
        sums_out.ref[row : row + 1, :] = values
    do_ref, d_ref = do_out.ref, d_out.ref
    scale = HEAD_DIM ** (-0.5)
    left = lane_mask(rows, 0)
    for side in range(2):
        if side == 0:
            grad_ctx = nt(do_ref[...], wout_in.all()[...])
        else:
            grad_ctx = nt(do_ref[:, first], near_in.all()[3]) + nt(do_ref[:, second], far_in.all()[3])
        grad_ctx = grad_ctx * cfac_in.wait(side)[side].astype(F32)
        low = (grad_ctx * rinv_in.wait(side)[side]).astype(BF16)
        product = low.astype(F32) * ctx_in.wait(side)[side]
        qkv_ref, e_ref = qkv_in.wait(side), e_in.wait(side)
        results = []
        for h, (lo, hi, which) in enumerate(HEADS):
            inner = jnp.sum(only_head(product[:, lo:hi], which), axis=1, keepdims=True)
            values = only_head(qkv_ref[side, 2, :, lo:hi], which)
            weights = e_ref[side, h]
            grad_weights = nt(low[:, lo:hi], values)
            grad_scores = (weights.astype(F32) * (grad_weights - inner)).astype(BF16)
            dq = nn(grad_scores, qkv_ref[side, 1, :, lo:hi]) * scale
            dk = tn(qkv_ref[side, 0, :, lo:hi], grad_scores).T
            dv = tn(low[:, lo:hi], weights).T
            results.append((dq, dk, dv))
        for j in range(3):
            pair = jnp.where(left, results[0][j], results[1][j]).astype(BF16)
            last = results[2][j].astype(BF16)
            d_ref[side, :, j * heads_width : j * heads_width + 128] = pair
            d_ref[side, :, j * heads_width + 128 : (j + 1) * heads_width] = last
            if j != 1:
                at = slice(j // 2, j // 2 + 1)
                hsum_out.ref[side, at, 0:128] = column_sums(pair.astype(F32))
                hsum_out.ref[side, at, 128:192] = column_sums(last.astype(F32))
        d_out.flush(side)
        if side == 0:
            da_scratch[...] = nn(d_ref[0], merge(wqkv_in.all()[...]))
    for i in range(2):
        place = slice(i * rows // 2, (i + 1) * rows // 2)
        for part, load in ((first, near_in), (second, far_in)):
            total = (da_scratch[place, part] + nn(d_ref[1, place, :], merge(load.ref[0:3]))).astype(BF16)
            if split:
                outs[5 + i].ref[:, part] = total
            else:
                da_out.ref[place, part] = total
        if split:
            outs[5 + i].flush()
        else:
            da_out.flush(i)


def bands(bit_value, count, band):
    return [pl.ds(pl.multiple_of((2 * k + bit_value) * band, band), band) for k in range(count)]


def cut_bands(scratch, mine, away, keep_ref, send_ref, band):
    for k, (take, give) in enumerate(zip(mine, away)):
        place = slice(k * band, (k + 1) * band)
        send_ref[place, :] = scratch[give, :].astype(BF16)
        keep_ref[place, :] = scratch[take, :].astype(BF16)


def grad_body(kind, bit, band, scal, ins, outs, scratch):
    if kind == "ffn":
        df_in, gq_in, hq_in, du_in = ins
        columns = hq_in.ref.shape[1]
        x_first = lambda side: tn(hq_in.all()[...], du_in.all()[side])

        def y_first(side, put):
            put(slice(None), tn(df_in.all()[...], gq_in.all()[side]))

    else:
        a_in, d_in, do_in, c_in = ins
        width = c_in.ref.shape[2]
        columns = 2 * width
        x_first = lambda side: tn(a_in.all()[...], d_in.all()[side, :, 0:columns])

        def y_first(side, put):
            put(slice(0, width), tn(a_in.all()[...], d_in.all()[side, :, columns : 3 * width]))
            put(slice(width, columns), tn(do_in.all()[...], c_in.all()[side]))

    if bit is None:
        for side, out in ((0, outs[0]), (1, outs[1])):

            def put(at, values):
                out.ref[1, :, at] = values.astype(BF16)

            out.ref[0] = x_first(side).astype(BF16)
            y_first(side, put)
        return

    def put(at, values):
        scratch[:, at] = values

    keep_out, send_out = outs[-2:]
    value = (scal[DP] // bit) % 2
    count = keep_out.ref.shape[-2] // band
    mine, away = bands(value, count, band), bands(1 - value, count, band)
    if len(outs) == 4:
        own_out, oth_out = outs[:2]
        for side, out in ((1, oth_out), (0, own_out)):
            out.ref[...] = x_first(side).astype(BF16)
            out.flush()
            y_first(side, put)
            cut_bands(scratch, mine, away, keep_out.ref.at[side], send_out.ref.at[side], band)
            send_out.flush(side)
            keep_out.flush(side)
        return
    for side in range(2):
        scratch[...] = x_first(side)
        cut_bands(scratch, mine, away, keep_out.ref.at[side, 0], send_out.ref.at[side, 0], band)
        y_first(side, put)
        cut_bands(scratch, mine, away, keep_out.ref.at[side, 1], send_out.ref.at[side, 1], band)
        send_out.flush(side)
        keep_out.flush(side)


def second_kernel(band, scal, own_ref, recv_ref, keep_ref, got_ref, xkeep_ref, xsend_ref, yown_ref, yoth_ref, scratch):
    count = xkeep_ref.shape[0] // band
    scratch[...] = own_ref[...].astype(F32) + recv_ref[...].astype(F32)
    mine, away = bands(scal[Y], count, band), bands(1 - scal[Y], count, band)
    yoth_ref[...] = (keep_ref[1].astype(F32) + got_ref[1].astype(F32)).astype(BF16)
    yown_ref[...] = (keep_ref[0].astype(F32) + got_ref[0].astype(F32)).astype(BF16)
    cut_bands(scratch, mine, away, xkeep_ref, xsend_ref, band)


def fold_kernel(band, bit, scal, *refs):
    refs, (keep_out, send_out, scratch) = refs[:-3], refs[-3:]
    lead = scratch.shape[0]
    if len(refs) == 4:
        scratch[0] = refs[0][...].astype(F32) + refs[1][...].astype(F32)
        scratch[1] = refs[2][...].astype(F32) + refs[3][...].astype(F32)
    else:
        scratch[...] = refs[0][...].astype(F32) + refs[1][...].astype(F32)
    count = keep_out.shape[1] // band
    value = (scal[DP] // bit) % 2
    mine, away = bands(value, count, band), bands(1 - value, count, band)
    for part in range(lead):
        cut_bands(scratch.at[part], mine, away, keep_out.at[part], send_out.at[part], band)


def final_kernel(heads_width, scal, *refs):
    (ffn_one, attn_one, ffn_zero, attn_zero), outs = [refs[2 * i : 2 * i + 2] for i in range(4)], refs[8:]
    qkv_ref, out_ref, up_ref, down_ref = outs
    for layer, (keep_ref, recv_ref) in ((1, ffn_one), (0, ffn_zero)):
        up_ref[layer] = keep_ref[0].astype(F32) + recv_ref[0].astype(F32)
        down_ref[layer] = keep_ref[1].astype(F32) + recv_ref[1].astype(F32)
    for layer, (keep_ref, recv_ref) in ((1, attn_one), (0, attn_zero)):
        for part in range(2):
            total = keep_ref[part].astype(F32) + recv_ref[part].astype(F32)
            qkv_ref[layer, 2 * part] = total[:, 0:heads_width]
            if part == 0:
                qkv_ref[layer, 1] = total[:, heads_width : 2 * heads_width]
            else:
                out_ref[layer] = total[:, heads_width : 2 * heads_width].T


def pack_kernel(tensor_size, heads_width, scal, *refs):
    refs, out_ref = refs[:-1], refs[-1]
    out_ref[...] = jnp.zeros(out_ref.shape, F32)
    shard = scal[SHARD]
    for layer in range(LAYERS):
        one_ref, two_ref, heads_ref, units_ref = refs[4 * layer : 4 * layer + 4]
        base = layer * (6 + 2 * tensor_size)
        for row in range(3):
            out_ref[base + row] = one_ref[row : row + 1, :]
            out_ref[base + 3 + row] = two_ref[row : row + 1, :]
        for side in range(2):
            place = shard if side == 0 else shard + 2 - 4 * ((shard // 2) % 2)
            out_ref[base + 6 + place, :, 0:heads_width] = heads_ref[side, 0:1, :]
            out_ref[base + 6 + place, :, 256 : 256 + heads_width] = heads_ref[side, 1:2, :]
            out_ref[base + 6 + tensor_size + place] = units_ref[side : side + 1, :]
    base = LAYERS * (6 + 2 * tensor_size)
    for i, ref in enumerate(refs[4 * LAYERS :]):
        out_ref[base, :, 128 * i : 128 * (i + 1)] = ref[0:1, :]


def total_kernel(scal, in_ref, out_ref):
    devices = out_ref.shape[0]
    total = jnp.sum(in_ref[...].reshape(devices, -1, in_ref.shape[2]), axis=0, keepdims=True)
    out_ref[...] = jnp.broadcast_to(total, out_ref.shape)


def unpack_kernel(tensor_size, heads_width, count, scal, in_ref, hb_ref, ob_ref, gain_ref, shift_ref, ub_ref, db_ref, rms_ref):
    shard = scal[SHARD]
    for layer in range(LAYERS):
        base = layer * (6 + 2 * tensor_size)
        for k in range(2):
            gain_ref[layer, k : k + 1, :] = in_ref[base + 3 * k]
            shift_ref[layer, k : k + 1, :] = in_ref[base + 3 * k + 1]
        ob_ref[layer : layer + 1, :] = in_ref[base + 2]
        db_ref[layer : layer + 1, :] = in_ref[base + 5]
        heads = in_ref[base + 6 + shard]
        hb_ref[layer, 0:1, :] = heads[:, 0:heads_width]
        hb_ref[layer, 1:2, :] = heads[:, 256 : 256 + heads_width]
        ub_ref[layer : layer + 1, :] = in_ref[base + 6 + tensor_size + shard]
    base = LAYERS * (6 + 2 * tensor_size)
    row = jnp.sqrt(in_ref[base] * (1.0 / count))
    for layer in range(LAYERS):
        for k in range(3):
            i = 3 * layer + k
            rms_ref[layer : layer + 1, k : k + 1] = row[:, 128 * i : 128 * i + 1]


def dx_kernel(scal, self_ref, recv_ref, fac_ref, skip_ref, out_ref):
    grad = self_ref[...].astype(F32) + recv_ref[...].astype(F32)
    out_ref[...] = grad * fac_ref[...].astype(F32) + skip_ref[...]


def body(
    hidden,
    long_lengths,
    short_lengths,
    w_qkv,
    bias_qv,
    w_out,
    bias_out,
    ln_gain,
    ln_bias,
    w_up,
    bias_up,
    w_down,
    bias_down,
    cotangent,
):
    own_rows, width = hidden.shape
    rows = 2 * own_rows
    heads_width = w_qkv.shape[-1]
    units = w_up.shape[-1]
    dp_size, tensor_size = lax.axis_size("dp"), lax.axis_size("tensor")
    devices = dp_size * tensor_size
    count_model = float(own_rows * devices * width)
    dp_index, tensor_index = lax.axis_index("dp"), lax.axis_index("tensor")
    core_pairs = [(i, i ^ 1) for i in range(tensor_size)]
    x_pairs = [(i, i ^ 2) for i in range(tensor_size)]
    core_swap = lambda v: lax.ppermute(v, "tensor", core_pairs)
    x_swap = lambda v: lax.ppermute(v, "tensor", x_pairs)
    dp_swap = lambda v, bit: lax.ppermute(v, "dp", [(i, i ^ bit) for i in range(dp_size)])
    over_ranks = lambda top: lax.all_to_all(top, BOTH, 0, 0)

    scal = jnp.concatenate(
        [
            jnp.stack([tensor_index // 2, dp_index % 2, tensor_index % 2, dp_index, tensor_index]).astype(jnp.int32),
            long_lengths,
            short_lengths,
        ]
    )
    w_qkv = jnp.swapaxes(w_qkv, 2, 3)

    chain = [scal]

    def ordered(outs):
        small = min(outs, key=lambda a: a.size)
        chain[0] = lax.optimization_barrier((scal, small))[0]
        return outs

    def run(kernel, ins, outs, name, scratch=()):
        return ordered(
            pl.pallas_call(
                kernel,
                grid_spec=pltpu.PrefetchScalarGridSpec(
                    num_scalar_prefetch=1,
                    grid=(1,),
                    in_specs=[s for _, s in ins],
                    out_specs=[pl.BlockSpec(s, lambda i, t, n=len(s): (0,) * n) for s, _ in outs],
                    scratch_shapes=list(scratch),
                ),
                out_shape=[jax.ShapeDtypeStruct(s, d) for s, d in outs],
                name=name,
                cost_estimate=pl.CostEstimate(flops=0 if name in LIGHT else HEAVY, bytes_accessed=1, transcendentals=0),
                compiler_params=pltpu.CompilerParams(vmem_limit_bytes=VMEM_LIMIT),
            )(chain[0], *[array for array, _ in ins])
        )

    def flow(*args, **named):
        return ordered(stream(chain[0], *args, **named))

    def tie(value, token):
        return lax.optimization_barrier((value, token))[0]

    def settle(*arrived):
        chain[0] = lax.optimization_barrier((chain[0],) + arrived)[0]

    spec = pl.BlockSpec
    full = lambda a: (a, spec(a.shape, lambda i, s: (0,) * len(a.shape)))
    top_rows = lambda a, n: (a, spec((n,) + a.shape[1:], lambda i, s: (0,) * len(a.shape)))
    top_shape = (devices, 1, 128)
    top_store = Store(top_shape, F32)

    def weight_halves(l):
        return run(
            halves_kernel,
            [
                (w_qkv, spec((None, 3, heads_width, width // 2), lambda i, s: (l, 0, 0, s[Y]))),
                (w_out, spec((None, heads_width, width // 2), lambda i, s: (l, 0, s[Y]))),
                (w_up, spec((None, width // 2, units), lambda i, s: (l, s[Y], 0))),
                (w_down, spec((None, units // 2, width), lambda i, s: (l, s[Y], 0))),
            ],
            [((4, heads_width, width // 2), BF16), ((width // 2, units), BF16), ((units // 2, width), BF16)],
            "halves",
        )

    sends = weight_halves(0)
    vecs, small, top, input_sum = run(
        start_kernel,
        [full(a) for a in (hidden, bias_out, ln_gain, ln_bias, bias_down, bias_qv, bias_up)],
        [((LAYERS * VECS, width), F32), ((LAYERS * 3, units), F32), (top_shape, F32), ((1, 128), F32)],
        "start",
    )
    top = over_ranks(top)
    other_hidden = core_swap(hidden)
    small = x_swap(small)
    near = [[x_swap(sends[0]), x_swap(tie(sends[1], (top, small))), None], [None] * 3]
    far = [[dp_swap(tie(near[0][0], top), 1), None, None], [None] * 3]
    other_cotangent = core_swap(cotangent)

    saved = []
    square_terms = []
    states = None
    for l in range(LAYERS):
        last = l == LAYERS - 1
        first = l == 0
        attend_stores = lambda n: [
            per_side_out((n, 3, rows, heads_width), BF16),
            side_rows_out((n, rows, heads_width), F32, 0, 512 // 512),
            side_rows_out((n, 3, rows, rows), BF16, 1, 4),
            side_rows_out((n, rows, heads_width), F32, 0, 512 // 512),
            top_store,
        ]
        low_stores = [rows_out((rows, width), BF16, 2), rows_out((rows, width), BF16, 2)]
        own_loads = [whole_in(top), whole_in(vecs), layer_in(w_qkv, l)]
        scores = [pltpu.VMEM((rows, 128), BF16)] * 4
        if first:
            low_in, fac_in, *parts, own_top = flow(
                partial(attend_body, l, 2, (0,)),
                [pair_in(hidden, other_hidden, 2)] + own_loads,
                low_stores + attend_stores(1),
                "attend_own",
                scratch=scores,
            )
            next_sends = weight_halves(1)
            settle(near[0][1], other_cotangent)
            near[0][2] = x_swap(tie(sends[2], next_sends[0]))
            far[0][1] = dp_swap(tie(near[0][1], next_sends[0]), 1)
            *more, top = flow(
                partial(attend_body, l, 2, (1,)),
                [whole_in(low_in), whole_in(near[l][0]), whole_in(far[l][0]), whole_in(small), whole_in(own_top)],
                attend_stores(1),
                "attend_oth",
                scratch=scores,
            )
            qkv, ctx, soft, rinv = zip(parts, more)
        else:
            low_in, fac_in, *parts, top = flow(
                partial(attend_body, l, 2, (0, 1)),
                [rows_in(states, 2)] + own_loads + [whole_in(near[l][0]), whole_in(far[l][0]), whole_in(small)],
                low_stores + attend_stores(2),
                "attend",
                scratch=scores,
            )
            qkv, ctx, soft, rinv = [(v,) for v in parts]
        if first:
            top = over_ranks(tie(top, (near[0][2], far[0][1])))
            near[1][0] = x_swap(tie(next_sends[0], top))
            far[0][2] = dp_swap(tie(near[0][2], top), 1)
            window = (near[1][0], far[0][2])
        else:
            top = over_ranks(tie(top, (near[1][2], far[1][1])))
            far[1][2] = dp_swap(tie(near[1][2], top), 1)
            window = (far[1][2],)
        att_near, up_near, down_near = near[l]
        att_far, up_far, down_far = far[l]
        low_ctx, fac_ctx, *parts = flow(
            out_body,
            [whole_in(top), side_rows_in(ctx, 2), layer_in(w_out, l), whole_in(att_near), whole_in(att_far)],
            [sides_out((2, rows, heads_width), BF16, 2), sides_out((2, rows, heads_width), BF16, 2)] + [Store((own_rows, width), BF16)] * 2,
            "out_proj",
        )
        norm_stores = [rows_out((rows, width), F32, 4), rows_out((rows, width), BF16, 4), rows_out((rows, 128), F32, 4),
                       Store((2, 128), F32), top_store]
        middle, unit_one, inv_one, sums_one, top = flow(
            partial(norm_body, l, False, 4),
            [whole_in(vecs), pair_in(hidden, other_hidden, 4) if first else rows_in(states, 4), pair_in(*parts, 4),
             pair_in(*[core_swap(v) for v in parts[::-1]], 4)],
            norm_stores,
            "norm_one",
        )
        top = over_ranks(tie(top, window))
        low_mid, fac_mid, active, slope, top = flow(
            partial(up_body, l, 2),
            [whole_in(top), rows_in(middle, 2), whole_in(vecs), layer_in(w_up, l), whole_in(up_near), whole_in(up_far), whole_in(small)],
            [rows_out((rows, width), BF16, 2), rows_out((rows, width), BF16, 2), sides_out((2, rows, units), F32, 2),
             sides_out((2, rows, units), BF16, 2), top_store],
            "up_proj",
        )
        top = over_ranks(top)
        if first:
            near[1][1] = x_swap(tie(next_sends[1], top))
            far[1][0] = dp_swap(tie(near[1][0], top), 1)
        low_act, fac_act, *parts = flow(
            down_body,
            [whole_in(top), sides_in(active, 2), sides_in(slope, 2), layer_in(w_down, l), whole_in(down_near), whole_in(down_far)],
            [sides_out((2, rows, units), BF16, 2), sides_out((2, rows, units), BF16, 2)] + [Store((own_rows, width), BF16)] * 2,
            "down_proj",
        )
        square_terms += [input_sum, sums_one]
        keep = (low_in, fac_in, qkv, ctx, soft, rinv, low_ctx, fac_ctx, unit_one, inv_one, low_mid, fac_mid, low_act, fac_act)
        recvs = [core_swap(v) for v in parts[::-1]]
        if not last:
            states, unit_two, inv_two, sums_two, top = flow(
                partial(norm_body, l, True, 4),
                [whole_in(vecs), rows_in(middle, 4), pair_in(*parts, 4), pair_in(*recvs, 4)],
                norm_stores,
                "norm_two",
            )
            square_terms.append(sums_two)
            input_sum = sums_two[1:2]
            top = over_ranks(tie(top, (near[1][1], far[1][0])))
            near[1][2] = x_swap(tie(next_sends[2], top))
            far[1][1] = dp_swap(tie(near[1][1], top), 1)
            keep += (unit_two, inv_two)
        saved.append(keep)

    sums = [None] * LAYERS
    band = width // dp_size
    banded = band % 16 == 0

    half_width = width // 2

    def grad_group(kind, ins, columns, bit):
        cut = band * 2 if bit == 2 else band
        if not banded:
            stores = [per_side_out((2, width, columns), BF16)] * 2
            bit = None
        elif bit == 1:
            stores = [Store((width, columns), BF16)] * 2 + [per_side_out((2, half_width, columns), BF16)] * 2
        else:
            stores = [per_side_out((2, 2, half_width, columns), BF16)] * 2
        return flow(
            partial(grad_body, kind, bit, cut),
            [whole_in(a) for a in ins],
            stores,
            kind + "_grad",
            scratch=[pltpu.VMEM((width, columns), F32)],
        )

    def begin(group, token):
        own, oth, keep, send = group
        return own, x_swap(tie(oth, token)), keep, dp_swap(tie(send, token), 1)

    def second(pending):
        columns = pending[0].shape[1]
        return run(
            partial(second_kernel, band),
            [full(a) for a in pending],
            [((half_width, columns), BF16)] * 4,
            "second",
            scratch=[pltpu.VMEM((width, columns), F32)],
        )

    def crossed(outs, token):
        xkeep, xsend, yown, yoth = outs
        return xkeep, dp_swap(tie(xsend, token), 1), yown, x_swap(tie(yoth, token))

    def fold(ins, bit):
        remaining, columns = ins[0].shape[-2:]
        lead = 2 if len(ins) == 4 else ins[0].shape[0]
        return run(
            partial(fold_kernel, band, bit),
            [full(a) for a in ins],
            [((lead, remaining // 2, columns), BF16)] * 2,
            "fold",
            scratch=[pltpu.VMEM((lead, remaining, columns), F32)],
        )

    def sent(outs, bit, token):
        return outs[0], dp_swap(tie(outs[1], token), bit)

    count_rows = LAYERS * (6 + 2 * tensor_size) + 1
    packed_rows = -(-count_rows // devices) * devices
    chunk = packed_rows // devices

    def packed_sums():
        (packed,) = run(
            partial(pack_kernel, tensor_size, heads_width),
            [full(a) for l in range(LAYERS) for a in sums[l]] + [full(a) for a in square_terms],
            [((packed_rows, 1, width), F32)],
            "pack",
        )
        return over_ranks(packed.reshape(devices, chunk, width)).reshape(devices, chunk, width)

    def total_sums(packed):
        (totals,) = run(total_kernel, [full(packed)], [((devices, chunk, width), F32)], "total")
        return over_ranks(totals).reshape(packed_rows, 1, width)

    def unpacked_sums(totals):
        return run(
            partial(unpack_kernel, tensor_size, heads_width, count_model),
            [full(totals)],
            [(s, F32) for s in ((LAYERS, 2, heads_width), (LAYERS, width), (LAYERS, 2, width), (LAYERS, 2, width), (LAYERS, units),
                                (LAYERS, width), (LAYERS, 3))],
            "unpack",
        )

    def ffn_back(l, ins, extra):
        return flow(
            partial(ffn_back_body, l, l == LAYERS - 1, 2),
            ins + [sides_in(saved[l][13], 2), layer_in(w_down, l), whole_in(near[l][2]), whole_in(far[l][2]), layer_in(w_up, l),
                   whole_in(near[l][1]), whole_in(far[l][1])],
            [rows_out((rows, width), F32, 2), rows_out((rows, width), BF16, 2), sides_out((2, rows, units), BF16, 2),
             rows_out((rows, width), BF16, 2), Store((3, width), F32), Store((2, units), F32)] + extra,
            "ffn_back",
        )

    def attn_back(l, part, recv, dz_two, split):
        (low_in, fac_in, qkv, ctx, soft, rinv, low_ctx, fac_ctx, unit_one, inv_one, low_mid, fac_mid) = saved[l][:12]
        return flow(
            partial(attn_back_body, l, split, 2),
            [whole_in(vecs), rows_in(part, 2), rows_in(recv, 2, True), rows_in(fac_mid, 2), rows_in(dz_two, 2), rows_in(unit_one, 2),
             rows_in(inv_one, 2), layer_in(w_out, l), per_side_in((fac_ctx,)), per_side_in(rinv), per_side_in(ctx), per_side_in(qkv),
             per_side_in(soft), layer_in(w_qkv, l), whole_in(near[l][0]), whole_in(far[l][0])],
            [rows_out((rows, width), F32, 2), rows_out((rows, width), BF16, 2), per_side_out((2, rows, 3 * heads_width), BF16),
             Store((3, width), F32), Store((2, 2, heads_width), F32)]
            + ([Store((own_rows, width), BF16)] * 2 if split else [rows_out((rows, width), BF16, 2)]),
            "attn_back",
            scratch=[pltpu.VMEM((rows, width), F32)],
        )

    attn_columns = 2 * heads_width
    ins = [whole_in(vecs), rows_in(middle, 2), pair_in(*parts, 2), pair_in(*recvs, 2), pair_in(cotangent, other_cotangent, 2)]
    dz_two, df, du, part, sums_two, unit_sums, output, branch_sum = ffn_back(
        1, ins, [Store((own_rows, width), BF16), Store((1, 128), F32)]
    )
    square_terms.append(branch_sum)
    recv = core_swap(part)
    ffn_one = grad_group("ffn", [df, saved[1][12], saved[1][10], du], units, 1)
    if banded:
        ffn_one = begin(ffn_one, scal)
    dz_one, do, dqkv, sums_one, head_sums, part = attn_back(1, part, recv, dz_two, False)
    recv = core_swap(part)
    sums[1] = (sums_one, sums_two, head_sums, unit_sums)
    attn_one = grad_group("attn", [saved[1][0], dqkv, do, saved[1][6]], attn_columns, 1)
    if banded:
        attn_one = begin(attn_one, scal)
    ins = [whole_in(vecs), rows_in(part, 2), rows_in(recv, 2, True), rows_in(saved[1][1], 2), rows_in(dz_one, 2),
           rows_in(saved[0][14], 2), rows_in(saved[0][15], 2)]
    dz_two, df, du, part, sums_two, unit_sums = ffn_back(0, ins, [])
    recv = core_swap(part)
    if banded:
        ffn_one = second(ffn_one)
        ffn_one = crossed(ffn_one, scal)
    ffn_zero = grad_group("ffn", [df, saved[0][12], saved[0][10], du], units, 1)
    if banded:
        attn_one = second(attn_one)
        ffn_zero = begin(ffn_zero, attn_one[0])
        settle(ffn_one[1], ffn_one[3])
        ffn_one = fold(ffn_one, 2)
        ffn_one = sent(ffn_one, 2, scal)
    dz_one, do, dqkv, sums_one, head_sums, part, away = attn_back(0, part, recv, dz_two, True)
    recv = core_swap(away)
    sums[0] = (sums_one, sums_two, head_sums, unit_sums)
    attn_zero = grad_group("attn", [saved[0][0], dqkv, do, saved[0][6]], attn_columns, 1)
    (grad_hidden,) = run(
        dx_kernel,
        [full(part), full(recv), top_rows(saved[0][1], own_rows), top_rows(dz_one, own_rows)],
        [((own_rows, width), F32)],
        "dx",
    )
    if banded:
        attn_one = crossed(attn_one, grad_hidden)
        ffn_one = fold(ffn_one, 4)
        ffn_one = sent(ffn_one, 4, scal)
        ffn_zero = second(ffn_zero)
        ffn_zero = crossed(ffn_zero, scal)
        attn_one = fold(attn_one, 2)
        attn_zero = begin(attn_zero, attn_one[0])
    packed = packed_sums()
    if banded:
        attn_one = sent(attn_one, 2, ffn_one[1])
        ffn_zero = fold(ffn_zero, 2)
        ffn_zero = sent(ffn_zero, 2, scal)
        attn_one = fold(attn_one, 4)
        attn_one = sent(attn_one, 4, scal)
        totals = total_sums(packed)
        attn_zero = second(attn_zero)
        attn_zero = crossed(attn_zero, scal)
        ffn_zero = fold(ffn_zero, 4)
        ffn_zero = sent(ffn_zero, 4, scal)
        attn_zero = fold(attn_zero, 2)
        attn_zero = sent(attn_zero, 2, scal)
        small_outs = unpacked_sums(totals)
        attn_zero = fold(attn_zero, 4)
        attn_zero = sent(attn_zero, 4, scal)
        grad_qkv, grad_out, grad_up, grad_down = run(
            partial(final_kernel, heads_width),
            [full(a) for pair in (ffn_one, attn_one, ffn_zero, attn_zero) for a in pair],
            [((LAYERS, 3, band, heads_width), F32), ((LAYERS, heads_width, band), F32), ((LAYERS, band, units), F32),
             ((LAYERS, band, width), F32)],
            "final",
        )
    else:
        small_outs = unpacked_sums(total_sums(packed))
        totals = []
        for own, oth in (ffn_zero, ffn_one, attn_zero, attn_one):
            both = own.astype(F32) + x_swap(oth).astype(F32)
            totals.append(lax.psum_scatter(both, "dp", scatter_dimension=1, tiled=True))
        grad_up = jnp.stack([totals[0][0], totals[1][0]])
        grad_down = jnp.stack([totals[0][1], totals[1][1]])
        attn = jnp.stack(totals[2:])
        cut = lambda side, at: attn[:, side, :, at * heads_width : (at + 1) * heads_width]
        grad_qkv = jnp.stack([cut(0, 0), cut(0, 1), cut(1, 0)], 1)
        grad_out = jnp.swapaxes(cut(1, 1), 1, 2)

    head_bias, out_bias, gains, shifts, unit_bias, down_bias, rms = small_outs
    return (
        output,
        grad_hidden,
        grad_qkv,
        head_bias,
        grad_out,
        out_bias,
        gains,
        shifts,
        grad_up,
        unit_bias,
        jnp.swapaxes(grad_down, 1, 2),
        down_bias,
        rms,
    )


def solution(mesh):
    in_specs = (
        P(("dp", "tensor"), None),
        P("dp"),
        P("dp"),
        P(None, None, None, "tensor"),
        P(None, None, "tensor"),
        P(None, "tensor", None),
        P(),
        P(),
        P(),
        P(None, None, "tensor"),
        P(None, "tensor"),
        P(None, "tensor", None),
        P(),
        P(("dp", "tensor"), None),
    )
    out_specs = (
        P(("dp", "tensor"), None),
        P(("dp", "tensor"), None),
        P(None, None, "dp", "tensor"),
        P(None, None, "tensor"),
        P(None, "tensor", "dp"),
        P(),
        P(),
        P(),
        P(None, "dp", "tensor"),
        P(None, "tensor"),
        P(None, "tensor", "dp"),
        P(),
        P(),
    )
    return jax.shard_map(body, mesh=mesh, in_specs=in_specs, out_specs=out_specs, check_vma=False)
```

```python
from functools import partial

import jax
import jax.numpy as jnp
from jax import lax
from jax.experimental import pallas as pl
from jax.experimental.pallas import tpu as pltpu
from jax.sharding import PartitionSpec as P

HEAD_DIM = 64
LAYERS = 2
LONG_LEN = 512
SHORT_LEN = 128
LONG_DEV = 1
SHORT_DEV = 4

EPS = 1e-06
MASKED = -1e30
BOTH = ("dp", "tensor")
F32 = jnp.float32
BF16 = jnp.bfloat16
VMEM_LIMIT = 60 * 1024 * 1024
HEAVY = 10**15
LIGHT = {"halves", "norm_one", "norm_two", "up_proj", "second", "fold"}

X, Y, CORE, DP, SHARD, LENGTHS = range(6)


def nt(left, right):
    return lax.dot_general(left, right, (((1,), (1,)), ((), ())), preferred_element_type=F32)


def nn(left, right):
    return jnp.dot(left, right, preferred_element_type=F32)


def tn(left, right):
    return lax.dot_general(left, right, (((0,), (0,)), ((), ())), preferred_element_type=F32)


def merge(values):
    return values.reshape(values.shape[0] * values.shape[1], values.shape[2])


def bound_of(top_ref):
    return jnp.max(top_ref[...]) * 0.25 + EPS


def halves(scal, width):
    part = width // 2
    near = scal[Y]
    first = pl.ds(pl.multiple_of(near * part, part), part)
    second = pl.ds(pl.multiple_of((1 - near) * part, part), part)
    return first, second


class Load:
    def __init__(self, shape, dtype, pieces):
        self.shape, self.dtype, self.pieces = tuple(shape), dtype, pieces


class Store:
    def __init__(self, shape, dtype, pieces=((),)):
        self.shape, self.dtype, self.pieces = tuple(shape), dtype, pieces


def view(ref, index):
    return ref.at[index] if index else ref


class Arriving:
    def __init__(self, ref, copies):
        self.ref, self.copies, self.waited = ref, copies, set()

    def wait(self, piece):
        if piece not in self.waited:
            self.copies[piece].wait()
            self.waited.add(piece)
        return self.ref

    def all(self):
        for piece in range(len(self.copies)):
            self.wait(piece)
        return self.ref


class Leaving:
    def __init__(self, ref, copies):
        self.ref, self.copies, self.started = ref, copies, set()

    def flush(self, piece=0):
        self.copies[piece].start()
        self.started.add(piece)


def stream(scal, body, loads, stores, name, scratch=()):
    arrays = []

    def slot(array):
        for i, known in enumerate(arrays):
            if known is array:
                return i
        arrays.append(array)
        return len(arrays) - 1

    plan = [[(slot(a), src, dst) for a, src, dst in load.pieces] for load in loads]
    first_out = len(arrays)
    n_in = sum(len(p) for p in plan)
    n_out = sum(len(st.pieces) for st in stores)

    def kernel(scal_ref, *refs):
        sources = refs[: len(arrays)]
        targets = refs[first_out : first_out + len(stores)]
        at = first_out + len(stores)
        vin, at = refs[at : at + len(loads)], at + len(loads)
        vout, at = refs[at : at + len(stores)], at + len(stores)
        extra, (sem_in, sem_out) = refs[at:-2], refs[-2:]
        count = 0
        arriving = []
        for pieces, ref in zip(plan, vin):
            copies = []
            for i, src, dst in pieces:
                copies.append(pltpu.make_async_copy(view(sources[i], src), view(ref, dst), sem_in.at[count]))
                count += 1
            arriving.append(Arriving(ref, copies))
        for piece in range(max(len(p) for p in plan)):
            for a in arriving:
                if piece < len(a.copies):
                    a.copies[piece].start()
        count = 0
        leaving = []
        for st, ref, target in zip(stores, vout, targets):
            copies = []
            for index in st.pieces:
                copies.append(pltpu.make_async_copy(view(ref, index), view(target, index), sem_out.at[count]))
                count += 1
            leaving.append(Leaving(ref, copies))
        body(scal_ref, arriving, leaving, *extra)
        for a in arriving:
            a.all()
        for out in leaving:
            for piece, copy in enumerate(out.copies):
                if piece not in out.started:
                    copy.start()
        for out in leaving:
            for copy in out.copies:
                copy.wait()

    anywhere = pl.BlockSpec(memory_space=pl.ANY)
    return pl.pallas_call(
        kernel,
        in_specs=[pl.BlockSpec(memory_space=pltpu.SMEM)] + [anywhere] * first_out,
        out_specs=[anywhere] * len(stores),
        out_shape=[jax.ShapeDtypeStruct(st.shape, st.dtype) for st in stores],
        scratch_shapes=[pltpu.VMEM(x.shape, x.dtype) for x in list(loads) + list(stores)]
        + list(scratch)
        + [pltpu.SemaphoreType.DMA((n_in,)), pltpu.SemaphoreType.DMA((n_out,))],
        name=name,
        cost_estimate=pl.CostEstimate(flops=0 if name in LIGHT else HEAVY, bytes_accessed=1, transcendentals=0),
        compiler_params=pltpu.CompilerParams(vmem_limit_bytes=VMEM_LIMIT),
    )(scal, *arrays)


ALL = slice(None)


def span(i, size):
    return pl.ds(i * size, size)


def whole_in(a):
    return Load(a.shape, a.dtype, [(a, (), ())])


def layer_in(a, layer):
    return Load(a.shape[1:], a.dtype, [(a, (layer,), ())])


def rows_in(a, count, swap=False):
    size = a.shape[0] // count
    turn = count // 2 if swap else 0
    return Load(a.shape, a.dtype, [(a, (span((i + turn) % count, size),), (span(i, size),)) for i in range(count)])


def pair_in(mine, other, count):
    rows, width = mine.shape
    size = 2 * rows // count
    half = count // 2
    return Load(
        (2 * rows, width),
        mine.dtype,
        [((mine if i < half else other), (span(i % half, size),), (span(i, size),)) for i in range(count)],
    )


def sides_in(a, count):
    size = a.shape[1] // count
    return Load(a.shape, a.dtype, [(a, (ALL, span(i, size)), (ALL, span(i, size))) for i in range(count)])


def side_rows_in(parts, count):
    size = parts[0].shape[1] // count
    sources = [(a, i) for a in parts for i in range(a.shape[0])]
    return Load(
        (2,) + parts[0].shape[1:],
        parts[0].dtype,
        [(a, (s, span(i, size)), (side, span(i, size))) for i in range(count) for side, (a, s) in enumerate(sources)],
    )


def per_side_in(parts):
    pieces = [(a, (i,)) for a in parts for i in range(a.shape[0])]
    return Load((2,) + parts[0].shape[1:], parts[0].dtype, [(a, src, (i,)) for i, (a, src) in enumerate(pieces)])


def rows_out(shape, dtype, count):
    size = shape[0] // count
    return Store(shape, dtype, [(span(i, size),) for i in range(count)])


def sides_out(shape, dtype, count):
    size = shape[1] // count
    return Store(shape, dtype, [(ALL, span(i, size)) for i in range(count)])


def side_rows_out(shape, dtype, lead, count):
    size = shape[1 + lead] // count
    return Store(shape, dtype, [(s,) + (ALL,) * lead + (span(i, size),) for s in range(shape[0]) for i in range(count)])


def per_side_out(shape, dtype):
    return Store(shape, dtype, [(i,) for i in range(shape[0])])


B_OUT, GAIN_ONE, SHIFT_ONE, B_DOWN, GAIN_TWO, SHIFT_TWO, B_Q, B_V, B_UP, VECS = range(10)


def vec(ref, layer, row, width=None):
    at = layer * VECS + row
    return ref[at : at + 1, :] if width is None else ref[at : at + 1, 0:width]


def start_kernel(scal, hidden_ref, bout_ref, gain_ref, shift_ref, bdown_ref, bqv_ref, bup_ref, vecs_ref, small_ref, top_ref, sums_ref):
    heads_width = bqv_ref.shape[2]
    vecs_ref[...] = jnp.zeros(vecs_ref.shape, F32)
    small_ref[...] = jnp.zeros(small_ref.shape, F32)
    for layer in range(LAYERS):
        base = layer * VECS
        one = slice(layer, layer + 1)
        vecs_ref[base + B_OUT : base + B_OUT + 1, :] = bout_ref[one, :]
        vecs_ref[base + B_DOWN : base + B_DOWN + 1, :] = bdown_ref[one, :]
        vecs_ref[base + GAIN_ONE : base + GAIN_ONE + 1, :] = gain_ref[layer, 0:1, :]
        vecs_ref[base + GAIN_TWO : base + GAIN_TWO + 1, :] = gain_ref[layer, 1:2, :]
        vecs_ref[base + SHIFT_ONE : base + SHIFT_ONE + 1, :] = shift_ref[layer, 0:1, :]
        vecs_ref[base + SHIFT_TWO : base + SHIFT_TWO + 1, :] = shift_ref[layer, 1:2, :]
        for ref, at in ((vecs_ref, base + B_Q), (small_ref, 3 * layer)):
            ref[at : at + 1, 0:heads_width] = bqv_ref[layer, 0:1, :]
            ref[at + 1 : at + 2, 0:heads_width] = bqv_ref[layer, 1:2, :]
            ref[at + 2 : at + 3, :] = bup_ref[one, :]
    values = hidden_ref[...].astype(F32)
    top_ref[...] = jnp.full(top_ref.shape, jnp.max(jnp.abs(values)), F32)
    sums_ref[...] = jnp.full((1, 128), jnp.sum(values * values), F32)


def halves_kernel(scal, wqkv_ref, wout_ref, wup_ref, wdown_ref, att_ref, up_ref, down_ref):
    att_ref[0:3] = wqkv_ref[...]
    att_ref[3] = wout_ref[...]
    up_ref[...] = wup_ref[...]
    down_ref[...] = wdown_ref[...]


def row_ids(scal, slots, half_rows):
    rows = 2 * half_rows
    slot = slots + half_rows * scal[CORE]
    slot = jnp.where(slot >= rows, slot - rows, slot) + scal[X] * rows
    short = slot - LONG_DEV * LONG_LEN
    is_long = short < 0
    row = jnp.where(is_long, slot // LONG_LEN, LONG_DEV + short // SHORT_LEN)
    place = jnp.where(is_long, slot % LONG_LEN, short % SHORT_LEN)
    length = jnp.zeros_like(row)
    for i in range(LONG_DEV + SHORT_DEV):
        length = jnp.where(row == i, scal[LENGTHS + i], length)
    return row, jnp.where(place < length, 1, 0)


HEADS = ((0, 128, 0), (0, 128, 1), (128, 192, None))


def lane_mask(rows, which):
    lane = lax.broadcasted_iota(jnp.int32, (rows, 128), 1)
    return (lane < HEAD_DIM) if which == 0 else (lane >= HEAD_DIM)


def only_head(values, which):
    if which is None:
        return values
    return jnp.where(lane_mask(values.shape[0], which), values, jnp.zeros_like(values))


def largest(values):
    return jnp.max(jnp.abs(values))


def put_top(out, tops):
    top = tops[0]
    for other in tops[1:]:
        top = jnp.maximum(top, other)
    out.ref[...] = jnp.full(out.ref.shape, top, F32)
    out.flush()


def attend_body(layer, count, sides, scal, ins, outs, qcode_ref, kcode_ref, qlast_ref, klast_ref):
    if 0 in sides:
        x_in, top_in, vecs_in, own_in, ins = *ins[:4], ins[4:]
        low_out, fac_out, outs = *outs[:2], outs[2:]
        low_ref = low_out.ref
    else:
        low_in, ins = ins[0], ins[1:]
        low_ref = low_in.all()
    if 1 in sides:
        near_in, far_in, small_in, ins = *ins[:3], ins[3:]
    qkv_out, ctx_out, e_out, rinv_out, top_out = outs
    qkv_ref, ctx_ref, e_ref, rinv_ref = (o.ref for o in (qkv_out, ctx_out, e_out, rinv_out))
    rows, width = low_ref.shape
    heads_width = qkv_ref.shape[3]
    first, second = halves(scal, width)
    row, live = row_ids(scal, lax.broadcasted_iota(jnp.int32, (rows, 1), 0), rows // 2)
    code_lane = lax.broadcasted_iota(jnp.int32, (rows, 128), 1) % HEAD_DIM
    qcode_ref[...] = jnp.where(code_lane == row, 1.0, 0.0).astype(BF16)
    hidden_to = (code_lane < LONG_DEV + SHORT_DEV) & ((code_lane != row) | (live == 0))
    kcode_ref[...] = jnp.where(hidden_to, MASKED, 0.0).astype(BF16)
    qlast_ref[...] = qcode_ref[...]
    klast_ref[...] = kcode_ref[...]
    scale = HEAD_DIM ** (-0.5)
    if 0 in sides:
        bound = bound_of(top_in.all())
        size = rows // count
        vecs_ref = vecs_in.all()
        for i in range(count):
            place = slice(i * size, (i + 1) * size)
            tangent = jnp.tanh(x_in.wait(i)[place, :].astype(F32) * (1.0 / bound))
            low = (bound * tangent).astype(BF16)
            low_ref[place, :] = low
            low_out.flush(i)
            fac_out.ref[place, :] = (1.0 - tangent * tangent).astype(BF16)
            fac_out.flush(i)
            own_ref = own_in.all()
            for j in range(3):
                values = nt(low, own_ref[j])
                if j != 1:
                    values = values + vec(vecs_ref, layer, B_Q + j // 2, heads_width)
                qkv_ref[0, j, place, :] = (values * scale if j == 0 else values).astype(BF16)
        qkv_out.flush(0)
    chunk = 512
    chunks = rows // chunk
    tops = []
    for at, side in enumerate(sides):
        if side == 1:
            near_ref, far_ref, small_ref = near_in.all(), far_in.all(), small_in.all()
            for j in range(3):
                values = nt(low_ref[:, first], near_ref[j]) + nt(low_ref[:, second], far_ref[j])
                if j != 1:
                    row = 3 * layer + j // 2
                    values = values + small_ref[row : row + 1, 0:heads_width]
                qkv_ref[at, j] = (values * scale if j == 0 else values).astype(BF16)
            qkv_out.flush(at)
        qlast_ref[:, 0:HEAD_DIM] = qkv_ref[at, 0, :, 128:192]
        klast_ref[:, 0:HEAD_DIM] = qkv_ref[at, 1, :, 128:192]
        heads = []
        for h, (lo, hi, which) in enumerate(HEADS):
            if which is None:
                keys = klast_ref[...]
            else:
                keys = jnp.where(lane_mask(rows, which), qkv_ref[at, 1, :, lo:hi], kcode_ref[...])
            heads.append((h, lo, hi, which, keys, qkv_ref[at, 2, :, lo:hi]))
        left = lane_mask(chunk, 0)
        for i in range(chunks):
            place = slice(i * chunk, (i + 1) * chunk)
            done = []
            for h, lo, hi, which, keys, vals in heads:
                if which is None:
                    asking = qlast_ref[place, :]
                else:
                    asking = jnp.where(lane_mask(chunk, which), qkv_ref[at, 0, place, lo:hi], qcode_ref[place, :])
                scores = nt(asking, keys)
                weights = jnp.exp(scores - jnp.max(scores, axis=1, keepdims=True))
                inverse = 1.0 / jnp.sum(weights, axis=1, keepdims=True)
                low = weights.astype(BF16)
                e_ref[at, h, place, :] = low
                done.append((nn(low, vals) * inverse, inverse))
            pair = jnp.where(left, done[0][0], done[1][0])
            ctx_ref[at, place, 0:128] = pair
            ctx_ref[at, place, 128:192] = done[2][0]
            tops += [largest(pair), largest(done[2][0])]
            rinv_ref[at, place, 0:128] = jnp.where(left, done[0][1], done[1][1])
            rinv_ref[at, place, 128:192] = jnp.broadcast_to(done[2][1], (chunk, HEAD_DIM))
            for out in (e_out, ctx_out, rinv_out):
                out.flush(at * chunks + i)
    tops += [jnp.max(load.all()[...]) for load in ins]
    put_top(top_out, tops)


def out_body(scal, ins, outs):
    top_in, ctx_in, own_in, near_in, far_in = ins
    c_out, fac_out, *o_outs = outs
    bound = bound_of(top_in.all())
    size, width = o_outs[0].ref.shape
    for i, o_out in enumerate(o_outs):
        place = slice(i * size, (i + 1) * size)
        ctx_in.wait(2 * i)
        tangent = jnp.tanh(ctx_in.wait(2 * i + 1)[:, place, :] * (1.0 / bound))
        low = (bound * tangent).astype(BF16)
        c_out.ref[:, place, :] = low
        c_out.flush(i)
        fac_out.ref[:, place, :] = (1.0 - tangent * tangent).astype(BF16)
        fac_out.flush(i)
        own_ref = own_in.all()
        for part, load in zip(halves(scal, width), (near_in, far_in)):
            o_out.ref[:, part] = (nn(low[0], own_ref[:, part]) + nn(low[1], load.all()[3])).astype(BF16)
        o_out.flush()


def norm_forward(mixed, gain, shift):
    centred = mixed - jnp.mean(mixed, axis=1, keepdims=True)
    inverse = lax.rsqrt(jnp.mean(centred * centred, axis=1, keepdims=True) + EPS)
    unit = centred * inverse
    return unit * gain + shift, unit, inverse


def lane_fill(value):
    return jnp.full((1, 128), value, F32)


def norm_body(layer, second, count, scal, ins, outs):
    vecs_in, x_in, self_in, recv_in = ins
    h_out, unit_out, inv_out, sums_out, top_out = outs
    rows, width = h_out.ref.shape
    size = rows // count
    vecs_ref = vecs_in.all()
    bias = vec(vecs_ref, layer, B_DOWN if second else B_OUT)
    gain = vec(vecs_ref, layer, GAIN_TWO if second else GAIN_ONE)
    shift = vec(vecs_ref, layer, SHIFT_TWO if second else SHIFT_ONE)
    tops, branch_sum, result_sum = [], 0.0, 0.0
    for i in range(count):
        place = slice(i * size, (i + 1) * size)
        branch = self_in.wait(i)[place, :].astype(F32) + recv_in.wait(i)[place, :].astype(F32) + bias
        result, unit, inverse = norm_forward(x_in.wait(i)[place, :].astype(F32) + branch, gain, shift)
        h_out.ref[place, :] = result
        h_out.flush(i)
        unit_out.ref[place, :] = unit.astype(unit_out.ref.dtype)
        unit_out.flush(i)
        inv_out.ref[place, :] = jnp.broadcast_to(inverse, (size, 128))
        inv_out.flush(i)
        tops.append(largest(result))
        if i < count // 2:
            branch_sum = branch_sum + jnp.sum(branch * branch)
            result_sum = result_sum + jnp.sum(result * result)
    sums_out.ref[0:1, :] = lane_fill(branch_sum)
    sums_out.ref[1:2, :] = lane_fill(result_sum)
    sums_out.flush()
    put_top(top_out, tops)


def up_body(layer, count, scal, ins, outs):
    top_in, h_in, vecs_in, own_in, near_in, far_in, small_in = ins
    low_out, fac_out, g_out, slope_out, top_out = outs
    low_ref = low_out.ref
    rows, width = low_ref.shape
    size = rows // count
    bound = bound_of(top_in.all())
    first, second = halves(scal, width)
    tops = []
    for i in range(count):
        place = slice(i * size, (i + 1) * size)
        tangent = jnp.tanh(h_in.wait(i)[place, :] * (1.0 / bound))
        low = (bound * tangent).astype(BF16)
        low_ref[place, :] = low
        low_out.flush(i)
        fac_out.ref[place, :] = (1.0 - tangent * tangent).astype(BF16)
        fac_out.flush(i)
        for side in range(2):
            if side == 0:
                units = nn(low, own_in.all()[...]) + vec(vecs_in.all(), layer, B_UP)
            else:
                units = nn(low_ref[place, first], near_in.all()[...]) + nn(low_ref[place, second], far_in.all()[...])
                units = units + small_in.all()[3 * layer + 2 : 3 * layer + 3, :]
            area = 0.5 + 0.5 * lax.erf(units * (0.5**0.5))
            density = jnp.exp(-0.5 * units * units) * 0.3989422804014327
            active = units * area
            g_out.ref[side, place, :] = active
            slope_out.ref[side, place, :] = (area + units * density).astype(BF16)
            tops.append(largest(active))
        g_out.flush(i)
        slope_out.flush(i)
    put_top(top_out, tops)


def down_body(scal, ins, outs):
    top_in, g_in, slope_in, own_in, near_in, far_in = ins
    low_out, fac_out, *f_outs = outs
    low_ref = low_out.ref
    size = f_outs[0].ref.shape[0]
    bound = bound_of(top_in.all())
    first, second = halves(scal, low_ref.shape[2])
    for i, f_out in enumerate(f_outs):
        place = slice(i * size, (i + 1) * size)
        tangent = jnp.tanh(g_in.wait(i)[:, place, :] * (1.0 / bound))
        low_ref[:, place, :] = (bound * tangent).astype(BF16)
        low_out.flush(i)
        slope = slope_in.wait(i)[:, place, :].astype(F32)
        fac_out.ref[:, place, :] = ((1.0 - tangent * tangent) * slope).astype(BF16)
        fac_out.flush(i)
        f_out.ref[...] = (
            nn(low_ref[0, place, :], own_in.all()[...])
            + nn(low_ref[1, place, first], near_in.all()[...])
            + nn(low_ref[1, place, second], far_in.all()[...])
        ).astype(BF16)
        f_out.flush()


def norm_back(grad, unit, inverse, gain):
    scaled = grad * gain
    return (
        scaled
        - jnp.mean(scaled, axis=1, keepdims=True)
        - unit * jnp.mean(scaled * unit, axis=1, keepdims=True)
    ) * inverse


def column_sums(values):
    return jnp.sum(values, axis=0, keepdims=True)


def ffn_back_body(layer, last_layer, count, scal, ins, outs):
    vecs_in, ins = ins[0], ins[1:]
    if last_layer:
        (h_in, self_in, recv_in, cot_in), ins = ins[:4], ins[4:]
        result_out, fsum_out = outs[-2:]
    else:
        (self_in, recv_in, infac_in, skip_in, unit_in, inv_in), ins = ins[:6], ins[6:]
    fac_in, down_in, dnear_in, dfar_in, up_in, unear_in, ufar_in = ins
    dz_out, df_out, du_out, dh_out, sums_out, usum_out = outs[:6]
    rows, width = dz_out.ref.shape
    size = rows // count
    vecs_ref = vecs_in.all()
    gain = vec(vecs_ref, layer, GAIN_TWO)
    first, second = halves(scal, width)
    du_ref = du_out.ref
    totals = None
    unit_totals = None
    branch_sum = 0.0
    for i in range(count):
        place = slice(i * size, (i + 1) * size)
        mine = i < count // 2
        both = self_in.wait(i)[place, :].astype(F32) + recv_in.wait(i)[place, :].astype(F32)
        if last_layer:
            branch = both + vec(vecs_ref, layer, B_DOWN)
            result, unit, inverse = norm_forward(h_in.wait(i)[place, :] + branch, gain, vec(vecs_ref, layer, SHIFT_TWO))
            grad = cot_in.wait(i)[place, :].astype(F32)
            if mine:
                result_out.ref[place, :] = result.astype(BF16)
                result_out.flush(i)
                branch_sum = branch_sum + jnp.sum(branch * branch)
        else:
            grad = both * infac_in.wait(i)[place, :].astype(F32) + skip_in.wait(i)[place, :]
            unit = unit_in.wait(i)[place, :].astype(F32)
            inverse = inv_in.wait(i)[place, 0:1]
        mixed = norm_back(grad, unit, inverse, gain)
        low = mixed.astype(BF16)
        dz_out.ref[place, :] = mixed
        dz_out.flush(i)
        df_out.ref[place, :] = low
        df_out.flush(i)
        if mine:
            new = [column_sums(v) for v in (grad * unit, grad, low.astype(F32))]
            totals = new if totals is None else [a + b for a, b in zip(totals, new)]
        fac_ref = fac_in.wait(i)
        du_ref[0, place, :] = (nt(low, down_in.all()[...]) * fac_ref[0, place, :].astype(F32)).astype(BF16)
        for part, load in ((first, dnear_in), (second, dfar_in)):
            du_ref[1, place, part] = (nt(low, load.all()[...]) * fac_ref[1, place, part].astype(F32)).astype(BF16)
        du_out.flush(i)
        for part, load in ((first, unear_in), (second, ufar_in)):
            dh_out.ref[place, part] = (
                nt(du_ref[0, place, :], up_in.all()[part, :]) + nt(du_ref[1, place, :], load.all()[...])
            ).astype(BF16)
        dh_out.flush(i)
        new = [column_sums(du_ref[side, place, :].astype(F32)) for side in range(2)]
        unit_totals = new if unit_totals is None else [a + b for a, b in zip(unit_totals, new)]
    for row, values in enumerate(totals):
        sums_out.ref[row : row + 1, :] = values
    for row, values in enumerate(unit_totals):
        usum_out.ref[row : row + 1, :] = values
    if last_layer:
        fsum_out.ref[...] = lane_fill(branch_sum)


def attn_back_body(layer, split, count, scal, ins, outs, da_scratch):
    (vecs_in, self_in, recv_in, hfac_in, skip_in, unit_in, inv_in, wout_in, cfac_in, rinv_in, ctx_in, qkv_in, e_in, wqkv_in,
     near_in, far_in) = ins
    dz_out, do_out, d_out, sums_out, hsum_out, da_out = outs[:6]
    rows, width = dz_out.ref.shape
    heads_width = qkv_in.ref.shape[3]
    size = rows // count
    first, second = halves(scal, width)
    gain = vec(vecs_in.all(), layer, GAIN_ONE)
    totals = None
    for i in range(count):
        place = slice(i * size, (i + 1) * size)
        grad = self_in.wait(i)[place, :].astype(F32) + recv_in.wait(i)[place, :].astype(F32)
        grad = grad * hfac_in.wait(i)[place, :].astype(F32) + skip_in.wait(i)[place, :]
        unit = unit_in.wait(i)[place, :].astype(F32)
        mixed = norm_back(grad, unit, inv_in.wait(i)[place, 0:1], gain)
        low = mixed.astype(BF16)
        dz_out.ref[place, :] = mixed
        dz_out.flush(i)
        do_out.ref[place, :] = low
        do_out.flush(i)
        if i < count // 2:
            new = [column_sums(v) for v in (grad * unit, grad, low.astype(F32))]
            totals = new if totals is None else [a + b for a, b in zip(totals, new)]
    for row, values in enumerate(totals):
        sums_out.ref[row : row + 1, :] = values
    do_ref, d_ref = do_out.ref, d_out.ref
    scale = HEAD_DIM ** (-0.5)
    left = lane_mask(rows, 0)
    for side in range(2):
        if side == 0:
            grad_ctx = nt(do_ref[...], wout_in.all()[...])
        else:
            grad_ctx = nt(do_ref[:, first], near_in.all()[3]) + nt(do_ref[:, second], far_in.all()[3])
        grad_ctx = grad_ctx * cfac_in.wait(side)[side].astype(F32)
        low = (grad_ctx * rinv_in.wait(side)[side]).astype(BF16)
        product = low.astype(F32) * ctx_in.wait(side)[side]
        qkv_ref, e_ref = qkv_in.wait(side), e_in.wait(side)
        results = []
        for h, (lo, hi, which) in enumerate(HEADS):
            inner = jnp.sum(only_head(product[:, lo:hi], which), axis=1, keepdims=True)
            values = only_head(qkv_ref[side, 2, :, lo:hi], which)
            weights = e_ref[side, h]
            grad_weights = nt(low[:, lo:hi], values)
            grad_scores = (weights.astype(F32) * (grad_weights - inner)).astype(BF16)
            dq = nn(grad_scores, qkv_ref[side, 1, :, lo:hi]) * scale
            dk = tn(qkv_ref[side, 0, :, lo:hi], grad_scores).T
            dv = tn(low[:, lo:hi], weights).T
            results.append((dq, dk, dv))
        for j in range(3):
            pair = jnp.where(left, results[0][j], results[1][j]).astype(BF16)
            last = results[2][j].astype(BF16)
            d_ref[side, :, j * heads_width : j * heads_width + 128] = pair
            d_ref[side, :, j * heads_width + 128 : (j + 1) * heads_width] = last
            if j != 1:
                at = slice(j // 2, j // 2 + 1)
                hsum_out.ref[side, at, 0:128] = column_sums(pair.astype(F32))
                hsum_out.ref[side, at, 128:192] = column_sums(last.astype(F32))
        d_out.flush(side)
        if side == 0:
            da_scratch[...] = nn(d_ref[0], merge(wqkv_in.all()[...]))
    for i in range(2):
        place = slice(i * rows // 2, (i + 1) * rows // 2)
        for part, load in ((first, near_in), (second, far_in)):
            total = (da_scratch[place, part] + nn(d_ref[1, place, :], merge(load.ref[0:3]))).astype(BF16)
            if split:
                outs[5 + i].ref[:, part] = total
            else:
                da_out.ref[place, part] = total
        if split:
            outs[5 + i].flush()
        else:
            da_out.flush(i)


def bands(bit_value, count, band):
    return [pl.ds(pl.multiple_of((2 * k + bit_value) * band, band), band) for k in range(count)]


def cut_bands(scratch, mine, away, keep_ref, send_ref, band):
    for k, (take, give) in enumerate(zip(mine, away)):
        place = slice(k * band, (k + 1) * band)
        send_ref[place, :] = scratch[give, :].astype(BF16)
        keep_ref[place, :] = scratch[take, :].astype(BF16)


def grad_body(kind, bit, band, scal, ins, outs, scratch):
    if kind == "ffn":
        df_in, gq_in, hq_in, du_in = ins
        columns = hq_in.ref.shape[1]
        x_first = lambda side: tn(hq_in.all()[...], du_in.all()[side])

        def y_first(side, put):
            put(slice(None), tn(df_in.all()[...], gq_in.all()[side]))

    else:
        a_in, d_in, do_in, c_in = ins
        width = c_in.ref.shape[2]
        columns = 2 * width
        x_first = lambda side: tn(a_in.all()[...], d_in.all()[side, :, 0:columns])

        def y_first(side, put):
            put(slice(0, width), tn(a_in.all()[...], d_in.all()[side, :, columns : 3 * width]))
            put(slice(width, columns), tn(do_in.all()[...], c_in.all()[side]))

    if bit is None:
        for side, out in ((0, outs[0]), (1, outs[1])):

            def put(at, values):
                out.ref[1, :, at] = values.astype(BF16)

            out.ref[0] = x_first(side).astype(BF16)
            y_first(side, put)
        return

    def put(at, values):
        scratch[:, at] = values

    keep_out, send_out = outs[-2:]
    value = (scal[DP] // bit) % 2
    count = keep_out.ref.shape[-2] // band
    mine, away = bands(value, count, band), bands(1 - value, count, band)
    if len(outs) == 4:
        own_out, oth_out = outs[:2]
        for side, out in ((1, oth_out), (0, own_out)):
            out.ref[...] = x_first(side).astype(BF16)
            out.flush()
            y_first(side, put)
            cut_bands(scratch, mine, away, keep_out.ref.at[side], send_out.ref.at[side], band)
            send_out.flush(side)
            keep_out.flush(side)
        return
    for side in range(2):
        scratch[...] = x_first(side)
        cut_bands(scratch, mine, away, keep_out.ref.at[side, 0], send_out.ref.at[side, 0], band)
        y_first(side, put)
        cut_bands(scratch, mine, away, keep_out.ref.at[side, 1], send_out.ref.at[side, 1], band)
        send_out.flush(side)
        keep_out.flush(side)


def second_kernel(band, scal, own_ref, recv_ref, keep_ref, got_ref, xkeep_ref, xsend_ref, yown_ref, yoth_ref, scratch):
    count = xkeep_ref.shape[0] // band
    scratch[...] = own_ref[...].astype(F32) + recv_ref[...].astype(F32)
    mine, away = bands(scal[Y], count, band), bands(1 - scal[Y], count, band)
    yoth_ref[...] = (keep_ref[1].astype(F32) + got_ref[1].astype(F32)).astype(BF16)
    yown_ref[...] = (keep_ref[0].astype(F32) + got_ref[0].astype(F32)).astype(BF16)
    cut_bands(scratch, mine, away, xkeep_ref, xsend_ref, band)


def fold_kernel(band, bit, scal, *refs):
    refs, (keep_out, send_out, scratch) = refs[:-3], refs[-3:]
    lead = scratch.shape[0]
    if len(refs) == 4:
        scratch[0] = refs[0][...].astype(F32) + refs[1][...].astype(F32)
        scratch[1] = refs[2][...].astype(F32) + refs[3][...].astype(F32)
    else:
        scratch[...] = refs[0][...].astype(F32) + refs[1][...].astype(F32)
    count = keep_out.shape[1] // band
    value = (scal[DP] // bit) % 2
    mine, away = bands(value, count, band), bands(1 - value, count, band)
    for part in range(lead):
        cut_bands(scratch.at[part], mine, away, keep_out.at[part], send_out.at[part], band)


def final_kernel(heads_width, scal, *refs):
    (ffn_one, attn_one, ffn_zero, attn_zero), outs = [refs[2 * i : 2 * i + 2] for i in range(4)], refs[8:]
    qkv_ref, out_ref, up_ref, down_ref = outs
    for layer, (keep_ref, recv_ref) in ((1, ffn_one), (0, ffn_zero)):
        up_ref[layer] = keep_ref[0].astype(F32) + recv_ref[0].astype(F32)
        down_ref[layer] = keep_ref[1].astype(F32) + recv_ref[1].astype(F32)
    for layer, (keep_ref, recv_ref) in ((1, attn_one), (0, attn_zero)):
        for part in range(2):
            total = keep_ref[part].astype(F32) + recv_ref[part].astype(F32)
            qkv_ref[layer, 2 * part] = total[:, 0:heads_width]
            if part == 0:
                qkv_ref[layer, 1] = total[:, heads_width : 2 * heads_width]
            else:
                out_ref[layer] = total[:, heads_width : 2 * heads_width].T


def pack_kernel(tensor_size, heads_width, scal, *refs):
    refs, out_ref = refs[:-1], refs[-1]
    out_ref[...] = jnp.zeros(out_ref.shape, F32)
    shard = scal[SHARD]
    for layer in range(LAYERS):
        one_ref, two_ref, heads_ref, units_ref = refs[4 * layer : 4 * layer + 4]
        base = layer * (6 + 2 * tensor_size)
        for row in range(3):
            out_ref[base + row] = one_ref[row : row + 1, :]
            out_ref[base + 3 + row] = two_ref[row : row + 1, :]
        for side in range(2):
            place = shard if side == 0 else shard + 2 - 4 * ((shard // 2) % 2)
            out_ref[base + 6 + place, :, 0:heads_width] = heads_ref[side, 0:1, :]
            out_ref[base + 6 + place, :, 256 : 256 + heads_width] = heads_ref[side, 1:2, :]
            out_ref[base + 6 + tensor_size + place] = units_ref[side : side + 1, :]
    base = LAYERS * (6 + 2 * tensor_size)
    for i, ref in enumerate(refs[4 * LAYERS :]):
        out_ref[base, :, 128 * i : 128 * (i + 1)] = ref[0:1, :]


def total_kernel(scal, in_ref, out_ref):
    devices = out_ref.shape[0]
    total = jnp.sum(in_ref[...].reshape(devices, -1, in_ref.shape[2]), axis=0, keepdims=True)
    out_ref[...] = jnp.broadcast_to(total, out_ref.shape)


def unpack_kernel(tensor_size, heads_width, count, scal, in_ref, hb_ref, ob_ref, gain_ref, shift_ref, ub_ref, db_ref, rms_ref):
    shard = scal[SHARD]
    for layer in range(LAYERS):
        base = layer * (6 + 2 * tensor_size)
        for k in range(2):
            gain_ref[layer, k : k + 1, :] = in_ref[base + 3 * k]
            shift_ref[layer, k : k + 1, :] = in_ref[base + 3 * k + 1]
        ob_ref[layer : layer + 1, :] = in_ref[base + 2]
        db_ref[layer : layer + 1, :] = in_ref[base + 5]
        heads = in_ref[base + 6 + shard]
        hb_ref[layer, 0:1, :] = heads[:, 0:heads_width]
        hb_ref[layer, 1:2, :] = heads[:, 256 : 256 + heads_width]
        ub_ref[layer : layer + 1, :] = in_ref[base + 6 + tensor_size + shard]
    base = LAYERS * (6 + 2 * tensor_size)
    row = jnp.sqrt(in_ref[base] * (1.0 / count))
    for layer in range(LAYERS):
        for k in range(3):
            i = 3 * layer + k
            rms_ref[layer : layer + 1, k : k + 1] = row[:, 128 * i : 128 * i + 1]


def dx_kernel(scal, self_ref, recv_ref, fac_ref, skip_ref, out_ref):
    grad = self_ref[...].astype(F32) + recv_ref[...].astype(F32)
    out_ref[...] = grad * fac_ref[...].astype(F32) + skip_ref[...]


def body(
    hidden,
    long_lengths,
    short_lengths,
    w_qkv,
    bias_qv,
    w_out,
    bias_out,
    ln_gain,
    ln_bias,
    w_up,
    bias_up,
    w_down,
    bias_down,
    cotangent,
):
    own_rows, width = hidden.shape
    rows = 2 * own_rows
    heads_width = w_qkv.shape[-1]
    units = w_up.shape[-1]
    dp_size, tensor_size = lax.axis_size("dp"), lax.axis_size("tensor")
    devices = dp_size * tensor_size
    count_model = float(own_rows * devices * width)
    dp_index, tensor_index = lax.axis_index("dp"), lax.axis_index("tensor")
    core_pairs = [(i, i ^ 1) for i in range(tensor_size)]
    x_pairs = [(i, i ^ 2) for i in range(tensor_size)]
    core_swap = lambda v: lax.ppermute(v, "tensor", core_pairs)
    x_swap = lambda v: lax.ppermute(v, "tensor", x_pairs)
    dp_swap = lambda v, bit: lax.ppermute(v, "dp", [(i, i ^ bit) for i in range(dp_size)])
    over_ranks = lambda top: lax.all_to_all(top, BOTH, 0, 0)

    scal = jnp.concatenate(
        [
            jnp.stack([tensor_index // 2, dp_index % 2, tensor_index % 2, dp_index, tensor_index]).astype(jnp.int32),
            long_lengths,
            short_lengths,
        ]
    )
    w_qkv = jnp.swapaxes(w_qkv, 2, 3)

    chain = [scal]

    def ordered(outs):
        small = min(outs, key=lambda a: a.size)
        chain[0] = lax.optimization_barrier((scal, small))[0]
        return outs

    def run(kernel, ins, outs, name, scratch=()):
        return ordered(
            pl.pallas_call(
                kernel,
                grid_spec=pltpu.PrefetchScalarGridSpec(
                    num_scalar_prefetch=1,
                    grid=(1,),
                    in_specs=[s for _, s in ins],
                    out_specs=[pl.BlockSpec(s, lambda i, t, n=len(s): (0,) * n) for s, _ in outs],
                    scratch_shapes=list(scratch),
                ),
                out_shape=[jax.ShapeDtypeStruct(s, d) for s, d in outs],
                name=name,
                cost_estimate=pl.CostEstimate(flops=0 if name in LIGHT else HEAVY, bytes_accessed=1, transcendentals=0),
                compiler_params=pltpu.CompilerParams(vmem_limit_bytes=VMEM_LIMIT),
            )(chain[0], *[array for array, _ in ins])
        )

    def flow(*args, **named):
        return ordered(stream(chain[0], *args, **named))

    def tie(value, token):
        return lax.optimization_barrier((value, token))[0]

    def settle(*arrived):
        chain[0] = lax.optimization_barrier((chain[0],) + arrived)[0]

    spec = pl.BlockSpec
    full = lambda a: (a, spec(a.shape, lambda i, s: (0,) * len(a.shape)))
    top_rows = lambda a, n: (a, spec((n,) + a.shape[1:], lambda i, s: (0,) * len(a.shape)))
    top_shape = (devices, 1, 128)
    top_store = Store(top_shape, F32)

    def weight_halves(l):
        return run(
            halves_kernel,
            [
                (w_qkv, spec((None, 3, heads_width, width // 2), lambda i, s: (l, 0, 0, s[Y]))),
                (w_out, spec((None, heads_width, width // 2), lambda i, s: (l, 0, s[Y]))),
                (w_up, spec((None, width // 2, units), lambda i, s: (l, s[Y], 0))),
                (w_down, spec((None, units // 2, width), lambda i, s: (l, s[Y], 0))),
            ],
            [((4, heads_width, width // 2), BF16), ((width // 2, units), BF16), ((units // 2, width), BF16)],
            "halves",
        )

    sends = weight_halves(0)
    vecs, small, top, input_sum = run(
        start_kernel,
        [full(a) for a in (hidden, bias_out, ln_gain, ln_bias, bias_down, bias_qv, bias_up)],
        [((LAYERS * VECS, width), F32), ((LAYERS * 3, units), F32), (top_shape, F32), ((1, 128), F32)],
        "start",
    )
    top = over_ranks(top)
    other_hidden = core_swap(hidden)
    small = x_swap(small)
    near = [[x_swap(sends[0]), x_swap(tie(sends[1], (top, small))), None], [None] * 3]
    far = [[dp_swap(tie(near[0][0], top), 1), None, None], [None] * 3]
    other_cotangent = core_swap(cotangent)

    saved = []
    square_terms = []
    states = None
    for l in range(LAYERS):
        last = l == LAYERS - 1
        first = l == 0
        attend_stores = lambda n: [
            per_side_out((n, 3, rows, heads_width), BF16),
            side_rows_out((n, rows, heads_width), F32, 0, 512 // 512),
            side_rows_out((n, 3, rows, rows), BF16, 1, 4),
            side_rows_out((n, rows, heads_width), F32, 0, 512 // 512),
            top_store,
        ]
        low_stores = [rows_out((rows, width), BF16, 2), rows_out((rows, width), BF16, 2)]
        own_loads = [whole_in(top), whole_in(vecs), layer_in(w_qkv, l)]
        scores = [pltpu.VMEM((rows, 128), BF16)] * 4
        if first:
            low_in, fac_in, *parts, own_top = flow(
                partial(attend_body, l, 2, (0,)),
                [pair_in(hidden, other_hidden, 2)] + own_loads,
                low_stores + attend_stores(1),
                "attend_own",
                scratch=scores,
            )
            next_sends = weight_halves(1)
            settle(near[0][1], other_cotangent)
            near[0][2] = x_swap(tie(sends[2], next_sends[0]))
            far[0][1] = dp_swap(tie(near[0][1], next_sends[0]), 1)
            *more, top = flow(
                partial(attend_body, l, 2, (1,)),
                [whole_in(low_in), whole_in(near[l][0]), whole_in(far[l][0]), whole_in(small), whole_in(own_top)],
                attend_stores(1),
                "attend_oth",
                scratch=scores,
            )
            qkv, ctx, soft, rinv = zip(parts, more)
        else:
            low_in, fac_in, *parts, top = flow(
                partial(attend_body, l, 2, (0, 1)),
                [rows_in(states, 2)] + own_loads + [whole_in(near[l][0]), whole_in(far[l][0]), whole_in(small)],
                low_stores + attend_stores(2),
                "attend",
                scratch=scores,
            )
            qkv, ctx, soft, rinv = [(v,) for v in parts]
        if first:
            top = over_ranks(tie(top, (near[0][2], far[0][1])))
            near[1][0] = x_swap(tie(next_sends[0], top))
            far[0][2] = dp_swap(tie(near[0][2], top), 1)
            window = (near[1][0], far[0][2])
        else:
            top = over_ranks(tie(top, (near[1][2], far[1][1])))
            far[1][2] = dp_swap(tie(near[1][2], top), 1)
            window = (far[1][2],)
        att_near, up_near, down_near = near[l]
        att_far, up_far, down_far = far[l]
        low_ctx, fac_ctx, *parts = flow(
            out_body,
            [whole_in(top), side_rows_in(ctx, 2), layer_in(w_out, l), whole_in(att_near), whole_in(att_far)],
            [sides_out((2, rows, heads_width), BF16, 2), sides_out((2, rows, heads_width), BF16, 2)] + [Store((own_rows, width), BF16)] * 2,
            "out_proj",
        )
        norm_stores = [rows_out((rows, width), F32, 4), rows_out((rows, width), BF16, 4), rows_out((rows, 128), F32, 4),
                       Store((2, 128), F32), top_store]
        middle, unit_one, inv_one, sums_one, top = flow(
            partial(norm_body, l, False, 4),
            [whole_in(vecs), pair_in(hidden, other_hidden, 4) if first else rows_in(states, 4), pair_in(*parts, 4),
             pair_in(*[core_swap(v) for v in parts[::-1]], 4)],
            norm_stores,
            "norm_one",
        )
        top = over_ranks(tie(top, window))
        low_mid, fac_mid, active, slope, top = flow(
            partial(up_body, l, 2),
            [whole_in(top), rows_in(middle, 2), whole_in(vecs), layer_in(w_up, l), whole_in(up_near), whole_in(up_far), whole_in(small)],
            [rows_out((rows, width), BF16, 2), rows_out((rows, width), BF16, 2), sides_out((2, rows, units), F32, 2),
             sides_out((2, rows, units), BF16, 2), top_store],
            "up_proj",
        )
        top = over_ranks(top)
        if first:
            near[1][1] = x_swap(tie(next_sends[1], top))
            far[1][0] = dp_swap(tie(near[1][0], top), 1)
        low_act, fac_act, *parts = flow(
            down_body,
            [whole_in(top), sides_in(active, 2), sides_in(slope, 2), layer_in(w_down, l), whole_in(down_near), whole_in(down_far)],
            [sides_out((2, rows, units), BF16, 2), sides_out((2, rows, units), BF16, 2)] + [Store((own_rows, width), BF16)] * 2,
            "down_proj",
        )
        square_terms += [input_sum, sums_one]
        keep = (low_in, fac_in, qkv, ctx, soft, rinv, low_ctx, fac_ctx, unit_one, inv_one, low_mid, fac_mid, low_act, fac_act)
        recvs = [core_swap(v) for v in parts[::-1]]
        if not last:
            states, unit_two, inv_two, sums_two, top = flow(
                partial(norm_body, l, True, 4),
                [whole_in(vecs), rows_in(middle, 4), pair_in(*parts, 4), pair_in(*recvs, 4)],
                norm_stores,
                "norm_two",
            )
            square_terms.append(sums_two)
            input_sum = sums_two[1:2]
            top = over_ranks(tie(top, (near[1][1], far[1][0])))
            near[1][2] = x_swap(tie(next_sends[2], top))
            far[1][1] = dp_swap(tie(near[1][1], top), 1)
            keep += (unit_two, inv_two)
        saved.append(keep)

    sums = [None] * LAYERS
    band = width // dp_size
    banded = band % 16 == 0

    half_width = width // 2

    def grad_group(kind, ins, columns, bit):
        cut = band * 2 if bit == 2 else band
        if not banded:
            stores = [per_side_out((2, width, columns), BF16)] * 2
            bit = None
        elif bit == 1:
            stores = [Store((width, columns), BF16)] * 2 + [per_side_out((2, half_width, columns), BF16)] * 2
        else:
            stores = [per_side_out((2, 2, half_width, columns), BF16)] * 2
        return flow(
            partial(grad_body, kind, bit, cut),
            [whole_in(a) for a in ins],
            stores,
            kind + "_grad",
            scratch=[pltpu.VMEM((width, columns), F32)],
        )

    def begin(group, token):
        own, oth, keep, send = group
        return own, x_swap(tie(oth, token)), keep, dp_swap(tie(send, token), 1)

    def second(pending):
        columns = pending[0].shape[1]
        return run(
            partial(second_kernel, band),
            [full(a) for a in pending],
            [((half_width, columns), BF16)] * 4,
            "second",
            scratch=[pltpu.VMEM((width, columns), F32)],
        )

    def crossed(outs, token):
        xkeep, xsend, yown, yoth = outs
        return xkeep, dp_swap(tie(xsend, token), 1), yown, x_swap(tie(yoth, token))

    def fold(ins, bit):
        remaining, columns = ins[0].shape[-2:]
        lead = 2 if len(ins) == 4 else ins[0].shape[0]
        return run(
            partial(fold_kernel, band, bit),
            [full(a) for a in ins],
            [((lead, remaining // 2, columns), BF16)] * 2,
            "fold",
            scratch=[pltpu.VMEM((lead, remaining, columns), F32)],
        )

    def sent(outs, bit, token):
        return outs[0], dp_swap(tie(outs[1], token), bit)

    count_rows = LAYERS * (6 + 2 * tensor_size) + 1
    packed_rows = -(-count_rows // devices) * devices
    chunk = packed_rows // devices

    def packed_sums():
        (packed,) = run(
            partial(pack_kernel, tensor_size, heads_width),
            [full(a) for l in range(LAYERS) for a in sums[l]] + [full(a) for a in square_terms],
            [((packed_rows, 1, width), F32)],
            "pack",
        )
        return over_ranks(packed.reshape(devices, chunk, width)).reshape(devices, chunk, width)

    def total_sums(packed):
        (totals,) = run(total_kernel, [full(packed)], [((devices, chunk, width), F32)], "total")
        return over_ranks(totals).reshape(packed_rows, 1, width)

    def unpacked_sums(totals):
        return run(
            partial(unpack_kernel, tensor_size, heads_width, count_model),
            [full(totals)],
            [(s, F32) for s in ((LAYERS, 2, heads_width), (LAYERS, width), (LAYERS, 2, width), (LAYERS, 2, width), (LAYERS, units),
                                (LAYERS, width), (LAYERS, 3))],
            "unpack",
        )

    def ffn_back(l, ins, extra):
        return flow(
            partial(ffn_back_body, l, l == LAYERS - 1, 2),
            ins + [sides_in(saved[l][13], 2), layer_in(w_down, l), whole_in(near[l][2]), whole_in(far[l][2]), layer_in(w_up, l),
                   whole_in(near[l][1]), whole_in(far[l][1])],
            [rows_out((rows, width), F32, 2), rows_out((rows, width), BF16, 2), sides_out((2, rows, units), BF16, 2),
             rows_out((rows, width), BF16, 2), Store((3, width), F32), Store((2, units), F32)] + extra,
            "ffn_back",
        )

    def attn_back(l, part, recv, dz_two, split):
        (low_in, fac_in, qkv, ctx, soft, rinv, low_ctx, fac_ctx, unit_one, inv_one, low_mid, fac_mid) = saved[l][:12]
        return flow(
            partial(attn_back_body, l, split, 2),
            [whole_in(vecs), rows_in(part, 2), rows_in(recv, 2, True), rows_in(fac_mid, 2), rows_in(dz_two, 2), rows_in(unit_one, 2),
             rows_in(inv_one, 2), layer_in(w_out, l), per_side_in((fac_ctx,)), per_side_in(rinv), per_side_in(ctx), per_side_in(qkv),
             per_side_in(soft), layer_in(w_qkv, l), whole_in(near[l][0]), whole_in(far[l][0])],
            [rows_out((rows, width), F32, 2), rows_out((rows, width), BF16, 2), per_side_out((2, rows, 3 * heads_width), BF16),
             Store((3, width), F32), Store((2, 2, heads_width), F32)]
            + ([Store((own_rows, width), BF16)] * 2 if split else [rows_out((rows, width), BF16, 2)]),
            "attn_back",
            scratch=[pltpu.VMEM((rows, width), F32)],
        )

    attn_columns = 2 * heads_width
    ins = [whole_in(vecs), rows_in(middle, 2), pair_in(*parts, 2), pair_in(*recvs, 2), pair_in(cotangent, other_cotangent, 2)]
    dz_two, df, du, part, sums_two, unit_sums, output, branch_sum = ffn_back(
        1, ins, [Store((own_rows, width), BF16), Store((1, 128), F32)]
    )
    square_terms.append(branch_sum)
    recv = core_swap(part)
    ffn_one = grad_group("ffn", [df, saved[1][12], saved[1][10], du], units, 1)
    if banded:
        ffn_one = begin(ffn_one, scal)
    dz_one, do, dqkv, sums_one, head_sums, part = attn_back(1, part, recv, dz_two, False)
    recv = core_swap(part)
    sums[1] = (sums_one, sums_two, head_sums, unit_sums)
    attn_one = grad_group("attn", [saved[1][0], dqkv, do, saved[1][6]], attn_columns, 1)
    if banded:
        attn_one = begin(attn_one, scal)
    ins = [whole_in(vecs), rows_in(part, 2), rows_in(recv, 2, True), rows_in(saved[1][1], 2), rows_in(dz_one, 2),
           rows_in(saved[0][14], 2), rows_in(saved[0][15], 2)]
    dz_two, df, du, part, sums_two, unit_sums = ffn_back(0, ins, [])
    recv = core_swap(part)
    if banded:
        ffn_one = second(ffn_one)
        ffn_one = crossed(ffn_one, scal)
    ffn_zero = grad_group("ffn", [df, saved[0][12], saved[0][10], du], units, 1)
    if banded:
        attn_one = second(attn_one)
        ffn_zero = begin(ffn_zero, attn_one[0])
        settle(ffn_one[1], ffn_one[3])
        ffn_one = fold(ffn_one, 2)
        ffn_one = sent(ffn_one, 2, scal)
    dz_one, do, dqkv, sums_one, head_sums, part, away = attn_back(0, part, recv, dz_two, True)
    recv = core_swap(away)
    sums[0] = (sums_one, sums_two, head_sums, unit_sums)
    attn_zero = grad_group("attn", [saved[0][0], dqkv, do, saved[0][6]], attn_columns, 1)
    (grad_hidden,) = run(
        dx_kernel,
        [full(part), full(recv), top_rows(saved[0][1], own_rows), top_rows(dz_one, own_rows)],
        [((own_rows, width), F32)],
        "dx",
    )
    if banded:
        attn_one = crossed(attn_one, grad_hidden)
        ffn_one = fold(ffn_one, 4)
        ffn_one = sent(ffn_one, 4, scal)
        ffn_zero = second(ffn_zero)
        ffn_zero = crossed(ffn_zero, scal)
        attn_one = fold(attn_one, 2)
        attn_zero = begin(attn_zero, attn_one[0])
    packed = packed_sums()
    if banded:
        attn_one = sent(attn_one, 2, ffn_one[1])
        ffn_zero = fold(ffn_zero, 2)
        ffn_zero = sent(ffn_zero, 2, scal)
        totals = total_sums(packed)
        attn_one = fold(attn_one, 4)
        attn_one = sent(attn_one, 4, scal)
        attn_zero = second(attn_zero)
        attn_zero = crossed(attn_zero, scal)
        ffn_zero = fold(ffn_zero, 4)
        ffn_zero = sent(ffn_zero, 4, scal)
        attn_zero = fold(attn_zero, 2)
        attn_zero = sent(attn_zero, 2, scal)
        small_outs = unpacked_sums(totals)
        attn_zero = fold(attn_zero, 4)
        attn_zero = sent(attn_zero, 4, scal)
        grad_qkv, grad_out, grad_up, grad_down = run(
            partial(final_kernel, heads_width),
            [full(a) for pair in (ffn_one, attn_one, ffn_zero, attn_zero) for a in pair],
            [((LAYERS, 3, band, heads_width), F32), ((LAYERS, heads_width, band), F32), ((LAYERS, band, units), F32),
             ((LAYERS, band, width), F32)],
            "final",
        )
    else:
        small_outs = unpacked_sums(total_sums(packed))
        totals = []
        for own, oth in (ffn_zero, ffn_one, attn_zero, attn_one):
            both = own.astype(F32) + x_swap(oth).astype(F32)
            totals.append(lax.psum_scatter(both, "dp", scatter_dimension=1, tiled=True))
        grad_up = jnp.stack([totals[0][0], totals[1][0]])
        grad_down = jnp.stack([totals[0][1], totals[1][1]])
        attn = jnp.stack(totals[2:])
        cut = lambda side, at: attn[:, side, :, at * heads_width : (at + 1) * heads_width]
        grad_qkv = jnp.stack([cut(0, 0), cut(0, 1), cut(1, 0)], 1)
        grad_out = jnp.swapaxes(cut(1, 1), 1, 2)

    head_bias, out_bias, gains, shifts, unit_bias, down_bias, rms = small_outs
    return (
        output,
        grad_hidden,
        grad_qkv,
        head_bias,
        grad_out,
        out_bias,
        gains,
        shifts,
        grad_up,
        unit_bias,
        jnp.swapaxes(grad_down, 1, 2),
        down_bias,
        rms,
    )


def solution(mesh):
    in_specs = (
        P(("dp", "tensor"), None),
        P("dp"),
        P("dp"),
        P(None, None, None, "tensor"),
        P(None, None, "tensor"),
        P(None, "tensor", None),
        P(),
        P(),
        P(),
        P(None, None, "tensor"),
        P(None, "tensor"),
        P(None, "tensor", None),
        P(),
        P(("dp", "tensor"), None),
    )
    out_specs = (
        P(("dp", "tensor"), None),
        P(("dp", "tensor"), None),
        P(None, None, "dp", "tensor"),
        P(None, None, "tensor"),
        P(None, "tensor", "dp"),
        P(),
        P(),
        P(),
        P(None, "dp", "tensor"),
        P(None, "tensor"),
        P(None, "tensor", "dp"),
        P(),
        P(),
    )
    return jax.shard_map(body, mesh=mesh, in_specs=in_specs, out_specs=out_specs, check_vma=False)
```

```python
from functools import partial

import jax
import jax.numpy as jnp
from jax import lax
from jax.experimental import pallas as pl
from jax.experimental.pallas import tpu as pltpu
from jax.sharding import PartitionSpec as P

HEAD_DIM = 64
LAYERS = 2
LONG_LEN = 512
SHORT_LEN = 128
LONG_DEV = 1
SHORT_DEV = 4

EPS = 1e-06
MASKED = -1e30
BOTH = ("dp", "tensor")
F32 = jnp.float32
BF16 = jnp.bfloat16
VMEM_LIMIT = 60 * 1024 * 1024
HEAVY = 10**15
LIGHT = {"halves", "norm_one", "norm_two", "up_proj", "second", "fold"}

X, Y, CORE, DP, SHARD, LENGTHS = range(6)


def nt(left, right):
    return lax.dot_general(left, right, (((1,), (1,)), ((), ())), preferred_element_type=F32)


def nn(left, right):
    return jnp.dot(left, right, preferred_element_type=F32)


def tn(left, right):
    return lax.dot_general(left, right, (((0,), (0,)), ((), ())), preferred_element_type=F32)


def merge(values):
    return values.reshape(values.shape[0] * values.shape[1], values.shape[2])


def bound_of(top_ref):
    return jnp.max(top_ref[...]) * 0.25 + EPS


def halves(scal, width):
    part = width // 2
    near = scal[Y]
    first = pl.ds(pl.multiple_of(near * part, part), part)
    second = pl.ds(pl.multiple_of((1 - near) * part, part), part)
    return first, second


class Load:
    def __init__(self, shape, dtype, pieces):
        self.shape, self.dtype, self.pieces = tuple(shape), dtype, pieces


class Store:
    def __init__(self, shape, dtype, pieces=((),)):
        self.shape, self.dtype, self.pieces = tuple(shape), dtype, pieces


def view(ref, index):
    return ref.at[index] if index else ref


class Arriving:
    def __init__(self, ref, copies):
        self.ref, self.copies, self.waited = ref, copies, set()

    def wait(self, piece):
        if piece not in self.waited:
            self.copies[piece].wait()
            self.waited.add(piece)
        return self.ref

    def all(self):
        for piece in range(len(self.copies)):
            self.wait(piece)
        return self.ref


class Leaving:
    def __init__(self, ref, copies):
        self.ref, self.copies, self.started = ref, copies, set()

    def flush(self, piece=0):
        self.copies[piece].start()
        self.started.add(piece)


def stream(scal, body, loads, stores, name, scratch=()):
    arrays = []

    def slot(array):
        for i, known in enumerate(arrays):
            if known is array:
                return i
        arrays.append(array)
        return len(arrays) - 1

    plan = [[(slot(a), src, dst) for a, src, dst in load.pieces] for load in loads]
    first_out = len(arrays)
    n_in = sum(len(p) for p in plan)
    n_out = sum(len(st.pieces) for st in stores)

    def kernel(scal_ref, *refs):
        sources = refs[: len(arrays)]
        targets = refs[first_out : first_out + len(stores)]
        at = first_out + len(stores)
        vin, at = refs[at : at + len(loads)], at + len(loads)
        vout, at = refs[at : at + len(stores)], at + len(stores)
        extra, (sem_in, sem_out) = refs[at:-2], refs[-2:]
        count = 0
        arriving = []
        for pieces, ref in zip(plan, vin):
            copies = []
            for i, src, dst in pieces:
                copies.append(pltpu.make_async_copy(view(sources[i], src), view(ref, dst), sem_in.at[count]))
                count += 1
            arriving.append(Arriving(ref, copies))
        for piece in range(max(len(p) for p in plan)):
            for a in arriving:
                if piece < len(a.copies):
                    a.copies[piece].start()
        count = 0
        leaving = []
        for st, ref, target in zip(stores, vout, targets):
            copies = []
            for index in st.pieces:
                copies.append(pltpu.make_async_copy(view(ref, index), view(target, index), sem_out.at[count]))
                count += 1
            leaving.append(Leaving(ref, copies))
        body(scal_ref, arriving, leaving, *extra)
        for a in arriving:
            a.all()
        for out in leaving:
            for piece, copy in enumerate(out.copies):
                if piece not in out.started:
                    copy.start()
        for out in leaving:
            for copy in out.copies:
                copy.wait()

    anywhere = pl.BlockSpec(memory_space=pl.ANY)
    return pl.pallas_call(
        kernel,
        in_specs=[pl.BlockSpec(memory_space=pltpu.SMEM)] + [anywhere] * first_out,
        out_specs=[anywhere] * len(stores),
        out_shape=[jax.ShapeDtypeStruct(st.shape, st.dtype) for st in stores],
        scratch_shapes=[pltpu.VMEM(x.shape, x.dtype) for x in list(loads) + list(stores)]
        + list(scratch)
        + [pltpu.SemaphoreType.DMA((n_in,)), pltpu.SemaphoreType.DMA((n_out,))],
        name=name,
        cost_estimate=pl.CostEstimate(flops=0 if name in LIGHT else HEAVY, bytes_accessed=1, transcendentals=0),
        compiler_params=pltpu.CompilerParams(vmem_limit_bytes=VMEM_LIMIT),
    )(scal, *arrays)


ALL = slice(None)


def span(i, size):
    return pl.ds(i * size, size)


def whole_in(a):
    return Load(a.shape, a.dtype, [(a, (), ())])


def layer_in(a, layer):
    return Load(a.shape[1:], a.dtype, [(a, (layer,), ())])


def rows_in(a, count, swap=False):
    size = a.shape[0] // count
    turn = count // 2 if swap else 0
    return Load(a.shape, a.dtype, [(a, (span((i + turn) % count, size),), (span(i, size),)) for i in range(count)])


def pair_in(mine, other, count):
    rows, width = mine.shape
    size = 2 * rows // count
    half = count // 2
    return Load(
        (2 * rows, width),
        mine.dtype,
        [((mine if i < half else other), (span(i % half, size),), (span(i, size),)) for i in range(count)],
    )


def sides_in(a, count):
    size = a.shape[1] // count
    return Load(a.shape, a.dtype, [(a, (ALL, span(i, size)), (ALL, span(i, size))) for i in range(count)])


def side_rows_in(parts, count):
    size = parts[0].shape[1] // count
    sources = [(a, i) for a in parts for i in range(a.shape[0])]
    return Load(
        (2,) + parts[0].shape[1:],
        parts[0].dtype,
        [(a, (s, span(i, size)), (side, span(i, size))) for i in range(count) for side, (a, s) in enumerate(sources)],
    )


def per_side_in(parts):
    pieces = [(a, (i,)) for a in parts for i in range(a.shape[0])]
    return Load((2,) + parts[0].shape[1:], parts[0].dtype, [(a, src, (i,)) for i, (a, src) in enumerate(pieces)])


def rows_out(shape, dtype, count):
    size = shape[0] // count
    return Store(shape, dtype, [(span(i, size),) for i in range(count)])


def sides_out(shape, dtype, count):
    size = shape[1] // count
    return Store(shape, dtype, [(ALL, span(i, size)) for i in range(count)])


def side_rows_out(shape, dtype, lead, count):
    size = shape[1 + lead] // count
    return Store(shape, dtype, [(s,) + (ALL,) * lead + (span(i, size),) for s in range(shape[0]) for i in range(count)])


def per_side_out(shape, dtype):
    return Store(shape, dtype, [(i,) for i in range(shape[0])])


B_OUT, GAIN_ONE, SHIFT_ONE, B_DOWN, GAIN_TWO, SHIFT_TWO, B_Q, B_V, B_UP, VECS = range(10)


def vec(ref, layer, row, width=None):
    at = layer * VECS + row
    return ref[at : at + 1, :] if width is None else ref[at : at + 1, 0:width]


def start_kernel(scal, hidden_ref, bout_ref, gain_ref, shift_ref, bdown_ref, bqv_ref, bup_ref, vecs_ref, small_ref, top_ref, sums_ref):
    heads_width = bqv_ref.shape[2]
    vecs_ref[...] = jnp.zeros(vecs_ref.shape, F32)
    small_ref[...] = jnp.zeros(small_ref.shape, F32)
    for layer in range(LAYERS):
        base = layer * VECS
        one = slice(layer, layer + 1)
        vecs_ref[base + B_OUT : base + B_OUT + 1, :] = bout_ref[one, :]
        vecs_ref[base + B_DOWN : base + B_DOWN + 1, :] = bdown_ref[one, :]
        vecs_ref[base + GAIN_ONE : base + GAIN_ONE + 1, :] = gain_ref[layer, 0:1, :]
        vecs_ref[base + GAIN_TWO : base + GAIN_TWO + 1, :] = gain_ref[layer, 1:2, :]
        vecs_ref[base + SHIFT_ONE : base + SHIFT_ONE + 1, :] = shift_ref[layer, 0:1, :]
        vecs_ref[base + SHIFT_TWO : base + SHIFT_TWO + 1, :] = shift_ref[layer, 1:2, :]
        for ref, at in ((vecs_ref, base + B_Q), (small_ref, 3 * layer)):
            ref[at : at + 1, 0:heads_width] = bqv_ref[layer, 0:1, :]
            ref[at + 1 : at + 2, 0:heads_width] = bqv_ref[layer, 1:2, :]
            ref[at + 2 : at + 3, :] = bup_ref[one, :]
    values = hidden_ref[...].astype(F32)
    top_ref[...] = jnp.full(top_ref.shape, jnp.max(jnp.abs(values)), F32)
    sums_ref[...] = jnp.full((1, 128), jnp.sum(values * values), F32)


def halves_kernel(scal, wqkv_ref, wout_ref, wup_ref, wdown_ref, att_ref, up_ref, down_ref):
    att_ref[0:3] = wqkv_ref[...]
    att_ref[3] = wout_ref[...]
    up_ref[...] = wup_ref[...]
    down_ref[...] = wdown_ref[...]


def row_ids(scal, slots, half_rows):
    rows = 2 * half_rows
    slot = slots + half_rows * scal[CORE]
    slot = jnp.where(slot >= rows, slot - rows, slot) + scal[X] * rows
    short = slot - LONG_DEV * LONG_LEN
    is_long = short < 0
    row = jnp.where(is_long, slot // LONG_LEN, LONG_DEV + short // SHORT_LEN)
    place = jnp.where(is_long, slot % LONG_LEN, short % SHORT_LEN)
    length = jnp.zeros_like(row)
    for i in range(LONG_DEV + SHORT_DEV):
        length = jnp.where(row == i, scal[LENGTHS + i], length)
    return row, jnp.where(place < length, 1, 0)


HEADS = ((0, 128, 0), (0, 128, 1), (128, 192, None))


def lane_mask(rows, which):
    lane = lax.broadcasted_iota(jnp.int32, (rows, 128), 1)
    return (lane < HEAD_DIM) if which == 0 else (lane >= HEAD_DIM)


def only_head(values, which):
    if which is None:
        return values
    return jnp.where(lane_mask(values.shape[0], which), values, jnp.zeros_like(values))


def largest(values):
    return jnp.max(jnp.abs(values))


def put_top(out, tops):
    top = tops[0]
    for other in tops[1:]:
        top = jnp.maximum(top, other)
    out.ref[...] = jnp.full(out.ref.shape, top, F32)
    out.flush()


def attend_body(layer, count, sides, scal, ins, outs, qcode_ref, kcode_ref, qlast_ref, klast_ref):
    if 0 in sides:
        x_in, top_in, vecs_in, own_in, ins = *ins[:4], ins[4:]
        low_out, fac_out, outs = *outs[:2], outs[2:]
        low_ref = low_out.ref
    else:
        low_in, ins = ins[0], ins[1:]
        low_ref = low_in.all()
    if 1 in sides:
        near_in, far_in, small_in, ins = *ins[:3], ins[3:]
    qkv_out, ctx_out, e_out, rinv_out, top_out = outs
    qkv_ref, ctx_ref, e_ref, rinv_ref = (o.ref for o in (qkv_out, ctx_out, e_out, rinv_out))
    rows, width = low_ref.shape
    heads_width = qkv_ref.shape[3]
    first, second = halves(scal, width)
    row, live = row_ids(scal, lax.broadcasted_iota(jnp.int32, (rows, 1), 0), rows // 2)
    code_lane = lax.broadcasted_iota(jnp.int32, (rows, 128), 1) % HEAD_DIM
    qcode_ref[...] = jnp.where(code_lane == row, 1.0, 0.0).astype(BF16)
    hidden_to = (code_lane < LONG_DEV + SHORT_DEV) & ((code_lane != row) | (live == 0))
    kcode_ref[...] = jnp.where(hidden_to, MASKED, 0.0).astype(BF16)
    qlast_ref[...] = qcode_ref[...]
    klast_ref[...] = kcode_ref[...]
    scale = HEAD_DIM ** (-0.5)
    if 0 in sides:
        bound = bound_of(top_in.all())
        size = rows // count
        vecs_ref = vecs_in.all()
        for i in range(count):
            place = slice(i * size, (i + 1) * size)
            tangent = jnp.tanh(x_in.wait(i)[place, :].astype(F32) * (1.0 / bound))
            low = (bound * tangent).astype(BF16)
            low_ref[place, :] = low
            low_out.flush(i)
            fac_out.ref[place, :] = (1.0 - tangent * tangent).astype(BF16)
            fac_out.flush(i)
            own_ref = own_in.all()
            for j in range(3):
                values = nt(low, own_ref[j])
                if j != 1:
                    values = values + vec(vecs_ref, layer, B_Q + j // 2, heads_width)
                qkv_ref[0, j, place, :] = (values * scale if j == 0 else values).astype(BF16)
        qkv_out.flush(0)
    chunk = 512
    chunks = rows // chunk
    tops = []
    for at, side in enumerate(sides):
        if side == 1:
            near_ref, far_ref, small_ref = near_in.all(), far_in.all(), small_in.all()
            for j in range(3):
                values = nt(low_ref[:, first], near_ref[j]) + nt(low_ref[:, second], far_ref[j])
                if j != 1:
                    row = 3 * layer + j // 2
                    values = values + small_ref[row : row + 1, 0:heads_width]
                qkv_ref[at, j] = (values * scale if j == 0 else values).astype(BF16)
            qkv_out.flush(at)
        qlast_ref[:, 0:HEAD_DIM] = qkv_ref[at, 0, :, 128:192]
        klast_ref[:, 0:HEAD_DIM] = qkv_ref[at, 1, :, 128:192]
        heads = []
        for h, (lo, hi, which) in enumerate(HEADS):
            if which is None:
                keys = klast_ref[...]
            else:
                keys = jnp.where(lane_mask(rows, which), qkv_ref[at, 1, :, lo:hi], kcode_ref[...])
            heads.append((h, lo, hi, which, keys, qkv_ref[at, 2, :, lo:hi]))
        left = lane_mask(chunk, 0)
        for i in range(chunks):
            place = slice(i * chunk, (i + 1) * chunk)
            done = []
            for h, lo, hi, which, keys, vals in heads:
                if which is None:
                    asking = qlast_ref[place, :]
                else:
                    asking = jnp.where(lane_mask(chunk, which), qkv_ref[at, 0, place, lo:hi], qcode_ref[place, :])
                scores = nt(asking, keys)
                weights = jnp.exp(scores - jnp.max(scores, axis=1, keepdims=True))
                inverse = 1.0 / jnp.sum(weights, axis=1, keepdims=True)
                low = weights.astype(BF16)
                e_ref[at, h, place, :] = low
                done.append((nn(low, vals) * inverse, inverse))
            pair = jnp.where(left, done[0][0], done[1][0])
            ctx_ref[at, place, 0:128] = pair
            ctx_ref[at, place, 128:192] = done[2][0]
            tops += [largest(pair), largest(done[2][0])]
            rinv_ref[at, place, 0:128] = jnp.where(left, done[0][1], done[1][1])
            rinv_ref[at, place, 128:192] = jnp.broadcast_to(done[2][1], (chunk, HEAD_DIM))
            for out in (e_out, ctx_out, rinv_out):
                out.flush(at * chunks + i)
    tops += [jnp.max(load.all()[...]) for load in ins]
    put_top(top_out, tops)


def out_body(scal, ins, outs):
    top_in, ctx_in, own_in, near_in, far_in = ins
    c_out, fac_out, *o_outs = outs
    bound = bound_of(top_in.all())
    size, width = o_outs[0].ref.shape
    for i, o_out in enumerate(o_outs):
        place = slice(i * size, (i + 1) * size)
        ctx_in.wait(2 * i)
        tangent = jnp.tanh(ctx_in.wait(2 * i + 1)[:, place, :] * (1.0 / bound))
        low = (bound * tangent).astype(BF16)
        c_out.ref[:, place, :] = low
        c_out.flush(i)
        fac_out.ref[:, place, :] = (1.0 - tangent * tangent).astype(BF16)
        fac_out.flush(i)
        own_ref = own_in.all()
        for part, load in zip(halves(scal, width), (near_in, far_in)):
            o_out.ref[:, part] = (nn(low[0], own_ref[:, part]) + nn(low[1], load.all()[3])).astype(BF16)
        o_out.flush()


def norm_forward(mixed, gain, shift):
    centred = mixed - jnp.mean(mixed, axis=1, keepdims=True)
    inverse = lax.rsqrt(jnp.mean(centred * centred, axis=1, keepdims=True) + EPS)
    unit = centred * inverse
    return unit * gain + shift, unit, inverse


def lane_fill(value):
    return jnp.full((1, 128), value, F32)


def norm_body(layer, second, count, scal, ins, outs):
    vecs_in, x_in, self_in, recv_in = ins
    h_out, unit_out, inv_out, sums_out, top_out = outs
    rows, width = h_out.ref.shape
    size = rows // count
    vecs_ref = vecs_in.all()
    bias = vec(vecs_ref, layer, B_DOWN if second else B_OUT)
    gain = vec(vecs_ref, layer, GAIN_TWO if second else GAIN_ONE)
    shift = vec(vecs_ref, layer, SHIFT_TWO if second else SHIFT_ONE)
    tops, branch_sum, result_sum = [], 0.0, 0.0
    for i in range(count):
        place = slice(i * size, (i + 1) * size)
        branch = self_in.wait(i)[place, :].astype(F32) + recv_in.wait(i)[place, :].astype(F32) + bias
        result, unit, inverse = norm_forward(x_in.wait(i)[place, :].astype(F32) + branch, gain, shift)
        h_out.ref[place, :] = result
        h_out.flush(i)
        unit_out.ref[place, :] = unit.astype(unit_out.ref.dtype)
        unit_out.flush(i)
        inv_out.ref[place, :] = jnp.broadcast_to(inverse, (size, 128))
        inv_out.flush(i)
        tops.append(largest(result))
        if i < count // 2:
            branch_sum = branch_sum + jnp.sum(branch * branch)
            result_sum = result_sum + jnp.sum(result * result)
    sums_out.ref[0:1, :] = lane_fill(branch_sum)
    sums_out.ref[1:2, :] = lane_fill(result_sum)
    sums_out.flush()
    put_top(top_out, tops)


def up_body(layer, count, scal, ins, outs):
    top_in, h_in, vecs_in, own_in, near_in, far_in, small_in = ins
    low_out, fac_out, g_out, slope_out, top_out = outs
    low_ref = low_out.ref
    rows, width = low_ref.shape
    size = rows // count
    bound = bound_of(top_in.all())
    first, second = halves(scal, width)
    tops = []
    for i in range(count):
        place = slice(i * size, (i + 1) * size)
        tangent = jnp.tanh(h_in.wait(i)[place, :] * (1.0 / bound))
        low = (bound * tangent).astype(BF16)
        low_ref[place, :] = low
        low_out.flush(i)
        fac_out.ref[place, :] = (1.0 - tangent * tangent).astype(BF16)
        fac_out.flush(i)
        for side in range(2):
            if side == 0:
                units = nn(low, own_in.all()[...]) + vec(vecs_in.all(), layer, B_UP)
            else:
                units = nn(low_ref[place, first], near_in.all()[...]) + nn(low_ref[place, second], far_in.all()[...])
                units = units + small_in.all()[3 * layer + 2 : 3 * layer + 3, :]
            area = 0.5 + 0.5 * lax.erf(units * (0.5**0.5))
            density = jnp.exp(-0.5 * units * units) * 0.3989422804014327
            active = units * area
            g_out.ref[side, place, :] = active
            slope_out.ref[side, place, :] = (area + units * density).astype(BF16)
            tops.append(largest(active))
        g_out.flush(i)
        slope_out.flush(i)
    put_top(top_out, tops)


def down_body(scal, ins, outs):
    top_in, g_in, slope_in, own_in, near_in, far_in = ins
    low_out, fac_out, *f_outs = outs
    low_ref = low_out.ref
    size = f_outs[0].ref.shape[0]
    bound = bound_of(top_in.all())
    first, second = halves(scal, low_ref.shape[2])
    for i, f_out in enumerate(f_outs):
        place = slice(i * size, (i + 1) * size)
        tangent = jnp.tanh(g_in.wait(i)[:, place, :] * (1.0 / bound))
        low_ref[:, place, :] = (bound * tangent).astype(BF16)
        low_out.flush(i)
        slope = slope_in.wait(i)[:, place, :].astype(F32)
        fac_out.ref[:, place, :] = ((1.0 - tangent * tangent) * slope).astype(BF16)
        fac_out.flush(i)
        f_out.ref[...] = (
            nn(low_ref[0, place, :], own_in.all()[...])
            + nn(low_ref[1, place, first], near_in.all()[...])
            + nn(low_ref[1, place, second], far_in.all()[...])
        ).astype(BF16)
        f_out.flush()


def norm_back(grad, unit, inverse, gain):
    scaled = grad * gain
    return (
        scaled
        - jnp.mean(scaled, axis=1, keepdims=True)
        - unit * jnp.mean(scaled * unit, axis=1, keepdims=True)
    ) * inverse


def column_sums(values):
    return jnp.sum(values, axis=0, keepdims=True)


def ffn_back_body(layer, last_layer, count, scal, ins, outs):
    vecs_in, ins = ins[0], ins[1:]
    if last_layer:
        (h_in, self_in, recv_in, cot_in), ins = ins[:4], ins[4:]
        result_out, fsum_out = outs[-2:]
    else:
        (self_in, recv_in, infac_in, skip_in, unit_in, inv_in), ins = ins[:6], ins[6:]
    fac_in, down_in, dnear_in, dfar_in, up_in, unear_in, ufar_in = ins
    dz_out, df_out, du_out, dh_out, sums_out, usum_out = outs[:6]
    rows, width = dz_out.ref.shape
    size = rows // count
    vecs_ref = vecs_in.all()
    gain = vec(vecs_ref, layer, GAIN_TWO)
    first, second = halves(scal, width)
    du_ref = du_out.ref
    totals = None
    unit_totals = None
    branch_sum = 0.0
    for i in range(count):
        place = slice(i * size, (i + 1) * size)
        mine = i < count // 2
        both = self_in.wait(i)[place, :].astype(F32) + recv_in.wait(i)[place, :].astype(F32)
        if last_layer:
            branch = both + vec(vecs_ref, layer, B_DOWN)
            result, unit, inverse = norm_forward(h_in.wait(i)[place, :] + branch, gain, vec(vecs_ref, layer, SHIFT_TWO))
            grad = cot_in.wait(i)[place, :].astype(F32)
            if mine:
                result_out.ref[place, :] = result.astype(BF16)
                result_out.flush(i)
                branch_sum = branch_sum + jnp.sum(branch * branch)
        else:
            grad = both * infac_in.wait(i)[place, :].astype(F32) + skip_in.wait(i)[place, :]
            unit = unit_in.wait(i)[place, :].astype(F32)
            inverse = inv_in.wait(i)[place, 0:1]
        mixed = norm_back(grad, unit, inverse, gain)
        low = mixed.astype(BF16)
        dz_out.ref[place, :] = mixed
        dz_out.flush(i)
        df_out.ref[place, :] = low
        df_out.flush(i)
        if mine:
            new = [column_sums(v) for v in (grad * unit, grad, low.astype(F32))]
            totals = new if totals is None else [a + b for a, b in zip(totals, new)]
        fac_ref = fac_in.wait(i)
        du_ref[0, place, :] = (nt(low, down_in.all()[...]) * fac_ref[0, place, :].astype(F32)).astype(BF16)
        for part, load in ((first, dnear_in), (second, dfar_in)):
            du_ref[1, place, part] = (nt(low, load.all()[...]) * fac_ref[1, place, part].astype(F32)).astype(BF16)
        du_out.flush(i)
        for part, load in ((first, unear_in), (second, ufar_in)):
            dh_out.ref[place, part] = (
                nt(du_ref[0, place, :], up_in.all()[part, :]) + nt(du_ref[1, place, :], load.all()[...])
            ).astype(BF16)
        dh_out.flush(i)
        new = [column_sums(du_ref[side, place, :].astype(F32)) for side in range(2)]
        unit_totals = new if unit_totals is None else [a + b for a, b in zip(unit_totals, new)]
    for row, values in enumerate(totals):
        sums_out.ref[row : row + 1, :] = values
    for row, values in enumerate(unit_totals):
        usum_out.ref[row : row + 1, :] = values
    if last_layer:
        fsum_out.ref[...] = lane_fill(branch_sum)


def attn_back_body(layer, split, count, scal, ins, outs, da_scratch):
    (vecs_in, self_in, recv_in, hfac_in, skip_in, unit_in, inv_in, wout_in, cfac_in, rinv_in, ctx_in, qkv_in, e_in, wqkv_in,
     near_in, far_in) = ins
    dz_out, do_out, d_out, sums_out, hsum_out, da_out = outs[:6]
    rows, width = dz_out.ref.shape
    heads_width = qkv_in.ref.shape[3]
    size = rows // count
    first, second = halves(scal, width)
    gain = vec(vecs_in.all(), layer, GAIN_ONE)
    totals = None
    for i in range(count):
        place = slice(i * size, (i + 1) * size)
        grad = self_in.wait(i)[place, :].astype(F32) + recv_in.wait(i)[place, :].astype(F32)
        grad = grad * hfac_in.wait(i)[place, :].astype(F32) + skip_in.wait(i)[place, :]
        unit = unit_in.wait(i)[place, :].astype(F32)
        mixed = norm_back(grad, unit, inv_in.wait(i)[place, 0:1], gain)
        low = mixed.astype(BF16)
        dz_out.ref[place, :] = mixed
        dz_out.flush(i)
        do_out.ref[place, :] = low
        do_out.flush(i)
        if i < count // 2:
            new = [column_sums(v) for v in (grad * unit, grad, low.astype(F32))]
            totals = new if totals is None else [a + b for a, b in zip(totals, new)]
    for row, values in enumerate(totals):
        sums_out.ref[row : row + 1, :] = values
    do_ref, d_ref = do_out.ref, d_out.ref
    scale = HEAD_DIM ** (-0.5)
    left = lane_mask(rows, 0)
    for side in range(2):
        if side == 0:
            grad_ctx = nt(do_ref[...], wout_in.all()[...])
        else:
            grad_ctx = nt(do_ref[:, first], near_in.all()[3]) + nt(do_ref[:, second], far_in.all()[3])
        grad_ctx = grad_ctx * cfac_in.wait(side)[side].astype(F32)
        low = (grad_ctx * rinv_in.wait(side)[side]).astype(BF16)
        product = low.astype(F32) * ctx_in.wait(side)[side]
        qkv_ref, e_ref = qkv_in.wait(side), e_in.wait(side)
        results = []
        for h, (lo, hi, which) in enumerate(HEADS):
            inner = jnp.sum(only_head(product[:, lo:hi], which), axis=1, keepdims=True)
            values = only_head(qkv_ref[side, 2, :, lo:hi], which)
            weights = e_ref[side, h]
            grad_weights = nt(low[:, lo:hi], values)
            grad_scores = (weights.astype(F32) * (grad_weights - inner)).astype(BF16)
            dq = nn(grad_scores, qkv_ref[side, 1, :, lo:hi]) * scale
            dk = tn(qkv_ref[side, 0, :, lo:hi], grad_scores).T
            dv = tn(low[:, lo:hi], weights).T
            results.append((dq, dk, dv))
        for j in range(3):
            pair = jnp.where(left, results[0][j], results[1][j]).astype(BF16)
            last = results[2][j].astype(BF16)
            d_ref[side, :, j * heads_width : j * heads_width + 128] = pair
            d_ref[side, :, j * heads_width + 128 : (j + 1) * heads_width] = last
            if j != 1:
                at = slice(j // 2, j // 2 + 1)
                hsum_out.ref[side, at, 0:128] = column_sums(pair.astype(F32))
                hsum_out.ref[side, at, 128:192] = column_sums(last.astype(F32))
        d_out.flush(side)
        if side == 0:
            da_scratch[...] = nn(d_ref[0], merge(wqkv_in.all()[...]))
    for i in range(2):
        place = slice(i * rows // 2, (i + 1) * rows // 2)
        for part, load in ((first, near_in), (second, far_in)):
            total = (da_scratch[place, part] + nn(d_ref[1, place, :], merge(load.ref[0:3]))).astype(BF16)
            if split:
                outs[5 + i].ref[:, part] = total
            else:
                da_out.ref[place, part] = total
        if split:
            outs[5 + i].flush()
        else:
            da_out.flush(i)


def bands(bit_value, count, band):
    return [pl.ds(pl.multiple_of((2 * k + bit_value) * band, band), band) for k in range(count)]


def cut_bands(scratch, mine, away, keep_ref, send_ref, band):
    for k, (take, give) in enumerate(zip(mine, away)):
        place = slice(k * band, (k + 1) * band)
        send_ref[place, :] = scratch[give, :].astype(BF16)
        keep_ref[place, :] = scratch[take, :].astype(BF16)


def grad_body(kind, bit, band, scal, ins, outs, scratch):
    if kind == "ffn":
        df_in, gq_in, hq_in, du_in = ins
        columns = hq_in.ref.shape[1]
        x_first = lambda side: tn(hq_in.all()[...], du_in.all()[side])

        def y_first(side, put):
            put(slice(None), tn(df_in.all()[...], gq_in.all()[side]))

    else:
        a_in, d_in, do_in, c_in = ins
        width = c_in.ref.shape[2]
        columns = 2 * width
        x_first = lambda side: tn(a_in.all()[...], d_in.all()[side, :, 0:columns])

        def y_first(side, put):
            put(slice(0, width), tn(a_in.all()[...], d_in.all()[side, :, columns : 3 * width]))
            put(slice(width, columns), tn(do_in.all()[...], c_in.all()[side]))

    if bit is None:
        for side, out in ((0, outs[0]), (1, outs[1])):

            def put(at, values):
                out.ref[1, :, at] = values.astype(BF16)

            out.ref[0] = x_first(side).astype(BF16)
            y_first(side, put)
        return

    def put(at, values):
        scratch[:, at] = values

    keep_out, send_out = outs[-2:]
    value = (scal[DP] // bit) % 2
    count = keep_out.ref.shape[-2] // band
    mine, away = bands(value, count, band), bands(1 - value, count, band)
    if len(outs) == 4:
        own_out, oth_out = outs[:2]
        for side, out in ((1, oth_out), (0, own_out)):
            out.ref[...] = x_first(side).astype(BF16)
            out.flush()
            y_first(side, put)
            cut_bands(scratch, mine, away, keep_out.ref.at[side], send_out.ref.at[side], band)
            send_out.flush(side)
            keep_out.flush(side)
        return
    for side in range(2):
        scratch[...] = x_first(side)
        cut_bands(scratch, mine, away, keep_out.ref.at[side, 0], send_out.ref.at[side, 0], band)
        y_first(side, put)
        cut_bands(scratch, mine, away, keep_out.ref.at[side, 1], send_out.ref.at[side, 1], band)
        send_out.flush(side)
        keep_out.flush(side)


def second_kernel(band, scal, own_ref, recv_ref, keep_ref, got_ref, xkeep_ref, xsend_ref, yown_ref, yoth_ref, scratch):
    count = xkeep_ref.shape[0] // band
    scratch[...] = own_ref[...].astype(F32) + recv_ref[...].astype(F32)
    mine, away = bands(scal[Y], count, band), bands(1 - scal[Y], count, band)
    yoth_ref[...] = (keep_ref[1].astype(F32) + got_ref[1].astype(F32)).astype(BF16)
    yown_ref[...] = (keep_ref[0].astype(F32) + got_ref[0].astype(F32)).astype(BF16)
    cut_bands(scratch, mine, away, xkeep_ref, xsend_ref, band)


def fold_kernel(band, bit, scal, *refs):
    refs, (keep_out, send_out, scratch) = refs[:-3], refs[-3:]
    lead = scratch.shape[0]
    if len(refs) == 4:
        scratch[0] = refs[0][...].astype(F32) + refs[1][...].astype(F32)
        scratch[1] = refs[2][...].astype(F32) + refs[3][...].astype(F32)
    else:
        scratch[...] = refs[0][...].astype(F32) + refs[1][...].astype(F32)
    count = keep_out.shape[1] // band
    value = (scal[DP] // bit) % 2
    mine, away = bands(value, count, band), bands(1 - value, count, band)
    for part in range(lead):
        cut_bands(scratch.at[part], mine, away, keep_out.at[part], send_out.at[part], band)


def final_kernel(heads_width, scal, *refs):
    (ffn_one, attn_one, ffn_zero, attn_zero), outs = [refs[2 * i : 2 * i + 2] for i in range(4)], refs[8:]
    qkv_ref, out_ref, up_ref, down_ref = outs
    for layer, (keep_ref, recv_ref) in ((1, ffn_one), (0, ffn_zero)):
        up_ref[layer] = keep_ref[0].astype(F32) + recv_ref[0].astype(F32)
        down_ref[layer] = keep_ref[1].astype(F32) + recv_ref[1].astype(F32)
    for layer, (keep_ref, recv_ref) in ((1, attn_one), (0, attn_zero)):
        for part in range(2):
            total = keep_ref[part].astype(F32) + recv_ref[part].astype(F32)
            qkv_ref[layer, 2 * part] = total[:, 0:heads_width]
            if part == 0:
                qkv_ref[layer, 1] = total[:, heads_width : 2 * heads_width]
            else:
                out_ref[layer] = total[:, heads_width : 2 * heads_width].T


def pack_kernel(tensor_size, heads_width, scal, *refs):
    refs, out_ref = refs[:-1], refs[-1]
    out_ref[...] = jnp.zeros(out_ref.shape, F32)
    shard = scal[SHARD]
    for layer in range(LAYERS):
        one_ref, two_ref, heads_ref, units_ref = refs[4 * layer : 4 * layer + 4]
        base = layer * (6 + 2 * tensor_size)
        for row in range(3):
            out_ref[base + row] = one_ref[row : row + 1, :]
            out_ref[base + 3 + row] = two_ref[row : row + 1, :]
        for side in range(2):
            place = shard if side == 0 else shard + 2 - 4 * ((shard // 2) % 2)
            out_ref[base + 6 + place, :, 0:heads_width] = heads_ref[side, 0:1, :]
            out_ref[base + 6 + place, :, 256 : 256 + heads_width] = heads_ref[side, 1:2, :]
            out_ref[base + 6 + tensor_size + place] = units_ref[side : side + 1, :]
    base = LAYERS * (6 + 2 * tensor_size)
    for i, ref in enumerate(refs[4 * LAYERS :]):
        out_ref[base, :, 128 * i : 128 * (i + 1)] = ref[0:1, :]


def total_kernel(scal, in_ref, out_ref):
    devices = out_ref.shape[0]
    total = jnp.sum(in_ref[...].reshape(devices, -1, in_ref.shape[2]), axis=0, keepdims=True)
    out_ref[...] = jnp.broadcast_to(total, out_ref.shape)


def unpack_kernel(tensor_size, heads_width, count, scal, in_ref, hb_ref, ob_ref, gain_ref, shift_ref, ub_ref, db_ref, rms_ref):
    shard = scal[SHARD]
    for layer in range(LAYERS):
        base = layer * (6 + 2 * tensor_size)
        for k in range(2):
            gain_ref[layer, k : k + 1, :] = in_ref[base + 3 * k]
            shift_ref[layer, k : k + 1, :] = in_ref[base + 3 * k + 1]
        ob_ref[layer : layer + 1, :] = in_ref[base + 2]
        db_ref[layer : layer + 1, :] = in_ref[base + 5]
        heads = in_ref[base + 6 + shard]
        hb_ref[layer, 0:1, :] = heads[:, 0:heads_width]
        hb_ref[layer, 1:2, :] = heads[:, 256 : 256 + heads_width]
        ub_ref[layer : layer + 1, :] = in_ref[base + 6 + tensor_size + shard]
    base = LAYERS * (6 + 2 * tensor_size)
    row = jnp.sqrt(in_ref[base] * (1.0 / count))
    for layer in range(LAYERS):
        for k in range(3):
            i = 3 * layer + k
            rms_ref[layer : layer + 1, k : k + 1] = row[:, 128 * i : 128 * i + 1]


def dx_kernel(scal, self_ref, recv_ref, fac_ref, skip_ref, out_ref):
    grad = self_ref[...].astype(F32) + recv_ref[...].astype(F32)
    out_ref[...] = grad * fac_ref[...].astype(F32) + skip_ref[...]


def body(
    hidden,
    long_lengths,
    short_lengths,
    w_qkv,
    bias_qv,
    w_out,
    bias_out,
    ln_gain,
    ln_bias,
    w_up,
    bias_up,
    w_down,
    bias_down,
    cotangent,
):
    own_rows, width = hidden.shape
    rows = 2 * own_rows
    heads_width = w_qkv.shape[-1]
    units = w_up.shape[-1]
    dp_size, tensor_size = lax.axis_size("dp"), lax.axis_size("tensor")
    devices = dp_size * tensor_size
    count_model = float(own_rows * devices * width)
    dp_index, tensor_index = lax.axis_index("dp"), lax.axis_index("tensor")
    core_pairs = [(i, i ^ 1) for i in range(tensor_size)]
    x_pairs = [(i, i ^ 2) for i in range(tensor_size)]
    core_swap = lambda v: lax.ppermute(v, "tensor", core_pairs)
    x_swap = lambda v: lax.ppermute(v, "tensor", x_pairs)
    dp_swap = lambda v, bit: lax.ppermute(v, "dp", [(i, i ^ bit) for i in range(dp_size)])
    over_ranks = lambda top: lax.all_to_all(top, BOTH, 0, 0)

    scal = jnp.concatenate(
        [
            jnp.stack([tensor_index // 2, dp_index % 2, tensor_index % 2, dp_index, tensor_index]).astype(jnp.int32),
            long_lengths,
            short_lengths,
        ]
    )
    w_qkv = jnp.swapaxes(w_qkv, 2, 3)

    chain = [scal]

    def ordered(outs):
        small = min(outs, key=lambda a: a.size)
        chain[0] = lax.optimization_barrier((scal, small))[0]
        return outs

    def run(kernel, ins, outs, name, scratch=()):
        return ordered(
            pl.pallas_call(
                kernel,
                grid_spec=pltpu.PrefetchScalarGridSpec(
                    num_scalar_prefetch=1,
                    grid=(1,),
                    in_specs=[s for _, s in ins],
                    out_specs=[pl.BlockSpec(s, lambda i, t, n=len(s): (0,) * n) for s, _ in outs],
                    scratch_shapes=list(scratch),
                ),
                out_shape=[jax.ShapeDtypeStruct(s, d) for s, d in outs],
                name=name,
                cost_estimate=pl.CostEstimate(flops=0 if name in LIGHT else HEAVY, bytes_accessed=1, transcendentals=0),
                compiler_params=pltpu.CompilerParams(vmem_limit_bytes=VMEM_LIMIT),
            )(chain[0], *[array for array, _ in ins])
        )

    def flow(*args, **named):
        return ordered(stream(chain[0], *args, **named))

    def tie(value, token):
        return lax.optimization_barrier((value, token))[0]

    def settle(*arrived):
        chain[0] = lax.optimization_barrier((chain[0],) + arrived)[0]

    spec = pl.BlockSpec
    full = lambda a: (a, spec(a.shape, lambda i, s: (0,) * len(a.shape)))
    top_rows = lambda a, n: (a, spec((n,) + a.shape[1:], lambda i, s: (0,) * len(a.shape)))
    top_shape = (devices, 1, 128)
    top_store = Store(top_shape, F32)

    def weight_halves(l):
        return run(
            halves_kernel,
            [
                (w_qkv, spec((None, 3, heads_width, width // 2), lambda i, s: (l, 0, 0, s[Y]))),
                (w_out, spec((None, heads_width, width // 2), lambda i, s: (l, 0, s[Y]))),
                (w_up, spec((None, width // 2, units), lambda i, s: (l, s[Y], 0))),
                (w_down, spec((None, units // 2, width), lambda i, s: (l, s[Y], 0))),
            ],
            [((4, heads_width, width // 2), BF16), ((width // 2, units), BF16), ((units // 2, width), BF16)],
            "halves",
        )

    sends = weight_halves(0)
    vecs, small, top, input_sum = run(
        start_kernel,
        [full(a) for a in (hidden, bias_out, ln_gain, ln_bias, bias_down, bias_qv, bias_up)],
        [((LAYERS * VECS, width), F32), ((LAYERS * 3, units), F32), (top_shape, F32), ((1, 128), F32)],
        "start",
    )
    top = over_ranks(top)
    other_hidden = core_swap(hidden)
    small = x_swap(small)
    near = [[x_swap(sends[0]), x_swap(tie(sends[1], (top, small))), None], [None] * 3]
    far = [[dp_swap(tie(near[0][0], top), 1), None, None], [None] * 3]
    other_cotangent = core_swap(cotangent)

    saved = []
    square_terms = []
    states = None
    for l in range(LAYERS):
        last = l == LAYERS - 1
        first = l == 0
        attend_stores = lambda n: [
            per_side_out((n, 3, rows, heads_width), BF16),
            side_rows_out((n, rows, heads_width), F32, 0, 512 // 512),
            side_rows_out((n, 3, rows, rows), BF16, 1, 4),
            side_rows_out((n, rows, heads_width), F32, 0, 512 // 512),
            top_store,
        ]
        low_stores = [rows_out((rows, width), BF16, 2), rows_out((rows, width), BF16, 2)]
        own_loads = [whole_in(top), whole_in(vecs), layer_in(w_qkv, l)]
        scores = [pltpu.VMEM((rows, 128), BF16)] * 4
        if first:
            low_in, fac_in, *parts, own_top = flow(
                partial(attend_body, l, 2, (0,)),
                [pair_in(hidden, other_hidden, 2)] + own_loads,
                low_stores + attend_stores(1),
                "attend_own",
                scratch=scores,
            )
            next_sends = weight_halves(1)
            settle(near[0][1], other_cotangent)
            near[0][2] = x_swap(tie(sends[2], next_sends[0]))
            far[0][1] = dp_swap(tie(near[0][1], next_sends[0]), 1)
            *more, top = flow(
                partial(attend_body, l, 2, (1,)),
                [whole_in(low_in), whole_in(near[l][0]), whole_in(far[l][0]), whole_in(small), whole_in(own_top)],
                attend_stores(1),
                "attend_oth",
                scratch=scores,
            )
            qkv, ctx, soft, rinv = zip(parts, more)
        else:
            low_in, fac_in, *parts, top = flow(
                partial(attend_body, l, 2, (0, 1)),
                [rows_in(states, 2)] + own_loads + [whole_in(near[l][0]), whole_in(far[l][0]), whole_in(small)],
                low_stores + attend_stores(2),
                "attend",
                scratch=scores,
            )
            qkv, ctx, soft, rinv = [(v,) for v in parts]
        if first:
            top = over_ranks(tie(top, (near[0][2], far[0][1])))
            near[1][0] = x_swap(tie(next_sends[0], top))
            far[0][2] = dp_swap(tie(near[0][2], top), 1)
            window = (near[1][0], far[0][2])
        else:
            top = over_ranks(tie(top, (near[1][2], far[1][1])))
            far[1][2] = dp_swap(tie(near[1][2], top), 1)
            window = (far[1][2],)
        att_near, up_near, down_near = near[l]
        att_far, up_far, down_far = far[l]
        low_ctx, fac_ctx, *parts = flow(
            out_body,
            [whole_in(top), side_rows_in(ctx, 2), layer_in(w_out, l), whole_in(att_near), whole_in(att_far)],
            [sides_out((2, rows, heads_width), BF16, 2), sides_out((2, rows, heads_width), BF16, 2)] + [Store((own_rows, width), BF16)] * 2,
            "out_proj",
        )
        norm_stores = [rows_out((rows, width), F32, 2), rows_out((rows, width), BF16, 2), rows_out((rows, 128), F32, 2),
                       Store((2, 128), F32), top_store]
        middle, unit_one, inv_one, sums_one, top = flow(
            partial(norm_body, l, False, 2),
            [whole_in(vecs), pair_in(hidden, other_hidden, 2) if first else rows_in(states, 2), pair_in(*parts, 2),
             pair_in(*[core_swap(v) for v in parts[::-1]], 2)],
            norm_stores,
            "norm_one",
        )
        top = over_ranks(tie(top, window))
        low_mid, fac_mid, active, slope, top = flow(
            partial(up_body, l, 2),
            [whole_in(top), rows_in(middle, 2), whole_in(vecs), layer_in(w_up, l), whole_in(up_near), whole_in(up_far), whole_in(small)],
            [rows_out((rows, width), BF16, 2), rows_out((rows, width), BF16, 2), sides_out((2, rows, units), F32, 2),
             sides_out((2, rows, units), BF16, 2), top_store],
            "up_proj",
        )
        top = over_ranks(top)
        if first:
            near[1][1] = x_swap(tie(next_sends[1], top))
            far[1][0] = dp_swap(tie(near[1][0], top), 1)
        low_act, fac_act, *parts = flow(
            down_body,
            [whole_in(top), sides_in(active, 2), sides_in(slope, 2), layer_in(w_down, l), whole_in(down_near), whole_in(down_far)],
            [sides_out((2, rows, units), BF16, 2), sides_out((2, rows, units), BF16, 2)] + [Store((own_rows, width), BF16)] * 2,
            "down_proj",
        )
        square_terms += [input_sum, sums_one]
        keep = (low_in, fac_in, qkv, ctx, soft, rinv, low_ctx, fac_ctx, unit_one, inv_one, low_mid, fac_mid, low_act, fac_act)
        recvs = [core_swap(v) for v in parts[::-1]]
        if not last:
            states, unit_two, inv_two, sums_two, top = flow(
                partial(norm_body, l, True, 2),
                [whole_in(vecs), rows_in(middle, 2), pair_in(*parts, 2), pair_in(*recvs, 2)],
                norm_stores,
                "norm_two",
            )
            square_terms.append(sums_two)
            input_sum = sums_two[1:2]
            top = over_ranks(tie(top, (near[1][1], far[1][0])))
            near[1][2] = x_swap(tie(next_sends[2], top))
            far[1][1] = dp_swap(tie(near[1][1], top), 1)
            keep += (unit_two, inv_two)
        saved.append(keep)

    sums = [None] * LAYERS
    band = width // dp_size
    banded = band % 16 == 0

    half_width = width // 2

    def grad_group(kind, ins, columns, bit):
        cut = band * 2 if bit == 2 else band
        if not banded:
            stores = [per_side_out((2, width, columns), BF16)] * 2
            bit = None
        elif bit == 1:
            stores = [Store((width, columns), BF16)] * 2 + [per_side_out((2, half_width, columns), BF16)] * 2
        else:
            stores = [per_side_out((2, 2, half_width, columns), BF16)] * 2
        return flow(
            partial(grad_body, kind, bit, cut),
            [whole_in(a) for a in ins],
            stores,
            kind + "_grad",
            scratch=[pltpu.VMEM((width, columns), F32)],
        )

    def begin(group, token):
        own, oth, keep, send = group
        return own, x_swap(tie(oth, token)), keep, dp_swap(tie(send, token), 1)

    def second(pending):
        columns = pending[0].shape[1]
        return run(
            partial(second_kernel, band),
            [full(a) for a in pending],
            [((half_width, columns), BF16)] * 4,
            "second",
            scratch=[pltpu.VMEM((width, columns), F32)],
        )

    def crossed(outs, token):
        xkeep, xsend, yown, yoth = outs
        return xkeep, dp_swap(tie(xsend, token), 1), yown, x_swap(tie(yoth, token))

    def fold(ins, bit):
        remaining, columns = ins[0].shape[-2:]
        lead = 2 if len(ins) == 4 else ins[0].shape[0]
        return run(
            partial(fold_kernel, band, bit),
            [full(a) for a in ins],
            [((lead, remaining // 2, columns), BF16)] * 2,
            "fold",
            scratch=[pltpu.VMEM((lead, remaining, columns), F32)],
        )

    def sent(outs, bit, token):
        return outs[0], dp_swap(tie(outs[1], token), bit)

    count_rows = LAYERS * (6 + 2 * tensor_size) + 1
    packed_rows = -(-count_rows // devices) * devices
    chunk = packed_rows // devices

    def packed_sums():
        (packed,) = run(
            partial(pack_kernel, tensor_size, heads_width),
            [full(a) for l in range(LAYERS) for a in sums[l]] + [full(a) for a in square_terms],
            [((packed_rows, 1, width), F32)],
            "pack",
        )
        return over_ranks(packed.reshape(devices, chunk, width)).reshape(devices, chunk, width)

    def total_sums(packed):
        (totals,) = run(total_kernel, [full(packed)], [((devices, chunk, width), F32)], "total")
        return over_ranks(totals).reshape(packed_rows, 1, width)

    def unpacked_sums(totals):
        return run(
            partial(unpack_kernel, tensor_size, heads_width, count_model),
            [full(totals)],
            [(s, F32) for s in ((LAYERS, 2, heads_width), (LAYERS, width), (LAYERS, 2, width), (LAYERS, 2, width), (LAYERS, units),
                                (LAYERS, width), (LAYERS, 3))],
            "unpack",
        )

    def ffn_back(l, ins, extra):
        return flow(
            partial(ffn_back_body, l, l == LAYERS - 1, 2),
            ins + [sides_in(saved[l][13], 2), layer_in(w_down, l), whole_in(near[l][2]), whole_in(far[l][2]), layer_in(w_up, l),
                   whole_in(near[l][1]), whole_in(far[l][1])],
            [rows_out((rows, width), F32, 2), rows_out((rows, width), BF16, 2), sides_out((2, rows, units), BF16, 2),
             rows_out((rows, width), BF16, 2), Store((3, width), F32), Store((2, units), F32)] + extra,
            "ffn_back",
        )

    def attn_back(l, part, recv, dz_two, split):
        (low_in, fac_in, qkv, ctx, soft, rinv, low_ctx, fac_ctx, unit_one, inv_one, low_mid, fac_mid) = saved[l][:12]
        return flow(
            partial(attn_back_body, l, split, 2),
            [whole_in(vecs), rows_in(part, 2), rows_in(recv, 2, True), rows_in(fac_mid, 2), rows_in(dz_two, 2), rows_in(unit_one, 2),
             rows_in(inv_one, 2), layer_in(w_out, l), per_side_in((fac_ctx,)), per_side_in(rinv), per_side_in(ctx), per_side_in(qkv),
             per_side_in(soft), layer_in(w_qkv, l), whole_in(near[l][0]), whole_in(far[l][0])],
            [rows_out((rows, width), F32, 2), rows_out((rows, width), BF16, 2), per_side_out((2, rows, 3 * heads_width), BF16),
             Store((3, width), F32), Store((2, 2, heads_width), F32)]
            + ([Store((own_rows, width), BF16)] * 2 if split else [rows_out((rows, width), BF16, 2)]),
            "attn_back",
            scratch=[pltpu.VMEM((rows, width), F32)],
        )

    attn_columns = 2 * heads_width
    ins = [whole_in(vecs), rows_in(middle, 2), pair_in(*parts, 2), pair_in(*recvs, 2), pair_in(cotangent, other_cotangent, 2)]
    dz_two, df, du, part, sums_two, unit_sums, output, branch_sum = ffn_back(
        1, ins, [Store((own_rows, width), BF16), Store((1, 128), F32)]
    )
    square_terms.append(branch_sum)
    recv = core_swap(part)
    ffn_one = grad_group("ffn", [df, saved[1][12], saved[1][10], du], units, 1)
    if banded:
        ffn_one = begin(ffn_one, scal)
    dz_one, do, dqkv, sums_one, head_sums, part = attn_back(1, part, recv, dz_two, False)
    recv = core_swap(part)
    sums[1] = (sums_one, sums_two, head_sums, unit_sums)
    attn_one = grad_group("attn", [saved[1][0], dqkv, do, saved[1][6]], attn_columns, 1)
    if banded:
        attn_one = begin(attn_one, scal)
    ins = [whole_in(vecs), rows_in(part, 2), rows_in(recv, 2, True), rows_in(saved[1][1], 2), rows_in(dz_one, 2),
           rows_in(saved[0][14], 2), rows_in(saved[0][15], 2)]
    dz_two, df, du, part, sums_two, unit_sums = ffn_back(0, ins, [])
    recv = core_swap(part)
    if banded:
        ffn_one = second(ffn_one)
        ffn_one = crossed(ffn_one, scal)
    ffn_zero = grad_group("ffn", [df, saved[0][12], saved[0][10], du], units, 1)
    if banded:
        attn_one = second(attn_one)
        ffn_zero = begin(ffn_zero, attn_one[0])
        settle(ffn_one[1], ffn_one[3])
        ffn_one = fold(ffn_one, 2)
        ffn_one = sent(ffn_one, 2, scal)
    dz_one, do, dqkv, sums_one, head_sums, part, away = attn_back(0, part, recv, dz_two, True)
    recv = core_swap(away)
    sums[0] = (sums_one, sums_two, head_sums, unit_sums)
    attn_zero = grad_group("attn", [saved[0][0], dqkv, do, saved[0][6]], attn_columns, 1)
    (grad_hidden,) = run(
        dx_kernel,
        [full(part), full(recv), top_rows(saved[0][1], own_rows), top_rows(dz_one, own_rows)],
        [((own_rows, width), F32)],
        "dx",
    )
    if banded:
        attn_one = crossed(attn_one, grad_hidden)
        ffn_one = fold(ffn_one, 4)
        ffn_one = sent(ffn_one, 4, scal)
        ffn_zero = second(ffn_zero)
        ffn_zero = crossed(ffn_zero, scal)
        attn_one = fold(attn_one, 2)
        attn_zero = begin(attn_zero, attn_one[0])
    packed = packed_sums()
    if banded:
        attn_one = sent(attn_one, 2, ffn_one[1])
        ffn_zero = fold(ffn_zero, 2)
        ffn_zero = sent(ffn_zero, 2, scal)
        totals = total_sums(packed)
        attn_one = fold(attn_one, 4)
        attn_one = sent(attn_one, 4, scal)
        attn_zero = second(attn_zero)
        attn_zero = crossed(attn_zero, scal)
        ffn_zero = fold(ffn_zero, 4)
        ffn_zero = sent(ffn_zero, 4, scal)
        attn_zero = fold(attn_zero, 2)
        attn_zero = sent(attn_zero, 2, scal)
        small_outs = unpacked_sums(totals)
        attn_zero = fold(attn_zero, 4)
        attn_zero = sent(attn_zero, 4, scal)
        grad_qkv, grad_out, grad_up, grad_down = run(
            partial(final_kernel, heads_width),
            [full(a) for pair in (ffn_one, attn_one, ffn_zero, attn_zero) for a in pair],
            [((LAYERS, 3, band, heads_width), F32), ((LAYERS, heads_width, band), F32), ((LAYERS, band, units), F32),
             ((LAYERS, band, width), F32)],
            "final",
        )
    else:
        small_outs = unpacked_sums(total_sums(packed))
        totals = []
        for own, oth in (ffn_zero, ffn_one, attn_zero, attn_one):
            both = own.astype(F32) + x_swap(oth).astype(F32)
            totals.append(lax.psum_scatter(both, "dp", scatter_dimension=1, tiled=True))
        grad_up = jnp.stack([totals[0][0], totals[1][0]])
        grad_down = jnp.stack([totals[0][1], totals[1][1]])
        attn = jnp.stack(totals[2:])
        cut = lambda side, at: attn[:, side, :, at * heads_width : (at + 1) * heads_width]
        grad_qkv = jnp.stack([cut(0, 0), cut(0, 1), cut(1, 0)], 1)
        grad_out = jnp.swapaxes(cut(1, 1), 1, 2)

    head_bias, out_bias, gains, shifts, unit_bias, down_bias, rms = small_outs
    return (
        output,
        grad_hidden,
        grad_qkv,
        head_bias,
        grad_out,
        out_bias,
        gains,
        shifts,
        grad_up,
        unit_bias,
        jnp.swapaxes(grad_down, 1, 2),
        down_bias,
        rms,
    )


def solution(mesh):
    in_specs = (
        P(("dp", "tensor"), None),
        P("dp"),
        P("dp"),
        P(None, None, None, "tensor"),
        P(None, None, "tensor"),
        P(None, "tensor", None),
        P(),
        P(),
        P(),
        P(None, None, "tensor"),
        P(None, "tensor"),
        P(None, "tensor", None),
        P(),
        P(("dp", "tensor"), None),
    )
    out_specs = (
        P(("dp", "tensor"), None),
        P(("dp", "tensor"), None),
        P(None, None, "dp", "tensor"),
        P(None, None, "tensor"),
        P(None, "tensor", "dp"),
        P(),
        P(),
        P(),
        P(None, "dp", "tensor"),
        P(None, "tensor"),
        P(None, "tensor", "dp"),
        P(),
        P(),
    )
    return jax.shard_map(body, mesh=mesh, in_specs=in_specs, out_specs=out_specs, check_vma=False)
```
